32 devices in a mesh: dp: 16 (over z, x, core), fsdp: 2 (over y).
Axes of the slice: x: 2, y: 2, z: 4, core: 2. Of those that a mesh axis runs over, the one named last changes fastest.
Arguments:
- hidden: bfloat16 [64, 640, 768], P(('dp', 'fsdp')), may hold values from -6 to 6
- segment_ids: int32 [64, 640], P(('dp', 'fsdp')), may hold values from 0 to 3, never falling along the last dimension, each value on 1 to 256 neighbouring positions
- token_types: int32 [64, 640], P(('dp', 'fsdp')), may hold values 0 or 1
- w_query: bfloat16 [768, 3072], P('fsdp'), may hold values from -0.21875 to 0.21875
- b_query: bfloat16 [3072], P('fsdp'), may hold values from -1.796875 to 1.796875
- w_key_value: bfloat16 [768, 1536], P('fsdp'), may hold values from -0.21875 to 0.21875
- b_value: bfloat16 [768], P('fsdp'), may hold values from -1.796875 to 1.796875
- w_output: bfloat16 [768, 768], P('fsdp'), may hold values from -0.625 to 0.625
- b_output: bfloat16 [768], P('fsdp'), may hold values from -1.796875 to 1.796875
- gain_attn: bfloat16 [768], P('fsdp'), may hold values from 0.5 to 1.5
- bias_attn: bfloat16 [768], P('fsdp'), may hold values from -1.796875 to 1.796875
- w_inner: bfloat16 [768, 3072], P('fsdp'), may hold values from -0.21875 to 0.21875
- b_inner: bfloat16 [3072], P('fsdp'), may hold values from -1.796875 to 1.796875
- w_down: bfloat16 [3072, 768], P('fsdp'), may hold values from -0.21875 to 0.21875
- b_down: bfloat16 [768], P('fsdp'), may hold values from -1.796875 to 1.796875
- gain_ffn: bfloat16 [768], P('fsdp'), may hold values from 0.5 to 1.5
- bias_ffn: bfloat16 [768], P('fsdp'), may hold values from -1.796875 to 1.796875
- cotangent: bfloat16 [64, 640, 768], P(('dp', 'fsdp')), may hold values from -6 to 6
Outputs:
- output: bfloat16 [64, 640, 768], P(('dp', 'fsdp'))
- grad_hidden: bfloat16 [64, 640, 768], P(('dp', 'fsdp'))
- grad_w_query: float32 [768, 3072], P('fsdp')
- grad_b_query: float32 [3072], P('fsdp')
- grad_w_key_value: float32 [768, 1536], P('fsdp')
- grad_b_value: float32 [768], P('fsdp')
- grad_w_output: float32 [768, 768], P('fsdp')
- grad_b_output: float32 [768], P('fsdp')
- grad_gain_attn: float32 [768], P('fsdp')
- grad_bias_attn: float32 [768], P('fsdp')
- grad_w_inner: float32 [768, 3072], P('fsdp')
- grad_b_inner: float32 [3072], P('fsdp')
- grad_w_down: float32 [3072, 768], P('fsdp')
- grad_b_down: float32 [768], P('fsdp')
- grad_gain_ffn: float32 [768], P('fsdp')
- grad_bias_ffn: float32 [768], P('fsdp')
The draws below stay inside these ranges and needn't reach their ends.
Inputs may be any that keep to these rules, and one draw needn't show every extreme that they name: `segment_ids`: along a sequence the document number never falls; a document holds at most 256 tokens, and some document in each sequence holds exactly that many.
All inputs are finite; a program needn't handle non-finite values. No bound on the sum of `token_types` on one device may be relied on, other than what follows from the above.
Results may differ from the reference program's by a relative error of at most 0.02.
Values may be sent and summed in bfloat16 or wider, within the bound.
No kernel may reach another device: no remote copies, remote signals or barrier semaphores. Data moves between devices by JAX's collectives and lax.ppermute only.
A program may use at most 256 MiB of HBM per device.

```python
import math
import jax
import jax.numpy as jnp
import numpy as np
from jax import lax

D = 768
HEADS = 12
HEAD_DIM = 64
FF = 3072
LEN = 640
SEQS = 64


def plant(values, stream_key, least, top_value):
    shape = values.shape
    place = [jax.random.randint(jax.random.fold_in(stream_key, axis), (), 0, shape[axis]) for axis in range(len(shape))]
    values = values.at[tuple(place)].set(least)
    longest = shape.index(max(shape))
    place[longest] = (place[longest] + 1) % shape[longest]
    return values.at[tuple(place)].set(top_value)


def steps_of(stream_key, dims, split, low, largest):
    def one(position, parts):
        draws = jax.random.uniform(jax.random.fold_in(jax.random.fold_in(stream_key, 6), position), (parts,), jnp.float32, low / len(split), largest / len(split))
        return jnp.repeat(jnp.exp(draws), dims[position] // parts).reshape((-1,) + (1,) * (len(dims) - position - 1))

    level = one(*split[0])
    for cut in split[1:]:
        level = level * one(*cut)
    return level


def profile(number_of, total, most, skew):
    portions = [(1 << 20) // math.isqrt(standing ** skew) + 1 for standing in range(2, number_of + 1)]
    spare, given = total - most - (number_of - 1), [1] * (number_of - 1)
    while spare > 0:
        free = [i for i in range(number_of - 1) if given[i] < most]
        pool, left = sum([portions[i] for i in free]), spare
        for i in free:
            extra = min(most - given[i], max(1, left * portions[i] // pool), spare)
            given[i] = given[i] + extra
            spare = spare - extra
    return np.array([most] + given)


def uneven(stream_key, amount, total, reach, lean):
    if amount == 2:
        one = jax.random.randint(stream_key, (), max(1, total - reach), min(reach, total - 1) + 1)
        return jnp.stack([one, total - one])
    lengths = jnp.asarray(profile(amount, total, reach, lean), jnp.int32)
    pairs = (amount - 1) // 2
    giver, sink = lengths[1:1 + 2 * pairs:2], lengths[2:2 + 2 * pairs:2]
    room = jnp.minimum(giver - 1, reach - sink)
    shifted = jax.random.randint(jax.random.fold_in(stream_key, 1), (pairs,), 0, 1 << 20) % (room + 1)
    lengths = lengths.at[1:1 + 2 * pairs:2].set(giver - shifted).at[2:2 + 2 * pairs:2].set(sink + shifted)
    return lengths[jax.random.permutation(jax.random.fold_in(stream_key, 2), amount)]


def bell_draw(key, shape, deviation, reach, pieces=(), kind=jnp.bfloat16):
    values = jax.random.normal(key, shape, jnp.float32) * deviation
    if len(pieces) > 0:
        values = steps_of(key, shape, pieces, -0.22, 0.18) * values
    return jnp.clip(values, min=-reach, max=reach).astype(kind)


def setup_inputs(seed: int = 0) -> dict:
    arg_keys = jax.random.split(jax.random.key(seed), 19)
    hidden = bell_draw(arg_keys[0], (SEQS, LEN, D), 1.0, 6.0, ((0, 32),))
    segment_ids = jax.vmap(lambda own: jnp.searchsorted(jnp.cumsum(uneven(own, 4, LEN, LEN * 2 // 5, 0)), jnp.arange(LEN), side="right"))(jax.random.split(arg_keys[1], SEQS)).reshape((SEQS, LEN)).astype(jnp.int32)
    token_types = plant((jax.random.randint(arg_keys[2], (SEQS, LEN), 0, 5) < 1).astype(jnp.int32), jax.random.fold_in(arg_keys[2], 1), 0, 1)
    w_query = bell_draw(arg_keys[3], (D, 4 * D), D ** -0.5, 0.21875, ((0, 2),))
    b_query = bell_draw(arg_keys[4], (4 * D,), 0.3, 1.796875, ((0, 2),))
    w_key_value = bell_draw(arg_keys[5], (D, 2 * D), D ** -0.5, 0.21875, ((0, 2),))
    b_value = bell_draw(arg_keys[6], (D,), 0.3, 1.796875, ((0, 2),))
    w_output = bell_draw(arg_keys[7], (D, D), (D // 8) ** -0.5, 0.625, ((0, 2),))
    b_output = bell_draw(arg_keys[8], (D,), 0.3, 1.796875, ((0, 2),))
    gain_attn = jnp.clip(1.0 + 0.1 * jax.random.normal(arg_keys[9], (D,), jnp.float32), 0.5, 1.5).astype(jnp.bfloat16)
    bias_attn = bell_draw(arg_keys[10], (D,), 0.3, 1.796875, ((0, 2),))
    w_inner = bell_draw(arg_keys[11], (D, FF), D ** -0.5, 0.21875, ((0, 2),))
    b_inner = bell_draw(arg_keys[12], (FF,), 0.3, 1.796875, ((0, 2),))
    w_down = bell_draw(arg_keys[13], (FF, D), (FF // 4) ** -0.5, 0.21875, ((0, 2),))
    b_down = bell_draw(arg_keys[14], (D,), 0.3, 1.796875, ((0, 2),))
    gain_ffn = jnp.clip(1.0 + 0.1 * jax.random.normal(arg_keys[15], (D,), jnp.float32), 0.5, 1.5).astype(jnp.bfloat16)
    bias_ffn = bell_draw(arg_keys[16], (D,), 0.3, 1.796875, ((0, 2),))
    cotangent = bell_draw(arg_keys[17], (SEQS, LEN, D), 1.0, 6.0, ((0, 32),))
    return dict(hidden=hidden, segment_ids=segment_ids, token_types=token_types, w_query=w_query, b_query=b_query, w_key_value=w_key_value, b_value=b_value, w_output=w_output, b_output=b_output, gain_attn=gain_attn, bias_attn=bias_attn, w_inner=w_inner, b_inner=b_inner, w_down=w_down, b_down=b_down, gain_ffn=gain_ffn, bias_ffn=bias_ffn, cotangent=cotangent)


@jax.custom_vjp
def low(v):
    return lax.optimization_barrier(v.astype(jnp.bfloat16)).astype(jnp.float32)

@jax.custom_vjp
def low_back(v):
    return v

def low_keep(v):
    return (low(v), None)

def low_pass(kept, grad):
    return (grad,)

def back_keep(v):
    return (v, None)

def back_low(kept, grad):
    return (low(grad),)
low.defvjp(low_keep, low_pass)
low_back.defvjp(back_keep, back_low)
precise = lax.Precision.HIGHEST

def normalize(resid, branch, gain, offset):
    summed = resid + branch
    center = summed - lax.optimization_barrier(jnp.mean(summed, axis=-1, keepdims=True))
    spread = lax.optimization_barrier(jnp.mean(center * center, axis=-1, keepdims=True))
    return center * lax.rsqrt(spread + 1e-05) * gain + offset

def block_forward(tokens, params, segments, kinds):
    w_query, b_query, w_key_value, b_value, w_output, b_output, gain_attn, bias_attn, w_inner, b_inner, w_down, b_down, gain_ffn, bias_ffn = params
    length = tokens.shape[0]
    queries = low_back(jnp.dot(tokens, w_query, precision=precise) + b_query)
    is_word = (kinds == 0)[:, None]
    to_words = low(jnp.where(is_word, queries[:, :D], queries[:, 2 * D:3 * D]))
    to_entities = low(jnp.where(is_word, queries[:, D:2 * D], queries[:, 3 * D:]))
    projected = low_back(jnp.dot(tokens, w_key_value, precision=precise) + jnp.concatenate([jnp.zeros_like(b_value), b_value]))
    key_rows = low(projected[:, :D]).reshape(length, HEADS, HEAD_DIM)
    value_rows = low(projected[:, D:]).reshape(length, HEADS, HEAD_DIM)
    to_words = to_words.reshape(length, HEADS, HEAD_DIM)
    to_entities = to_entities.reshape(length, HEADS, HEAD_DIM)
    toward_words = jnp.einsum('qhe,khe->hqk', to_words, key_rows, precision=precise)
    toward_entities = jnp.einsum('qhe,khe->hqk', to_entities, key_rows, precision=precise)
    key_word = (kinds == 0)[None, None, :]
    scores = low_back(jnp.where(key_word, toward_words, toward_entities)) * HEAD_DIM ** (-0.5)
    same_doc = (segments[:, None] == segments[None, :])[None]
    scores = jnp.where(same_doc, scores, -1000000000.0)
    biggest = lax.optimization_barrier(jnp.max(scores, axis=-1, keepdims=True))
    exponents = jnp.exp(scores - biggest)
    probabilities = exponents / lax.optimization_barrier(jnp.sum(exponents, axis=-1, keepdims=True))
    context = jnp.einsum('hqk,khe->qhe', low(probabilities), value_rows, precision=precise)
    context = low(low_back(context.reshape(length, D)))
    attended = low_back(jnp.dot(context, w_output, precision=precise) + b_output)
    first_norm = normalize(tokens, attended, gain_attn, bias_attn)
    inner_act = low_back(jnp.dot(low(first_norm), w_inner, precision=precise) + b_inner)
    activated = low(jax.nn.gelu(inner_act, approximate=False))
    branch = low_back(jnp.dot(activated, w_down, precision=precise) + b_down)
    return normalize(first_norm, branch, gain_ffn, bias_ffn)

def reference(hidden, segment_ids, token_types, w_query, b_query, w_key_value, b_value, w_output, b_output, gain_attn, bias_attn, w_inner, b_inner, w_down, b_down, gain_ffn, bias_ffn, cotangent):
    params = tuple((weight.astype(jnp.float32) for weight in (w_query, b_query, w_key_value, b_value, w_output, b_output, gain_attn, bias_attn, w_inner, b_inner, w_down, b_down, gain_ffn, bias_ffn)))

    def one_sequence(totals, sequence_item):
        tokens, segments, kinds, incoming = sequence_item

        def forward(tokens_in, *weights):
            return block_forward(tokens_in, weights, segments, kinds)
        result, pullback = jax.vjp(forward, tokens.astype(jnp.float32), *params)
        grads = pullback(incoming.astype(jnp.float32))
        totals = tuple((running + update for running, update in zip(totals, grads[1:])))
        return (totals, (result.astype(jnp.bfloat16), grads[0].astype(jnp.bfloat16)))
    start = tuple((jnp.zeros(weight.shape, jnp.float32) for weight in params))
    totals, (outputs, input_grads) = lax.scan(one_sequence, start, (hidden, segment_ids, token_types, cotangent))
    return (outputs, input_grads, totals[0], totals[1], totals[2], totals[3], totals[4], totals[5], totals[6], totals[7], totals[8], totals[9], totals[10], totals[11], totals[12], totals[13])
```

```python
from functools import partial

import jax
import jax.numpy as jnp
from jax import lax
from jax.experimental import pallas as pl
from jax.experimental.pallas import tpu as pltpu
from jax.sharding import PartitionSpec as P

F32 = jnp.float32
BF = jnp.bfloat16
HEAD = 64
HEADS_PER_GROUP = 4
GROUP = HEAD * HEADS_PER_GROUP
BLOCK = 128
EXTRA = 16
EPS = 1e-05
LOG2E = 1.4426950408889634
SCALE = HEAD**-0.5
ROOT_HALF = 0.7071067811865476
INV_ROOT_2PI = 0.3989422804014327
FAR = float(2.0**33)
VMEM = 56 << 20
DP, FSDP = "dp", "fsdp"
VECTORS = range(9)
B_QUERY, B_VALUE, B_OUTPUT, GAIN_ATTN, BIAS_ATTN, B_INNER, B_DOWN, GAIN_FFN, BIAS_FFN = VECTORS
ROWS = 640


def dot(left, right, over_left=1, over_right=0):
    return lax.dot_general(
        left, right, (((over_left,), (over_right,)), ((), ())), preferred_element_type=F32
    )


def shaped(shape, dtype):
    return jax.ShapeDtypeStruct(shape, dtype)


def low_lanes(rows):
    return lax.broadcasted_iota(jnp.int32, (rows, 128), 1) < HEAD


def column_sums(values):
    return jnp.sum(values, axis=0, keepdims=True)


def row_block(rows, columns, part=0):
    return pl.BlockSpec((rows, columns), lambda i, *_: (i, part))


def whole(array):
    return pl.BlockSpec(array.shape, lambda i, *_: (0,) * array.ndim)


def settings():
    return pltpu.CompilerParams(vmem_limit_bytes=VMEM, dimension_semantics=("arbitrary",))


def cost(flops, nbytes):
    return pl.CostEstimate(flops=int(flops), bytes_accessed=int(nbytes), transcendentals=0)


def spans_of(spec, position):
    made = []
    for start, size in spec:
        if callable(start):
            start = pl.multiple_of(start(position), 16)
        made.append(pl.ds(start, size))
    return tuple(made)


def copies(position, refs, loads, targets, sems):
    made = []
    for i, (source, spec, to) in enumerate(loads):
        target = targets[i] if isinstance(targets, list) else targets
        made.append(
            pltpu.make_async_copy(
                refs[source].at[spans_of(spec, position)],
                target.at[spans_of(to, position)],
                sems.at[i],
            )
        )
    return made


def begin(made):
    for copy in made:
        copy.start()


def finish(made):
    for copy in made:
        copy.wait()


def moments(summed):
    center = summed - jnp.mean(summed, axis=-1, keepdims=True)
    inverse = lax.rsqrt(jnp.mean(center * center, axis=-1, keepdims=True) + EPS)
    return center * inverse, inverse


def norm_back(grad, hat, inverse, gain):
    scaled = grad * gain
    return inverse * (
        scaled
        - jnp.mean(scaled, axis=-1, keepdims=True)
        - hat * jnp.mean(scaled * hat, axis=-1, keepdims=True)
    )


def vector(vec_ref, spans, name):
    start, size = spans[name]
    rows = [vec_ref[i : i + 1, start : start + size] for i in range(vec_ref.shape[0])]
    return rows[0] if len(rows) == 1 else jnp.concatenate(rows, 1)


def qkv_attention(loads, spans, group, n_refs, lo_ref, n_ref, at_ref, x_ref, vec_ref, word_ref, mq_ref, mk_ref, *rest):
    refs, rest = rest[:n_refs], rest[n_refs:]
    qd_ref, kd_ref, v_ref, context_ref, log_ref, w_ref, vx_ref, sems = rest
    s = pl.program_id(0)

    @pl.when(s == 0)
    def _():
        made = copies(at_ref, refs, loads, w_ref, sems)
        begin(made)
        finish(made)

    x = x_ref[...]
    rows, width = x.shape
    blocks = rows // BLOCK
    word = word_ref[...]
    low = low_lanes(rows)
    key_mask = jnp.where(low, word, 1.0 - word)
    is_word = jnp.concatenate([word] * (GROUP // 128), 1) > 0.5

    def project(part, name, at):
        made = dot(x, w_ref[:, part * GROUP : (part + 1) * GROUP])
        if name is None:
            return made
        start = at + group * GROUP
        return made + vector(vec_ref, spans, name)[:, start : start + GROUP]

    to_words = jnp.where(
        is_word, project(0, B_QUERY, 0), project(2, B_QUERY, 2 * width)
    )
    to_entities = jnp.where(
        is_word, project(1, B_QUERY, width), project(3, B_QUERY, 3 * width)
    )
    keys = project(4, None, 0).astype(BF).astype(F32)
    vals = project(5, B_VALUE, 0).astype(BF)
    v_ref[...] = vals
    for p in range(GROUP // 128):
        lanes = slice(128 * p, 128 * p + 128)
        a, e, k = to_words[:, lanes], to_entities[:, lanes], keys[:, lanes]
        first, second = slice(256 * p, 256 * p + 128), slice(256 * p + 128, 256 * p + 256)
        qd_ref[:, first] = jnp.where(low, a, pltpu.roll(e, 64, 1)).astype(BF)
        qd_ref[:, second] = jnp.where(low, pltpu.roll(a, 64, 1), e).astype(BF)
        turned = pltpu.roll(k, 64, 1)
        kd_ref[:, first] = (jnp.where(low, k, turned) * key_mask).astype(BF)
        kd_ref[:, second] = (jnp.where(low, turned, k) * key_mask).astype(BF)
        v = vals[:, lanes].astype(F32)
        zero, one = jnp.zeros_like(v), jnp.ones_like(v)
        vx_ref[p, 0] = jnp.concatenate(
            [jnp.where(low, v, zero), jnp.where(low, one, zero)], 1
        ).astype(BF)
        vx_ref[p, 1] = jnp.concatenate(
            [jnp.where(low, zero, v), jnp.where(low, zero, one)], 1
        ).astype(BF)
    low_block = low_lanes(BLOCK)

    def query_block(i, carry):
        lo, n = lo_ref[s, i], n_ref[s, i]
        q_at = pl.ds(pl.multiple_of(i * BLOCK, BLOCK), BLOCK)
        for nk in range(1, blocks + 1):

            @pl.when(n == nk)
            def _(nk=nk):
                k_at = pl.ds(pl.multiple_of(lo * BLOCK, BLOCK), nk * BLOCK)
                mq, mk = mq_ref[q_at, :], mk_ref[k_at, :]
                logs = []
                for p in range(GROUP // 128):
                    parts, tops = [], []
                    for h in (2 * p, 2 * p + 1):
                        q = jnp.concatenate([qd_ref[q_at, 128 * h : 128 * h + 128], mq], 1)
                        k = jnp.concatenate([kd_ref[k_at, 128 * h : 128 * h + 128], mk], 1)
                        scores = dot(q, k, 1, 1)
                        top = jnp.max(scores, axis=1, keepdims=True)
                        parts.append(jnp.exp2((scores - top) * (LOG2E * SCALE)).astype(BF))
                        tops.append(top)
                    v = jnp.concatenate([vx_ref[p, 0, k_at, :], vx_ref[p, 1, k_at, :]], 0)
                    made = dot(jnp.concatenate(parts, 1), v)
                    total = made[:, 128:]
                    context_ref[q_at, 128 * p : 128 * p + 128] = (made[:, :128] / total).astype(BF)
                    top = jnp.where(low_block, tops[0], tops[1])
                    log_total = jnp.transpose(top * (LOG2E * SCALE) + jnp.log2(total))
                    logs += [log_total[0:1], log_total[64:65]]
                logs.append(jnp.zeros((8 - HEADS_PER_GROUP, 128), F32))
                log_ref[0, i] = jnp.concatenate(logs, 0)

        return carry

    lax.fori_loop(0, blocks, query_block, 0)


def call_qkv_attention(group, lo, n, at, x, vec, spans, word, mq, mk, refs, loads):
    tokens, width = x.shape
    seqs, blocks = lo.shape
    length = tokens // seqs
    return pl.pallas_call(
        partial(qkv_attention, loads, spans, group, len(refs)),
        out_shape=[
            shaped((tokens, 2 * GROUP), BF),
            shaped((tokens, 2 * GROUP), BF),
            shaped((tokens, GROUP), BF),
            shaped((tokens, GROUP), BF),
            shaped((seqs, blocks, 8, 128), F32),
        ],
        grid_spec=pltpu.PrefetchScalarGridSpec(
            num_scalar_prefetch=3,
            grid=(seqs,),
            in_specs=[row_block(length, width), whole(vec)]
            + [row_block(length, 128)] * 3
            + [pl.BlockSpec(memory_space=pl.ANY)] * len(refs),
            out_specs=[
                row_block(length, 2 * GROUP),
                row_block(length, 2 * GROUP),
                row_block(length, GROUP),
                row_block(length, GROUP),
                pl.BlockSpec((1, blocks, 8, 128), lambda i, *_: (i, 0, 0, 0)),
            ],
            scratch_shapes=[
                pltpu.VMEM((width, 6 * GROUP), BF),
                pltpu.VMEM((GROUP // 128, 2, length, 256), BF),
                pltpu.SemaphoreType.DMA((len(loads),)),
            ],
        ),
        compiler_params=settings(),
        cost_estimate=cost(6e9, 12 << 20),
        name="qkv_attention",
    )(lo, n, at, x, vec, word, mq, mk, *refs)


def attention_back(lo_ref, n_ref, qd_ref, kd_ref, v_ref, context_ref, gc_ref, log_ref, word_ref, mq_ref, mk_ref, out_ref, gq_ref, gx_ref, dots_ref):
    s = pl.program_id(0)
    rows = v_ref.shape[0]
    blocks = rows // BLOCK
    low, low_block = low_lanes(rows), low_lanes(BLOCK)
    gq_ref[...] = jnp.zeros_like(gq_ref)
    for p in range(GROUP // 128):
        lanes = slice(128 * p, 128 * p + 128)
        g = gc_ref[:, lanes].astype(F32)
        zero = jnp.zeros_like(g)
        gx_ref[p, 0] = jnp.where(low, g, zero).astype(BF)
        gx_ref[p, 1] = jnp.where(low, zero, g).astype(BF)
        product = g * context_ref[:, lanes].astype(F32)
        for i in range(blocks):
            turned = jnp.transpose(product[i * BLOCK : (i + 1) * BLOCK])
            dots_ref[i, 2 * p : 2 * p + 1] = column_sums(turned[:64])
            dots_ref[i, 2 * p + 1 : 2 * p + 2] = column_sums(turned[64:])

    def corner(first, second):
        zero = jnp.zeros_like(first)
        return jnp.concatenate(
            [jnp.concatenate([first, zero], 1), jnp.concatenate([zero, second], 1)], 0
        )

    def key_block(j, carry):
        lo, n = lo_ref[s, j], n_ref[s, j]
        k_at = pl.ds(pl.multiple_of(j * BLOCK, BLOCK), BLOCK)
        for nq in range(1, blocks + 1):

            @pl.when(n == nq)
            def _(nq=nq):
                q_at = pl.ds(pl.multiple_of(lo * BLOCK, BLOCK), nq * BLOCK)
                mq, mk = mq_ref[q_at, :], mk_ref[k_at, :]
                word = word_ref[k_at, :]
                key_mask = jnp.where(low_block, word, 1.0 - word) * SCALE
                logs = [log_ref[0, lo + t] for t in range(nq)]
                dots = [dots_ref[lo + t] for t in range(nq)]
                for p in range(GROUP // 128):
                    lanes = slice(128 * p, 128 * p + 128)
                    v = v_ref[k_at, lanes]
                    probs, grads, qs, ks = [], [], [], []
                    for half in range(2):
                        h = 2 * p + half
                        q = qd_ref[q_at, 128 * h : 128 * h + 128]
                        k = kd_ref[k_at, 128 * h : 128 * h + 128]
                        qs.append(q)
                        ks.append(k)
                        scores = dot(
                            jnp.concatenate([k, mk], 1), jnp.concatenate([q, mq], 1), 1, 1
                        )
                        log_row = jnp.concatenate([a[h : h + 1] for a in logs], 1)
                        dot_row = jnp.concatenate([a[h : h + 1] for a in dots], 1)
                        prob = jnp.exp2(scores * (LOG2E * SCALE) - log_row)
                        grad_prob = dot(v, gx_ref[p, half, q_at, :], 1, 1)
                        probs.append(prob.astype(BF))
                        grads.append((prob * (grad_prob - dot_row)).astype(BF))
                    grad_v = dot(
                        jnp.concatenate(probs, 1),
                        jnp.concatenate([gx_ref[p, 0, q_at, :], gx_ref[p, 1, q_at, :]], 0),
                    )
                    grad_k = dot(jnp.concatenate(grads, 1), corner(*qs))
                    a, b = grad_k[:, :128] * key_mask, grad_k[:, 128:] * key_mask
                    a, b = a + pltpu.roll(a, 64, 1), b + pltpu.roll(b, 64, 1)
                    at = 4 * GROUP + 128 * p
                    out_ref[k_at, at : at + 128] = jnp.where(low_block, a, b).astype(BF)
                    at = 5 * GROUP + 128 * p
                    out_ref[k_at, at : at + 128] = grad_v.astype(BF)
                    gq_ref[q_at, 256 * p : 256 * p + 256] += dot(
                        jnp.concatenate(grads, 0), corner(*ks), 0, 0
                    )

        return carry

    lax.fori_loop(0, blocks, key_block, 0)
    word = word_ref[...]
    entity = 1.0 - word
    for p in range(GROUP // 128):
        a = gq_ref[:, 256 * p : 256 * p + 128] * SCALE
        b = gq_ref[:, 256 * p + 128 : 256 * p + 256] * SCALE
        to_words = jnp.where(low, a, pltpu.roll(b, 64, 1))
        to_entities = jnp.where(low, pltpu.roll(a, 64, 1), b)
        made = (to_words * word, to_entities * word, to_words * entity, to_entities * entity)
        for part, value in enumerate(made):
            at = part * GROUP + 128 * p
            out_ref[:, at : at + 128] = value.astype(BF)


def call_attention_back(group, lo, n, kept, grad_context, word, mq, mk):
    qd, kd, v, context, log_total = kept
    tokens = v.shape[0]
    seqs, blocks = lo.shape
    length = tokens // seqs
    return pl.pallas_call(
        attention_back,
        out_shape=shaped((tokens, 6 * GROUP), BF),
        grid_spec=pltpu.PrefetchScalarGridSpec(
            num_scalar_prefetch=2,
            grid=(seqs,),
            in_specs=[
                row_block(length, 2 * GROUP),
                row_block(length, 2 * GROUP),
                row_block(length, GROUP),
                row_block(length, GROUP),
                row_block(length, GROUP, group),
                pl.BlockSpec((1, blocks, 8, 128), lambda i, *_: (i, 0, 0, 0)),
            ]
            + [row_block(length, 128)] * 3,
            out_specs=row_block(length, 6 * GROUP),
            scratch_shapes=[
                pltpu.VMEM((length, 2 * GROUP), F32),
                pltpu.VMEM((GROUP // 128, 2, length, 128), BF),
                pltpu.VMEM((blocks, 8, 128), F32),
            ],
        ),
        compiler_params=settings(),
        cost_estimate=cost(6e9, 12 << 20),
        name="attention_back",
    )(lo, n, qd, kd, v, context, grad_context, log_total, word, mq, mk)


def output_norm_inner(loads, spans, n_refs, n_parts, at_ref, x_ref, vec_ref, *rest):
    parts, rest = rest[:n_parts], rest[n_parts:]
    refs, rest = rest[:n_refs], rest[n_refs:]
    context_ref, hat_ref, inverse_ref, low_ref, act_ref, slope_ref, wo_ref, wi_ref, so, si = rest
    load_o = partial(copies, at_ref, refs, loads[0], wo_ref, so)
    load_i = partial(copies, at_ref, refs, loads[1], wi_ref, si)
    first = pl.program_id(0) == 0

    @pl.when(first)
    def _():
        made = load_o()
        begin(made)
        begin(load_i())
        finish(made)

    take = partial(vector, vec_ref, spans)
    context = jnp.concatenate([part[...] for part in parts], 1)
    context_ref[...] = context
    attended = dot(context, wo_ref[...]) + take(B_OUTPUT)
    hat, inverse = moments(x_ref[...].astype(F32) + attended)
    hat_ref[...] = hat
    inverse_ref[...] = jnp.broadcast_to(inverse, inverse_ref.shape)
    low = (hat * take(GAIN_ATTN) + take(BIAS_ATTN)).astype(BF)
    low_ref[...] = low

    @pl.when(first)
    def _():
        finish(load_i())

    hidden = wi_ref.shape[1]
    step = 512
    b_inner = take(B_INNER)
    for start in range(0, hidden, step):
        lanes = slice(start, start + step)
        inner = dot(low, wi_ref[:, lanes]) + b_inner[:, lanes]
        below = 0.5 * lax.erf(inner * ROOT_HALF) + 0.5
        act_ref[:, lanes] = (inner * below).astype(BF)
        bell = INV_ROOT_2PI * jnp.exp(-0.5 * inner * inner)
        slope_ref[:, lanes] = (below + inner * bell).astype(BF)


def call_output_norm_inner(at, parts, x, vec, spans, refs, loads, hidden):
    tokens, width = x.shape
    rows = ROWS
    return pl.pallas_call(
        partial(output_norm_inner, loads, spans, len(refs), len(parts)),
        out_shape=[
            shaped((tokens, width), BF),
            shaped((tokens, width), F32),
            shaped((tokens, 128), F32),
            shaped((tokens, width), BF),
            shaped((tokens, hidden), BF),
            shaped((tokens, hidden), BF),
        ],
        grid_spec=pltpu.PrefetchScalarGridSpec(
            num_scalar_prefetch=1,
            grid=(tokens // rows,),
            in_specs=[row_block(rows, width), whole(vec)]
            + [row_block(rows, GROUP)] * len(parts)
            + [pl.BlockSpec(memory_space=pl.ANY)] * len(refs),
            out_specs=[
                row_block(rows, width),
                row_block(rows, width),
                row_block(rows, 128),
                row_block(rows, width),
                row_block(rows, hidden),
                row_block(rows, hidden),
            ],
            scratch_shapes=[
                pltpu.VMEM((width, width), BF),
                pltpu.VMEM((width, hidden), BF),
                pltpu.SemaphoreType.DMA((len(loads[0]),)),
                pltpu.SemaphoreType.DMA((len(loads[1]),)),
            ],
        ),
        compiler_params=settings(),
        cost_estimate=cost(2 * tokens * width * (width + hidden), 30 << 20),
        name="output_norm_inner",
    )(at, x, vec, *parts, *refs)


def down_norm(loads, spans, n_refs, at_ref, act_ref, hat_ref, g_ref, vec_ref, *rest):
    refs, rest = rest[:n_refs], rest[n_refs:]
    out_ref, sum_ref, low_ref, small_ref, wd_ref, sd = rest

    @pl.when(pl.program_id(0) == 0)
    def _():
        made = copies(at_ref, refs, loads[2], wd_ref, sd)
        begin(made)
        small_ref[...] = jnp.zeros_like(small_ref)
        finish(made)

    take = partial(vector, vec_ref, spans)
    branch = dot(act_ref[...], wd_ref[...]) + take(B_DOWN)
    first = hat_ref[...] * take(GAIN_ATTN) + take(BIAS_ATTN)
    hat, inverse = moments(first + branch)
    out_ref[...] = (hat * take(GAIN_FFN) + take(BIAS_FFN)).astype(BF)
    g = g_ref[...].astype(F32)
    grad = norm_back(g, hat, inverse, take(GAIN_FFN))
    sum_ref[...] = grad
    low = grad.astype(BF)
    low_ref[...] = low
    small_ref[0:1] += column_sums(g * hat)
    small_ref[1:2] += column_sums(g)
    small_ref[2:3] += column_sums(low.astype(F32))


def call_down_norm(at, act, hat, g, vec, spans, refs, loads):
    tokens, width = hat.shape
    hidden = act.shape[1]
    rows = ROWS
    return pl.pallas_call(
        partial(down_norm, loads, spans, len(refs)),
        out_shape=[
            shaped((tokens, width), BF),
            shaped((tokens, width), F32),
            shaped((tokens, width), BF),
            shaped((8, width), F32),
        ],
        grid_spec=pltpu.PrefetchScalarGridSpec(
            num_scalar_prefetch=1,
            grid=(tokens // rows,),
            in_specs=[row_block(rows, hidden), row_block(rows, width), row_block(rows, width), whole(vec)]
            + [pl.BlockSpec(memory_space=pl.ANY)] * len(refs),
            out_specs=[
                row_block(rows, width),
                row_block(rows, width),
                row_block(rows, width),
                pl.BlockSpec((8, width), lambda i, *_: (0, 0)),
            ],
            scratch_shapes=[
                pltpu.VMEM((hidden, width), BF),
                pltpu.SemaphoreType.DMA((len(loads[2]),)),
            ],
        ),
        compiler_params=settings(),
        cost_estimate=cost(2 * tokens * width * hidden, 20 << 20),
        name="down_norm",
    )(at, act, hat, g, vec, *refs)


def inner_back(loads, spans, n_refs, at_ref, gb_ref, slope_ref, sum_ref, hat_ref, inverse_ref, vec_ref, *rest):
    refs, rest = rest[:n_refs], rest[n_refs:]
    gi_ref, gx_ref, ga_ref, gc_ref, small_ref, wo_ref, wi_ref, wd_ref, so, si, sd = rest
    load_o = partial(copies, at_ref, refs, loads[0], wo_ref, so)
    load_i = partial(copies, at_ref, refs, loads[1], wi_ref, si)
    load_d = partial(copies, at_ref, refs, loads[2], wd_ref, sd)
    start = pl.program_id(0) == 0

    @pl.when(start)
    def _():
        made = load_d()
        begin(made)
        begin(load_i())
        begin(load_o())
        small_ref[...] = jnp.zeros_like(small_ref)
        finish(made)

    gb = gb_ref[...]
    hidden = wi_ref.shape[1]
    step = 512
    for at in range(0, hidden, step):
        lanes = slice(at, at + step)
        grad = dot(gb, wd_ref[lanes, :], 1, 1) * slope_ref[:, lanes].astype(F32)
        gi_ref[:, lanes] = grad.astype(BF)

    @pl.when(start)
    def _():
        finish(load_i())

    grad_first = sum_ref[...] + dot(gi_ref[...], wi_ref[...], 1, 1)
    hat = hat_ref[...]
    grad = norm_back(grad_first, hat, inverse_ref[:, :1], vector(vec_ref, spans, GAIN_ATTN))
    gx_ref[...] = grad
    low = grad.astype(BF)
    ga_ref[...] = low
    small_ref[0:1] += column_sums(grad_first * hat)
    small_ref[1:2] += column_sums(grad_first)
    small_ref[2:3] += column_sums(low.astype(F32))

    @pl.when(start)
    def _():
        finish(load_o())

    gc_ref[...] = dot(low, wo_ref[...], 1, 1).astype(BF)


def call_inner_back(at, gb, slope, summed, hat, inverse, vec, spans, refs, loads):
    tokens, width = hat.shape
    hidden = slope.shape[1]
    rows = BACK_ROWS
    return pl.pallas_call(
        partial(inner_back, loads, spans, len(refs)),
        out_shape=[
            shaped((tokens, hidden), BF),
            shaped((tokens, width), F32),
            shaped((tokens, width), BF),
            shaped((tokens, width), BF),
            shaped((8, width), F32),
        ],
        grid_spec=pltpu.PrefetchScalarGridSpec(
            num_scalar_prefetch=1,
            grid=(tokens // rows,),
            in_specs=[
                row_block(rows, width),
                row_block(rows, hidden),
                row_block(rows, width),
                row_block(rows, width),
                row_block(rows, 128),
                whole(vec),
            ]
            + [pl.BlockSpec(memory_space=pl.ANY)] * len(refs),
            out_specs=[
                row_block(rows, hidden),
                row_block(rows, width),
                row_block(rows, width),
                row_block(rows, width),
                pl.BlockSpec((8, width), lambda i, *_: (0, 0)),
            ],
            scratch_shapes=[
                pltpu.VMEM((width, width), BF),
                pltpu.VMEM((width, hidden), BF),
                pltpu.VMEM((hidden, width), BF),
            ]
            + [pltpu.SemaphoreType.DMA((len(load),)) for load in loads],
        ),
        compiler_params=settings(),
        cost_estimate=cost(2 * tokens * width * (width + 2 * hidden), 30 << 20),
        name="inner_back",
    )(at, gb, slope, summed, hat, inverse, vec, *refs)


def sides(c):
    return (1 - c, c)


def down_grad(pos_ref, left_ref, right_ref, send_ref, keep_ref):
    half = right_ref.shape[1] // 2
    for out_ref, side in zip((send_ref, keep_ref), sides(pos_ref[1])):
        lanes = pl.ds(pl.multiple_of(side * half, 128), half)
        out_ref[0] = dot(left_ref[...], right_ref[:, lanes], 0, 0).astype(BF)


def call_down_grad(pos, left, right):
    tokens, rows = left.shape
    columns = right.shape[1]
    quarter = rows // 4

    def block(i, pos):
        y, x = pos[0], pos[2]
        return (0, jnp.where(i < 2, 1 - y, y) * 2 + jnp.where(i % 2 == 0, 1 - x, x))

    return pl.pallas_call(
        down_grad,
        out_shape=[shaped((2, rows // 2, columns // 2), BF)] * 2,
        grid_spec=pltpu.PrefetchScalarGridSpec(
            num_scalar_prefetch=1,
            grid=(4,),
            in_specs=[pl.BlockSpec((tokens, quarter), block), whole(right)],
            out_specs=[pl.BlockSpec((1, quarter, columns // 2), lambda i, pos: (i // 2, i % 2, 0))] * 2,
        ),
        compiler_params=settings(),
        cost_estimate=cost(1.3e10, 12 << 20),
        name="down_grad",
    )(pos, left, right)


def grad_parts(pos_ref, left_ref, right_ref, out_refs, extras):
    rows = left_ref.shape[1]
    quarter = right_ref.shape[1] // 4
    c, x = pos_ref[1], pos_ref[2]
    for out_ref, side in zip(out_refs, sides(c)):
        for k, part in enumerate(sides(x)):
            index = 2 * side + part
            lanes = pl.ds(pl.multiple_of(index * quarter, 128), quarter)
            to = slice(k * quarter, (k + 1) * quarter)
            right = right_ref[:, lanes]
            out_ref[0, :rows, to] = dot(left_ref[...], right, 0, 0).astype(BF)
            lines = [column_sums(right.astype(F32))] + extras(index)
            lines.append(jnp.zeros((EXTRA - len(lines), quarter), F32))
            out_ref[0, rows : rows + EXTRA, to] = jnp.concatenate(lines, 0).astype(BF)


def projection_grad(pos_ref, left_ref, right_ref, send_ref, keep_ref):
    grad_parts(pos_ref, left_ref, right_ref, (send_ref, keep_ref), lambda index: [])


def inner_output_grad(pos_ref, left_ref, right_ref, context_ref, ga_ref, small_a, small_b, send_ref, keep_ref, held_ref):
    vectors = [small_a[i : i + 1] for i in range(3)] + [small_b[i : i + 1] for i in range(3)]
    vectors += [jnp.zeros_like(vectors[0])] * 2

    def extras(index):
        made = []
        for first in (0, 4):
            line = vectors[first]
            for k in range(1, 4):
                line = jnp.where(index == k, vectors[first + k], line)
            made.append(line)
        return made

    outs = (send_ref, keep_ref)
    grad_parts(pos_ref, left_ref, right_ref, outs, extras)
    rows = left_ref.shape[1]
    eighth, half = rows // 4, ga_ref.shape[1] // 2
    for out_ref, side in zip(outs, sides(pos_ref[1])):
        lanes = pl.ds(pl.multiple_of(side * half, 128), half)
        held_ref[...] = dot(context_ref[...], ga_ref[:, lanes], 0, 0).astype(BF)
        for k, part in enumerate(sides(pos_ref[2])):
            for i in range(2):
                at = pl.ds(pl.multiple_of((2 * part + i) * eighth, 16), eighth)
                to = (2 * k + i) * half
                out_ref[0, rows + EXTRA :, to : to + half] = held_ref[at, :]


def call_projection_grad(pos, left, right, more=()):
    tokens, rows = left.shape
    columns = right.shape[1]
    half = rows // 2
    out_rows = half + EXTRA + (half // 4 if more else 0)
    left_block = pl.BlockSpec((tokens, half), lambda i, pos: (0, jnp.where(i == 0, 1 - pos[0], pos[0])))
    specs, scratch = [left_block, whole(right)], []
    if more:
        specs += [left_block] + [whole(m) for m in more[1:]]
        scratch = [pltpu.VMEM((half, more[1].shape[1] // 2), BF)]
    return pl.pallas_call(
        inner_output_grad if more else projection_grad,
        out_shape=[shaped((2, out_rows, columns // 2), BF)] * 2,
        grid_spec=pltpu.PrefetchScalarGridSpec(
            num_scalar_prefetch=1,
            grid=(2,),
            in_specs=specs,
            out_specs=[pl.BlockSpec((1, out_rows, columns // 2), lambda i, pos: (i, 0, 0))] * 2,
            scratch_shapes=scratch,
        ),
        compiler_params=settings(),
        cost_estimate=cost(1.8e10 if more else 9e9, 12 << 20),
        name="projection_grad",
    )(pos, left, right, *more)


def plus(*terms):
    total = terms[0].astype(F32)
    for term in terms[1:]:
        total = total + term.astype(F32)
    return total.astype(BF)


def small_call(kernel, name, pos, inputs, shapes):
    return pl.pallas_call(
        kernel,
        out_shape=[shaped(shape, dtype) for shape, dtype in shapes],
        in_specs=[pl.BlockSpec(memory_space=pltpu.SMEM)]
        + [pl.BlockSpec(memory_space=pltpu.VMEM)] * len(inputs),
        out_specs=[pl.BlockSpec(memory_space=pltpu.VMEM)] * len(shapes),
        compiler_params=pltpu.CompilerParams(vmem_limit_bytes=VMEM),
        cost_estimate=cost(3e9, 4 << 20),
        name=name,
    )(pos, *inputs)


def corners(pos_ref):
    c, x = pos_ref[1], pos_ref[2]
    return ((c, x), (c, 1 - x), (1 - c, x), (1 - c, 1 - x))


def join_down(pos_ref, *rest):
    out_ref = rest[4]
    for ref, (c, x) in zip(rest[:4], corners(pos_ref)):
        rows, columns = ref.shape
        at = pl.ds(pl.multiple_of(x * rows, 16), rows)
        out_ref[at, pl.ds(pl.multiple_of(c * columns, 128), columns)] = ref[...].astype(F32)


def join_inner(pos_ref, *rest):
    out_ref, output_ref, extra_ref = rest[4:]
    for ref, (c, x) in zip(rest[:4], corners(pos_ref)):
        columns = ref.shape[1]
        rows = out_ref.shape[0]
        lanes = pl.ds(pl.multiple_of((2 * c + x) * columns, 128), columns)
        out_ref[:, lanes] = ref[:rows, :].astype(F32)
        extra_ref[:, lanes] = ref[rows : rows + EXTRA, :].astype(F32)
        eighth, half = rows // 4, columns // 2
        for i in range(2):
            at = pl.ds(pl.multiple_of((2 * x + i) * eighth, 16), eighth)
            to = pl.ds(pl.multiple_of(c * half, 128), half)
            output_ref[at, to] = ref[rows + EXTRA :, i * half : (i + 1) * half].astype(F32)


def join_groups(n_pieces, pos_ref, *rest):
    wide_ref, parts, outs = rest[0], rest[1 : 1 + 4 * n_pieces], rest[1 + 4 * n_pieces :]
    query_ref, key_value_ref, small_ref, extra_ref = outs
    width = GROUP * n_pieces
    rows = query_ref.shape[0]
    mine = 2 * pos_ref[1] + pos_ref[2]
    for case in range(4):

        @pl.when(mine == case)
        def _(case=case):
            for piece in range(n_pieces):
                for k in range(4):
                    ref = parts[4 * piece + k]
                    columns = ref.shape[1]
                    start = (case ^ k) * columns
                    extra_ref[piece, :, start : start + columns] = ref[rows:, :].astype(F32)
                    for at in range(0, columns, 128):
                        block, more = divmod(start + at, GROUP)
                        to = query_ref if block < 4 else key_value_ref
                        first = block % 4 * width + piece * GROUP + more
                        to[:, first : first + 128] = ref[:rows, at : at + 128].astype(F32)

    late = [extra_ref[k, 0:1, :] for k in range(n_pieces)]
    query = jnp.concatenate(
        [row[:, k * GROUP : (k + 1) * GROUP] for k in range(4) for row in late], 1
    )
    value = jnp.concatenate([row[:, 5 * GROUP :] for row in late], 1)
    early = [wide_ref[1 + i : 2 + i, k * width : (k + 1) * width] for i in range(2) for k in range(4)]
    gain_ffn, bias_ffn, b_down, gain_attn, bias_attn, b_output = early[:6]
    wide = wide_ref[0:1, :]
    order = (query, value, b_output, gain_attn, bias_attn, wide, b_down, gain_ffn, bias_ffn)
    lower = jnp.concatenate([v[:, : v.shape[1] // 2] for v in order], 1)
    upper = jnp.concatenate([v[:, v.shape[1] // 2 :] for v in order], 1)
    small_ref[...] = jnp.where(pos_ref[0] == 0, lower, upper)


def pack_kernel(loads, n_refs, n_outs, pos_ref, *rest):
    refs, outs, sems = rest[:n_refs], rest[n_refs : n_refs + n_outs], rest[-1]
    made = copies(
        pos_ref, refs, [load[:3] for load in loads], [outs[load[3]] for load in loads], sems
    )
    begin(made)
    finish(made)


def call_pack(pos, refs, shapes, loads):
    return pl.pallas_call(
        partial(pack_kernel, loads, len(refs), len(shapes)),
        out_shape=[shaped(shape, BF) for shape in shapes],
        in_specs=[pl.BlockSpec(memory_space=pltpu.SMEM)]
        + [pl.BlockSpec(memory_space=pl.ANY)] * len(refs),
        out_specs=[pl.BlockSpec(memory_space=pltpu.VMEM)] * len(shapes),
        scratch_shapes=[pltpu.SemaphoreType.DMA((len(loads),))],
        compiler_params=pltpu.CompilerParams(vmem_limit_bytes=VMEM),
        cost_estimate=cost(2e9, 2 << 20),
        name="pack",
    )(pos, *refs)


def token_grad(loads, n_refs, at_ref, sum_ref, part_ref, *rest):
    refs, rest = rest[:n_refs], rest[n_refs:]
    out_ref, w_ref, sems = rest

    @pl.when(pl.program_id(0) == 0)
    def _():
        made = copies(at_ref, refs, loads, w_ref, sems)
        begin(made)
        finish(made)

    out_ref[...] = (sum_ref[...] + dot(part_ref[...], w_ref[...], 1, 1)).astype(out_ref.dtype)


def call_token_grad(at, part, summed, refs, loads, kind):
    tokens, width = summed.shape
    columns = part.shape[1]
    rows = ROWS
    return pl.pallas_call(
        partial(token_grad, loads, len(refs)),
        out_shape=shaped((tokens, width), kind),
        grid_spec=pltpu.PrefetchScalarGridSpec(
            num_scalar_prefetch=1,
            grid=(tokens // rows,),
            in_specs=[row_block(rows, width), row_block(rows, columns)]
            + [pl.BlockSpec(memory_space=pl.ANY)] * len(refs),
            out_specs=row_block(rows, width),
            scratch_shapes=[
                pltpu.VMEM((width, columns), BF),
                pltpu.SemaphoreType.DMA((len(loads),)),
            ],
        ),
        compiler_params=settings(),
        cost_estimate=cost(8e9, 12 << 20),
        name="token_grad",
    )(at, summed, part, *refs)


def document_facts(segments, kinds):
    seqs, length = segments.shape
    tokens = seqs * length
    first, last = segments[:, ::BLOCK], segments[:, BLOCK - 1 :: BLOCK]
    meets = jnp.logical_and(
        first[:, :, None] <= last[:, None, :], first[:, None, :] <= last[:, :, None]
    )
    lo = jnp.argmax(meets, axis=2).astype(jnp.int32)
    n = jnp.sum(meets, axis=2).astype(jnp.int32)
    word = jnp.broadcast_to((kinds.reshape(tokens, 1) == 0).astype(F32), (tokens, 128))
    lane = lax.broadcasted_iota(jnp.int32, (tokens, 128), 1)
    own = segments.reshape(tokens, 1) == lane
    mk = own.astype(BF)
    mq = jnp.where(jnp.logical_and(lane < 4, jnp.logical_not(own)), -FAR, 0.0).astype(BF)
    return lo, n, word, mq, mk


def gathered_vectors(sizes, everyone):
    spans, parts, at, start = [], [], 0, 0
    for size in sizes:
        parts.append(everyone[:, at : at + size].reshape(1, -1))
        spans.append((start, size * everyone.shape[0]))
        at += size
        start += size * everyone.shape[0]
    return jnp.concatenate(parts, 1).astype(F32), spans


def tie(value, deps):
    return lax.optimization_barrier((value, *deps))[0] if deps else value


def by_dp(bit):
    return lambda v: lax.ppermute(v, DP, [(i, i ^ bit) for i in range(16)])


def over_y(v):
    return lax.ppermute(v, FSDP, [(0, 1), (1, 0)])


over_core, over_x, over_z, over_far_z = (by_dp(1 << k) for k in range(4))


class NearWeights:
    def __init__(self, weights, vectors, pos, width, hidden):
        self.weights, self.pos, self.width = weights, pos, width
        groups = width // GROUP
        self.shard, self.part = width // 2, width // 8
        self.d_shard, self.d_part = hidden // 2, hidden // 8
        self.columns = 2 * width
        o_rows, i_rows, d_rows = self.part // 2, self.part, self.d_part // 2
        self.rows = o_rows, i_rows, d_rows

        def chunk(size, more=0):
            return lambda pos: (2 * pos[2] + pos[1]) * size + more

        def group_loads(group, to, row):
            return [
                (source, ((chunk(self.part), self.part), (column, GROUP)), ((row, self.part), (k * GROUP, GROUP)), to)
                for k, (source, column) in enumerate(group_columns(group, width))
            ]

        first = call_pack(pos, weights[:2], [(self.part, self.columns)], group_loads(0, 0, 0))[0]
        loads = []
        for group in range(1, groups):
            loads += group_loads(group, 0, (group - 1) * self.part)
        for side in range(2):
            at = (side * width, width)
            loads.append((2, ((chunk(self.part, side * o_rows), o_rows), (0, width)), ((0, o_rows), at), 1))
            loads.append(
                (
                    3,
                    ((chunk(self.part), i_rows), (side * self.columns, self.columns)),
                    ((o_rows + side * i_rows, i_rows), (0, self.columns)),
                    1,
                )
            )
            loads.append((4, ((chunk(self.d_part, side * d_rows), d_rows), (0, width)), ((0, d_rows), at), 2))
        shapes = [(groups - 1) * self.part, o_rows + 2 * i_rows, d_rows]
        self.from_y = [over_y(first)]
        packs = call_pack(tie(pos, (first,)), weights, [(rows, self.columns) for rows in shapes], loads)
        other = over_y(tie(vectors, (first,)))
        self.from_y += [over_y(v) for v in packs]
        vec = jnp.where(pos[0] == 0, jnp.stack([vectors, other]), jnp.stack([other, vectors]))
        self.vec = vec.astype(F32)
        self.arrived = [None] * 4

    def spread(self, k, before_x=(), before_core=()):
        v = tie(self.from_y[k], before_x)
        from_x = over_x(v)
        self.arrived[k] = [v, from_x, over_core(v), over_core(tie(from_x, before_core))]

    def others(self, size, more=0):
        other = lambda turn: lambda pos: (4 * (1 - pos[0]) + ((2 * pos[2] + pos[1]) ^ turn)) * size + more
        return [other(turn) for turn in (0, 2, 1, 3)]

    def own(self, size):
        return lambda pos: pos[0] * size

    def group(self, group):
        width, part = self.width, self.part
        loads = [
            (source, ((0, self.shard), (column, GROUP)), ((self.own(self.shard), self.shard), (k * GROUP, GROUP)))
            for k, (source, column) in enumerate(group_columns(group, width))
        ]
        row = 0 if group == 0 else (group - 1) * part
        for k, place in enumerate(self.others(part)):
            at = (0, self.columns)
            loads.append((2 + k, ((row, part), at), ((place, part), at)))
        return self.weights[:2] + self.arrived[min(group, 1)], loads

    def rest(self):
        width, columns = self.width, self.columns
        o_rows, i_rows, d_rows = self.rows
        whole_o, whole_i = (0, width), (0, 2 * columns)
        loads = [
            [(0, ((0, self.shard), whole_o), ((self.own(self.shard), self.shard), whole_o))],
            [(1, ((0, self.shard), whole_i), ((self.own(self.shard), self.shard), whole_i))],
            [(2, ((0, self.d_shard), whole_o), ((self.own(self.d_shard), self.d_shard), whole_o))],
        ]
        for side in range(2):
            at = (side * width, width)
            for k, place in enumerate(self.others(self.part, side * o_rows)):
                loads[0].append((3 + k, ((0, o_rows), at), ((place, o_rows), whole_o)))
            for k, place in enumerate(self.others(self.part)):
                from_rows = (o_rows + side * i_rows, i_rows)
                to = (side * columns, columns)
                loads[1].append((3 + k, (from_rows, (0, columns)), ((place, i_rows), to)))
            for k, place in enumerate(self.others(self.d_part, side * d_rows)):
                loads[2].append((7 + k, ((0, d_rows), at), ((place, d_rows), whole_o)))
        return self.weights[2:] + self.arrived[2] + self.arrived[3], loads


class FarWeights:
    def __init__(self, weights, vectors, sizes, width, hidden):
        self.weights = [lax.all_gather(v, FSDP, axis=0, tiled=True) for v in weights]
        self.vec, self.spans = gathered_vectors(sizes, lax.all_gather(vectors, FSDP))
        self.width = width

    def group(self, group):
        rows = (0, self.width)
        loads = [
            (source, (rows, (column, GROUP)), (rows, (k * GROUP, GROUP)))
            for k, (source, column) in enumerate(group_columns(group, self.width))
        ]
        return self.weights[:2], loads

    def rest(self):
        loads = []
        for k, v in enumerate(self.weights[2:]):
            spec = tuple((0, size) for size in v.shape)
            loads.append([(k, spec, spec)])
        return self.weights[2:], loads


def group_columns(group, width):
    blocks = [(0, part * width + group * GROUP) for part in range(4)]
    return blocks + [(1, part * width + group * GROUP) for part in range(2)]


def body(mesh_shape, hidden_in, segments, kinds, *rest):
    weights = [rest[i] for i in (0, 2, 4, 8, 10)]
    vectors = [rest[i] for i in (1, 3, 5, 6, 7, 9, 11, 12, 13)]
    near = mesh_shape[DP] == 16 and mesh_shape[FSDP] == 2
    seqs, length, width = hidden_in.shape
    tokens = seqs * length
    groups = width // GROUP
    x = hidden_in.reshape(tokens, width)
    g = rest[14].reshape(tokens, width)
    fsdp = mesh_shape[FSDP]
    hidden = weights[4].shape[0] * fsdp
    y, place = lax.axis_index(FSDP), lax.axis_index(DP)
    sizes = [v.shape[0] for v in vectors]
    total, start, parts, spans = sum(sizes), 0, [], []
    for v, size in zip(vectors, sizes):
        parts.append(lax.pad(v, jnp.zeros((), BF), [(start, total - start - size, 0)]))
        spans.append((start, size))
        start += size
    vector_shard = sum(parts[1:], parts[0])
    if near:
        bits = jnp.array([0, 1, 2, 4], jnp.int32)
        pos = jnp.stack([y, place & 1, (place >> 1) & 1]).astype(jnp.int32)
        source = NearWeights(weights, vector_shard, pos, width, hidden)
        source.spread(0)
    else:
        pos = jnp.ones((3,), jnp.int32)
        source = FarWeights(weights, vector_shard, sizes, width, hidden)
        spans = source.spans
    vec = source.vec
    lo, n, word, mq, mk = document_facts(segments, kinds)
    kept = []
    for group in range(groups):
        deps = tuple(k[3] for k in kept[-1:])
        if near and group == 0:
            deps = (source.from_y[1],)
        if near and group == 1:
            source.spread(1, (), (kept[0][3],))
        refs, loads = source.group(group)
        kept.append(
            call_qkv_attention(
                group, lo, n, pos, tie(x, deps), vec, spans, word, mq, mk, refs, loads
            )
        )
    if near:
        source.spread(2, (kept[0][3],), (kept[1][3],))
        source.spread(3, (kept[0][3],), (kept[2][3],))
    refs, loads = source.rest()
    context, hat, inverse, first_low, act, slope = call_output_norm_inner(
        pos, [k[3] for k in kept], x, vec, spans, refs, loads, hidden
    )
    output, summed, gb, small_ffn = call_down_norm(pos, act, hat, g, vec, spans, refs, loads)

    made, sent, partial_sums, results = {}, {}, {}, {}

    def run(kernel, deps):
        kind, k = kernel
        if kind == DOWN:
            made[kind] = call_down_grad(pos, tie(act, deps), gb)
            return made[kind][:1]
        if kind == BACK:
            results[kind] = call_inner_back(
                pos, tie(gb, deps), slope, summed, hat, inverse, vec, spans, refs, loads
            )
            return results[kind][:1]
        gi, gx, ga, gc, small_attn = results[BACK]
        if kind == INNER:
            made[kind] = call_projection_grad(
                pos, tie(first_low, deps), gi, (context, ga, small_ffn, small_attn)
            )
            return made[kind][:1]
        if kind == ATTENTION:
            partial_sums[k] = call_attention_back(k, lo, n, kept[k], tie(gc, deps), word, mq, mk)
            return (partial_sums[k],)
        if kind == PROJECTION:
            made[k] = call_projection_grad(pos, tie(x, deps), partial_sums[k])
            return made[k][:1]
        group_refs, group_loads = source.group(k)
        results[TOKEN] = call_token_grad(
            pos, partial_sums[k], tie(results.get(TOKEN, gx), deps), group_refs, group_loads,
            BF if k == groups - 1 else F32,
        )
        return (results[TOKEN],)

    order = [(DOWN, 0), (BACK, 0), (INNER, 0)]
    for k in range(groups):
        order += [(ATTENTION, k), (PROJECTION, k)]
    order += [(TOKEN, k) for k in range(groups)]

    def halves(k, v):
        if k == DOWN:
            h = v.shape[0] // 2
            return v[:h], v[h:]
        h = v.shape[1] // 2
        return v[:, :h], v[:, h:]

    def advance(k, step, deps):
        if step == 0:
            sent[k] = (over_core(made[k][0]), made[k][1])
            return ()
        come, mine = sent[k]
        come = tie(come, deps)
        if step == 1:
            out = [plus(mine[i], come[i]) for i in range(2)]
            sent[k] = (over_y(out[0]), out[1])
        elif step == 2:
            out = [plus(a, b) for a, b in zip(halves(k, mine), halves(k, come))]
            sent[k] = (over_x(out[0]), out[1])
        elif step in (3, 4):
            out = [plus(mine, come)]
            sent[k] = ((over_z if step == 3 else over_far_z)(out[0]), out[0])
        elif step == 5:
            out = [plus(mine, come)]
            sent[k] = (over_x(out[0]), [out[0], over_core(out[0])])
        else:
            out = [come]
            sent[k] = [mine[0], come, mine[1], over_core(come)]
        return tuple(out)

    def finished(k):
        if k == DOWN:
            results[k] = small_call(join_down, "join_down", pos, sent[k], [((hidden // 2, width), F32)])[0]
            return (results[k],)
        shard = width // 2
        results[k] = small_call(
            join_inner, "join_inner", pos, sent[k],
            [((shard, hidden), F32), ((shard, width), F32), ((EXTRA, hidden), F32)],
        )
        return tuple(results[k][:1])

    if near:
        plan = {}
        for k, steps in STEPS.items():
            for step, after in enumerate(steps):
                plan.setdefault(after, []).append((step, k))
        deps = ()
        for i in range(max(plan) + 1):
            done = ()
            if i < len(order):
                done = run(order[i], deps)
            deps = done
            for step, k in sorted(plan.get(i, []), key=lambda item: -item[0]):
                deps = deps + (finished(k) if step == 7 else advance(k, step, done))
        grad_inner, grad_output, extra = results[INNER]
        shard = width // 2
        grad_query, grad_key_value, small, _ = small_call(
            partial(join_groups, groups), "join_groups", pos,
            [extra] + [v for k in range(groups) for v in sent[k]],
            [
                ((shard, 4 * width), F32),
                ((shard, 2 * width), F32),
                ((1, total), F32),
                ((groups, EXTRA, 6 * GROUP), F32),
            ],
        )
        small = small.reshape(total)
        shares = [small[start : start + size] for start, size in spans]
        grad_down = results[DOWN]
    else:
        for kernel in order:
            run(kernel, ())

        def flat(v):
            return v.reshape(v.shape[0], -1).astype(F32)

        def far(v):
            return lax.psum(lax.psum_scatter(v, FSDP, scatter_dimension=0, tiled=True), DP)

        def main_and_extra(k, rows):
            both = jnp.stack(made[k], 2)
            main = both[:, :rows].reshape(2 * rows, 2, -1)
            more = both[1, rows : rows + EXTRA]
            return flat(far(main)), flat(lax.psum(more, (DP, FSDP)))

        rows = width // 2
        grad_inner, wide = main_and_extra(INNER, rows)
        grad_down = flat(far(jnp.stack(made[DOWN], 2).reshape(hidden, 2, -1)))
        out = jnp.stack(made[INNER], 0)[:, :, rows + EXTRA :]
        eighth = out.shape[2]
        out = out.reshape(2, 2, eighth, 4, width // 2).transpose(1, 3, 2, 0, 4)
        grad_output = flat(far(out.reshape(width, 2, -1)))
        by_group, late = zip(*[main_and_extra(k, rows) for k in range(groups)])
        late = [e[0] for e in late]
        early = [wide[1 + i, k * width : (k + 1) * width] for i in range(2) for k in range(4)]
        gain_ffn, bias_ffn, b_down, gain_attn, bias_attn, b_output = early[:6]
        query = jnp.concatenate([e[k * GROUP : (k + 1) * GROUP] for k in range(4) for e in late])
        value = jnp.concatenate([e[5 * GROUP :] for e in late])
        order = (query, value, b_output, gain_attn, bias_attn, wide[0], b_down, gain_ffn, bias_ffn)
        shares = [lax.dynamic_slice_in_dim(v, y * size, size, 0) for v, size in zip(order, sizes)]
        grad_query = jnp.concatenate(
            [m[:, k * GROUP : (k + 1) * GROUP] for k in range(4) for m in by_group], 1
        )
        grad_key_value = jnp.concatenate(
            [m[:, k * GROUP : (k + 1) * GROUP] for k in range(4, 6) for m in by_group], 1
        )
    return (
        output.reshape(seqs, length, width),
        results[TOKEN].reshape(seqs, length, width),
        grad_query,
        shares[B_QUERY],
        grad_key_value,
        shares[B_VALUE],
        grad_output,
        shares[B_OUTPUT],
        shares[GAIN_ATTN],
        shares[BIAS_ATTN],
        grad_inner,
        shares[B_INNER],
        grad_down,
        shares[B_DOWN],
        shares[GAIN_FFN],
        shares[BIAS_FFN],
    )


DOWN, BACK, INNER, ATTENTION, PROJECTION, TOKEN = range(-6, 0)
STEPS = {
    DOWN: (0, 1, 3, 5, 6, 8, 9, 10),
    INNER: (2, 3, 6, 7, 8, 10, 11, 12),
    0: (4, 5, 8, 9, 10, 11, 12),
    1: (6, 7, 9, 10, 11, 12, 13),
    2: (8, 9, 10, 11, 12, 13, 14),
}
BACK_ROWS = 640


def solution(mesh):
    split = P((DP, FSDP), None, None)
    tokens = P((DP, FSDP), None)
    matrix, line = P(FSDP, None), P(FSDP)
    weights = (matrix, line, matrix, line, matrix, line, line, line, matrix, line, matrix, line, line, line)
    return jax.shard_map(
        partial(body, dict(mesh.shape)),
        mesh=mesh,
        in_specs=(split, tokens, tokens) + weights + (split,),
        out_specs=(split, split) + weights,
        check_vma=False,
    )
```

```python
from functools import partial

import jax
import jax.numpy as jnp
from jax import lax
from jax.experimental import pallas as pl
from jax.experimental.pallas import tpu as pltpu
from jax.sharding import PartitionSpec as P

F32 = jnp.float32
BF = jnp.bfloat16
HEAD = 64
HEADS_PER_GROUP = 4
GROUP = HEAD * HEADS_PER_GROUP
BLOCK = 128
EXTRA = 16
EPS = 1e-05
LOG2E = 1.4426950408889634
SCALE = HEAD**-0.5
ROOT_HALF = 0.7071067811865476
INV_ROOT_2PI = 0.3989422804014327
FAR = float(2.0**33)
VMEM = 24 << 20
MIDDLE_VMEM = 56 << 20
MOST_VMEM = 60 << 20
DP, FSDP = "dp", "fsdp"
VECTORS = range(9)
B_QUERY, B_VALUE, B_OUTPUT, GAIN_ATTN, BIAS_ATTN, B_INNER, B_DOWN, GAIN_FFN, BIAS_FFN = VECTORS
ROWS = 320
TOKEN_ROWS = 320


def dot(left, right, over_left=1, over_right=0):
    return lax.dot_general(
        left, right, (((over_left,), (over_right,)), ((), ())), preferred_element_type=F32
    )


def shaped(shape, dtype):
    return jax.ShapeDtypeStruct(shape, dtype)


def low_lanes(rows):
    return lax.broadcasted_iota(jnp.int32, (rows, 128), 1) < HEAD


def column_sums(values):
    return jnp.sum(values, axis=0, keepdims=True)


def row_block(rows, columns, part=0):
    return pl.BlockSpec((rows, columns), lambda i, *_: (i, part))


def whole(array):
    return pl.BlockSpec(array.shape, lambda i, *_: (0,) * array.ndim)


def settings(vmem=VMEM):
    return pltpu.CompilerParams(vmem_limit_bytes=vmem, dimension_semantics=("arbitrary",))


def cost(flops, nbytes):
    return pl.CostEstimate(flops=int(flops), bytes_accessed=int(nbytes), transcendentals=0)


def spans_of(spec, position):
    made = []
    for start, size in spec:
        if callable(start):
            start = pl.multiple_of(start(position), 16)
        made.append(pl.ds(start, size))
    return tuple(made)


def copies(position, refs, loads, targets, sems):
    made = []
    for i, (source, spec, to) in enumerate(loads):
        target = targets[i] if isinstance(targets, list) else targets
        made.append(
            pltpu.make_async_copy(
                refs[source].at[spans_of(spec, position)],
                target.at[spans_of(to, position)],
                sems.at[i],
            )
        )
    return made


def begin(made):
    for copy in made:
        copy.start()


def finish(made):
    for copy in made:
        copy.wait()


def moments(summed):
    center = summed - jnp.mean(summed, axis=-1, keepdims=True)
    inverse = lax.rsqrt(jnp.mean(center * center, axis=-1, keepdims=True) + EPS)
    return center * inverse, inverse


def norm_back(grad, hat, inverse, gain):
    scaled = grad * gain
    return inverse * (
        scaled
        - jnp.mean(scaled, axis=-1, keepdims=True)
        - hat * jnp.mean(scaled * hat, axis=-1, keepdims=True)
    )


def vector(vec_ref, spans, name):
    start, size = spans[name]
    rows = [vec_ref[i : i + 1, start : start + size] for i in range(vec_ref.shape[0])]
    return rows[0] if len(rows) == 1 else jnp.concatenate(rows, 1)


def qkv_attention(loads, spans, group, n_refs, lo_ref, n_ref, at_ref, x_ref, vec_ref, word_ref, mq_ref, mk_ref, *rest):
    refs, rest = rest[:n_refs], rest[n_refs:]
    qd_ref, kd_ref, v_ref, context_ref, log_ref, w_ref, vx_ref, sems = rest
    s = pl.program_id(0)

    @pl.when(s == 0)
    def _():
        made = copies(at_ref, refs, loads, w_ref, sems)
        begin(made)
        finish(made)

    x = x_ref[...]
    rows, width = x.shape
    blocks = rows // BLOCK
    word = word_ref[...]
    low = low_lanes(rows)
    key_mask = jnp.where(low, word, 1.0 - word)
    is_word = jnp.concatenate([word] * (GROUP // 128), 1) > 0.5

    def project(part, name, at):
        made = dot(x, w_ref[:, part * GROUP : (part + 1) * GROUP])
        if name is None:
            return made
        start = at + group * GROUP
        return made + vector(vec_ref, spans, name)[:, start : start + GROUP]

    to_words = jnp.where(
        is_word, project(0, B_QUERY, 0), project(2, B_QUERY, 2 * width)
    )
    to_entities = jnp.where(
        is_word, project(1, B_QUERY, width), project(3, B_QUERY, 3 * width)
    )
    keys = project(4, None, 0).astype(BF).astype(F32)
    vals = project(5, B_VALUE, 0).astype(BF)
    v_ref[...] = vals
    for p in range(GROUP // 128):
        lanes = slice(128 * p, 128 * p + 128)
        a, e, k = to_words[:, lanes], to_entities[:, lanes], keys[:, lanes]
        first, second = slice(256 * p, 256 * p + 128), slice(256 * p + 128, 256 * p + 256)
        qd_ref[:, first] = jnp.where(low, a, pltpu.roll(e, 64, 1)).astype(BF)
        qd_ref[:, second] = jnp.where(low, pltpu.roll(a, 64, 1), e).astype(BF)
        turned = pltpu.roll(k, 64, 1)
        kd_ref[:, first] = (jnp.where(low, k, turned) * key_mask).astype(BF)
        kd_ref[:, second] = (jnp.where(low, turned, k) * key_mask).astype(BF)
        v = vals[:, lanes].astype(F32)
        zero, one = jnp.zeros_like(v), jnp.ones_like(v)
        vx_ref[p, 0] = jnp.concatenate(
            [jnp.where(low, v, zero), jnp.where(low, one, zero)], 1
        ).astype(BF)
        vx_ref[p, 1] = jnp.concatenate(
            [jnp.where(low, zero, v), jnp.where(low, zero, one)], 1
        ).astype(BF)
    low_block = low_lanes(BLOCK)

    def query_block(i, carry):
        lo, n = lo_ref[s, i], n_ref[s, i]
        q_at = pl.ds(pl.multiple_of(i * BLOCK, BLOCK), BLOCK)
        for nk in range(1, blocks + 1):

            @pl.when(n == nk)
            def _(nk=nk):
                k_at = pl.ds(pl.multiple_of(lo * BLOCK, BLOCK), nk * BLOCK)
                mq, mk = mq_ref[q_at, :], mk_ref[k_at, :]
                logs = []
                for p in range(GROUP // 128):
                    parts, tops = [], []
                    for h in (2 * p, 2 * p + 1):
                        q = jnp.concatenate([qd_ref[q_at, 128 * h : 128 * h + 128], mq], 1)
                        k = jnp.concatenate([kd_ref[k_at, 128 * h : 128 * h + 128], mk], 1)
                        scores = dot(q, k, 1, 1)
                        top = jnp.max(scores, axis=1, keepdims=True)
                        parts.append(jnp.exp2((scores - top) * (LOG2E * SCALE)).astype(BF))
                        tops.append(top)
                    v = jnp.concatenate([vx_ref[p, 0, k_at, :], vx_ref[p, 1, k_at, :]], 0)
                    made = dot(jnp.concatenate(parts, 1), v)
                    total = made[:, 128:]
                    context_ref[q_at, 128 * p : 128 * p + 128] = (made[:, :128] / total).astype(BF)
                    top = jnp.where(low_block, tops[0], tops[1])
                    log_total = jnp.transpose(top * (LOG2E * SCALE) + jnp.log2(total))
                    logs += [log_total[0:1], log_total[64:65]]
                logs.append(jnp.zeros((8 - HEADS_PER_GROUP, 128), F32))
                log_ref[0, i] = jnp.concatenate(logs, 0)

        return carry

    lax.fori_loop(0, blocks, query_block, 0)


def call_qkv_attention(group, lo, n, at, x, vec, spans, word, mq, mk, refs, loads):
    tokens, width = x.shape
    seqs, blocks = lo.shape
    length = tokens // seqs
    return pl.pallas_call(
        partial(qkv_attention, loads, spans, group, len(refs)),
        out_shape=[
            shaped((tokens, 2 * GROUP), BF),
            shaped((tokens, 2 * GROUP), BF),
            shaped((tokens, GROUP), BF),
            shaped((tokens, GROUP), BF),
            shaped((seqs, blocks, 8, 128), F32),
        ],
        grid_spec=pltpu.PrefetchScalarGridSpec(
            num_scalar_prefetch=3,
            grid=(seqs,),
            in_specs=[row_block(length, width), whole(vec)]
            + [row_block(length, 128)] * 3
            + [pl.BlockSpec(memory_space=pl.ANY)] * len(refs),
            out_specs=[
                row_block(length, 2 * GROUP),
                row_block(length, 2 * GROUP),
                row_block(length, GROUP),
                row_block(length, GROUP),
                pl.BlockSpec((1, blocks, 8, 128), lambda i, *_: (i, 0, 0, 0)),
            ],
            scratch_shapes=[
                pltpu.VMEM((width, 6 * GROUP), BF),
                pltpu.VMEM((GROUP // 128, 2, length, 256), BF),
                pltpu.SemaphoreType.DMA((len(loads),)),
            ],
        ),
        compiler_params=settings(MOST_VMEM),
        cost_estimate=cost(6e9, 12 << 20),
        name="qkv_attention",
    )(lo, n, at, x, vec, word, mq, mk, *refs)


def attention_back(lo_ref, n_ref, pos_ref, qd_ref, kd_ref, v_ref, context_ref, gc_ref, log_ref, word_ref, mq_ref, mk_ref, x_ref, out_ref, send_ref, keep_ref, gq_ref, gx_ref, dots_ref, all_ref):
    s = pl.program_id(0)
    rows = v_ref.shape[0]
    blocks = rows // BLOCK
    low, low_block = low_lanes(rows), low_lanes(BLOCK)
    gq_ref[...] = jnp.zeros_like(gq_ref)
    for p in range(GROUP // 128):
        lanes = slice(128 * p, 128 * p + 128)
        g = gc_ref[:, lanes].astype(F32)
        zero = jnp.zeros_like(g)
        gx_ref[p, 0] = jnp.where(low, g, zero).astype(BF)
        gx_ref[p, 1] = jnp.where(low, zero, g).astype(BF)
        product = g * context_ref[:, lanes].astype(F32)
        for i in range(blocks):
            turned = jnp.transpose(product[i * BLOCK : (i + 1) * BLOCK])
            dots_ref[i, 2 * p : 2 * p + 1] = column_sums(turned[:64])
            dots_ref[i, 2 * p + 1 : 2 * p + 2] = column_sums(turned[64:])

    def corner(first, second):
        zero = jnp.zeros_like(first)
        return jnp.concatenate(
            [jnp.concatenate([first, zero], 1), jnp.concatenate([zero, second], 1)], 0
        )

    def key_block(j, carry):
        lo, n = lo_ref[s, j], n_ref[s, j]
        k_at = pl.ds(pl.multiple_of(j * BLOCK, BLOCK), BLOCK)
        for nq in range(1, blocks + 1):

            @pl.when(n == nq)
            def _(nq=nq):
                q_at = pl.ds(pl.multiple_of(lo * BLOCK, BLOCK), nq * BLOCK)
                mq, mk = mq_ref[q_at, :], mk_ref[k_at, :]
                word = word_ref[k_at, :]
                key_mask = jnp.where(low_block, word, 1.0 - word) * SCALE
                logs = [log_ref[0, lo + t] for t in range(nq)]
                dots = [dots_ref[lo + t] for t in range(nq)]
                for p in range(GROUP // 128):
                    lanes = slice(128 * p, 128 * p + 128)
                    v = v_ref[k_at, lanes]
                    probs, grads, qs, ks = [], [], [], []
                    for half in range(2):
                        h = 2 * p + half
                        q = qd_ref[q_at, 128 * h : 128 * h + 128]
                        k = kd_ref[k_at, 128 * h : 128 * h + 128]
                        qs.append(q)
                        ks.append(k)
                        scores = dot(
                            jnp.concatenate([k, mk], 1), jnp.concatenate([q, mq], 1), 1, 1
                        )
                        log_row = jnp.concatenate([a[h : h + 1] for a in logs], 1)
                        dot_row = jnp.concatenate([a[h : h + 1] for a in dots], 1)
                        prob = jnp.exp2(scores * (LOG2E * SCALE) - log_row)
                        grad_prob = dot(v, gx_ref[p, half, q_at, :], 1, 1)
                        probs.append(prob.astype(BF))
                        grads.append((prob * (grad_prob - dot_row)).astype(BF))
                    grad_v = dot(
                        jnp.concatenate(probs, 1),
                        jnp.concatenate([gx_ref[p, 0, q_at, :], gx_ref[p, 1, q_at, :]], 0),
                    )
                    grad_k = dot(jnp.concatenate(grads, 1), corner(*qs))
                    a, b = grad_k[:, :128] * key_mask, grad_k[:, 128:] * key_mask
                    a, b = a + pltpu.roll(a, 64, 1), b + pltpu.roll(b, 64, 1)
                    at = 4 * GROUP + 128 * p
                    out_ref[k_at, at : at + 128] = jnp.where(low_block, a, b).astype(BF)
                    at = 5 * GROUP + 128 * p
                    out_ref[k_at, at : at + 128] = grad_v.astype(BF)
                    gq_ref[q_at, 256 * p : 256 * p + 256] += dot(
                        jnp.concatenate(grads, 0), corner(*ks), 0, 0
                    )

        return carry

    lax.fori_loop(0, blocks, key_block, 0)
    word = word_ref[...]
    entity = 1.0 - word
    for p in range(GROUP // 128):
        a = gq_ref[:, 256 * p : 256 * p + 128] * SCALE
        b = gq_ref[:, 256 * p + 128 : 256 * p + 256] * SCALE
        to_words = jnp.where(low, a, pltpu.roll(b, 64, 1))
        to_entities = jnp.where(low, pltpu.roll(a, 64, 1), b)
        made = (to_words * word, to_entities * word, to_words * entity, to_entities * entity)
        for part, value in enumerate(made):
            at = part * GROUP + 128 * p
            out_ref[:, at : at + 128] = value.astype(BF)
    all_ref[pl.ds(pl.multiple_of(s * rows, BLOCK), rows), :] = out_ref[...]

    @pl.when(s == pl.num_programs(0) - 1)
    def _():
        half = x_ref.shape[1] // 2
        for i, side in enumerate(sides(pos_ref[0])):
            left = x_ref[:, pl.ds(pl.multiple_of(side * half, 128), half)]
            outs = (send_ref.at[i], keep_ref.at[i])
            grad_parts(pos_ref, left, all_ref, outs, lambda index: [], half // 2 + EXTRA)


def call_attention_back(group, lo, n, pos, kept, grad_context, word, mq, mk, x):
    qd, kd, v, context, log_total = kept
    tokens = v.shape[0]
    seqs, blocks = lo.shape
    length = tokens // seqs
    return pl.pallas_call(
        attention_back,
        out_shape=[shaped((tokens, 6 * GROUP), BF)]
        + [shaped((2, x.shape[1] // 2 + 2 * EXTRA, 3 * GROUP), BF)] * 2,
        grid_spec=pltpu.PrefetchScalarGridSpec(
            num_scalar_prefetch=3,
            grid=(seqs,),
            in_specs=[
                row_block(length, 2 * GROUP),
                row_block(length, 2 * GROUP),
                row_block(length, GROUP),
                row_block(length, GROUP),
                row_block(length, GROUP, group),
                pl.BlockSpec((1, blocks, 8, 128), lambda i, *_: (i, 0, 0, 0)),
            ]
            + [row_block(length, 128)] * 3
            + [whole(x)],
            out_specs=[row_block(length, 6 * GROUP)]
            + [pl.BlockSpec((2, x.shape[1] // 2 + 2 * EXTRA, 3 * GROUP), lambda i, *_: (0, 0, 0))] * 2,
            scratch_shapes=[
                pltpu.VMEM((length, 2 * GROUP), F32),
                pltpu.VMEM((GROUP // 128, 2, length, 128), BF),
                pltpu.VMEM((blocks, 8, 128), F32),
                pltpu.VMEM((tokens, 6 * GROUP), BF),
            ],
        ),
        compiler_params=settings(),
        cost_estimate=cost(2e10, 12 << 20),
        name="attention_back",
    )(lo, n, pos, qd, kd, v, context, grad_context, log_total, word, mq, mk, x)


def middle(loads, spans, n_refs, n_parts, pos_ref, x_ref, g_ref, vec_ref, *rest):
    parts, rest = rest[:n_parts], rest[n_parts:]
    refs, rest = rest[:n_refs], rest[n_refs:]
    outs, scratch = rest[:10], rest[10:]
    context_ref, low_ref, act_ref, output_ref, gb_ref, gi_ref, gx_ref, ga_ref, gc_ref, small_ref = outs
    wo_ref, wi_ref, wd_ref, slope_ref, so, si, sd = scratch
    load_o = partial(copies, pos_ref, refs, loads[0], wo_ref, so)
    load_i = partial(copies, pos_ref, refs, loads[1], wi_ref, si)
    load_d = partial(copies, pos_ref, refs, loads[2], wd_ref, sd)
    start = pl.program_id(0) == 0

    @pl.when(start)
    def _():
        made = load_o()
        begin(made)
        begin(load_i())
        begin(load_d())
        small_ref[...] = jnp.zeros_like(small_ref)
        finish(made)

    take = partial(vector, vec_ref, spans)
    context = jnp.concatenate([part[...] for part in parts], 1)
    context_ref[...] = context
    attended = dot(context, wo_ref[...]) + take(B_OUTPUT)
    first_hat, first_inverse = moments(x_ref[...].astype(F32) + attended)
    gain_attn = take(GAIN_ATTN)
    first = first_hat * gain_attn + take(BIAS_ATTN)
    low = first.astype(BF)
    low_ref[...] = low

    @pl.when(start)
    def _():
        finish(load_i())

    hidden = wi_ref.shape[1]
    step = 512
    b_inner = take(B_INNER)
    for at in range(0, hidden, step):
        lanes = slice(at, at + step)
        inner = dot(low, wi_ref[:, lanes]) + b_inner[:, lanes]
        below = 0.5 * lax.erf(inner * ROOT_HALF) + 0.5
        act_ref[:, lanes] = (inner * below).astype(BF)
        bell = INV_ROOT_2PI * jnp.exp(-0.5 * inner * inner)
        slope_ref[:, lanes] = (below + inner * bell).astype(BF)

    @pl.when(start)
    def _():
        finish(load_d())

    branch = dot(act_ref[...], wd_ref[...]) + take(B_DOWN)
    hat, inverse = moments(first + branch)
    gain_ffn = take(GAIN_FFN)
    output_ref[...] = (hat * gain_ffn + take(BIAS_FFN)).astype(BF)
    g = g_ref[...].astype(F32)
    grad_sum = norm_back(g, hat, inverse, gain_ffn)
    gb = grad_sum.astype(BF)
    gb_ref[...] = gb
    small_ref[0:1] += column_sums(g * hat)
    small_ref[1:2] += column_sums(g)
    small_ref[2:3] += column_sums(gb.astype(F32))
    for at in range(0, hidden, step):
        lanes = slice(at, at + step)
        grad = dot(gb, wd_ref[lanes, :], 1, 1) * slope_ref[:, lanes].astype(F32)
        gi_ref[:, lanes] = grad.astype(BF)
    grad_first = grad_sum + dot(gi_ref[...], wi_ref[...], 1, 1)
    grad = norm_back(grad_first, first_hat, first_inverse, gain_attn)
    gx_ref[...] = grad
    ga = grad.astype(BF)
    ga_ref[...] = ga
    small_ref[3:4] += column_sums(grad_first * first_hat)
    small_ref[4:5] += column_sums(grad_first)
    small_ref[5:6] += column_sums(ga.astype(F32))
    gc_ref[...] = dot(ga, wo_ref[...], 1, 1).astype(BF)


def call_middle(pos, parts, x, g, vec, spans, refs, loads, hidden):
    tokens, width = x.shape
    rows = ROWS
    narrow, broad = row_block(rows, width), row_block(rows, hidden)
    return pl.pallas_call(
        partial(middle, loads, spans, len(refs), len(parts)),
        out_shape=[
            shaped((tokens, width), BF),
            shaped((tokens, width), BF),
            shaped((tokens, hidden), BF),
            shaped((tokens, width), BF),
            shaped((tokens, width), BF),
            shaped((tokens, hidden), BF),
            shaped((tokens, width), F32),
            shaped((tokens, width), BF),
            shaped((tokens, width), BF),
            shaped((8, width), F32),
        ],
        grid_spec=pltpu.PrefetchScalarGridSpec(
            num_scalar_prefetch=1,
            grid=(tokens // rows,),
            in_specs=[narrow, narrow, whole(vec)]
            + [row_block(rows, GROUP)] * len(parts)
            + [pl.BlockSpec(memory_space=pl.ANY)] * len(refs),
            out_specs=[narrow, narrow, broad, narrow, narrow, broad, narrow, narrow, narrow]
            + [pl.BlockSpec((8, width), lambda i, *_: (0, 0))],
            scratch_shapes=[
                pltpu.VMEM((width, width), BF),
                pltpu.VMEM((width, hidden), BF),
                pltpu.VMEM((hidden, width), BF),
                pltpu.VMEM((rows, hidden), BF),
            ]
            + [pltpu.SemaphoreType.DMA((len(load),)) for load in loads],
        ),
        compiler_params=settings(MIDDLE_VMEM),
        cost_estimate=cost(5e10, 50 << 20),
        name="middle",
    )(pos, x, g, vec, *parts, *refs)


def sides(c):
    return (1 - c, c)


def down_grad(pos_ref, left_ref, right_ref, send_ref, keep_ref, held_ref):
    half = right_ref.shape[1] // 2
    held_ref[...] = dot(left_ref[...], right_ref[...], 0, 0).astype(BF)
    for out_ref, side in zip((send_ref, keep_ref), sides(pos_ref[1])):
        out_ref[0] = held_ref[:, pl.ds(pl.multiple_of(side * half, 128), half)]


def call_down_grad(pos, left, right):
    tokens, rows = left.shape
    columns = right.shape[1]
    eighth = rows // 8

    def block(i, pos):
        place = 0
        for k, at in ((i // 4, pos[0]), (i // 2 % 2, pos[2]), (i % 2, pos[3])):
            place = 2 * place + jnp.where(k == 0, 1 - at, at)
        return (0, place)

    return pl.pallas_call(
        down_grad,
        out_shape=[shaped((2, rows // 2, columns // 2), BF)] * 2,
        grid_spec=pltpu.PrefetchScalarGridSpec(
            num_scalar_prefetch=1,
            grid=(8,),
            in_specs=[pl.BlockSpec((tokens, eighth), block), whole(right)],
            out_specs=[pl.BlockSpec((1, eighth, columns // 2), lambda i, pos: (i // 4, i % 4, 0))] * 2,
            scratch_shapes=[pltpu.VMEM((eighth, columns), BF)],
        ),
        compiler_params=settings(MOST_VMEM),
        cost_estimate=cost(1.3e10, 12 << 20),
        name="down_grad",
    )(pos, left, right)


def grad_parts(pos_ref, left, right_ref, outs, extras, out_rows):
    half = left.shape[1] // 2
    quarter = right_ref.shape[1] // 4
    c, x, z = pos_ref[1], pos_ref[2], pos_ref[3]
    for out, side in zip(outs, sides(c)):
        right = right_ref[:, pl.ds(pl.multiple_of(2 * side * quarter, 128), 2 * quarter)]
        made = dot(left, right, 0, 0).astype(BF)
        lines = column_sums(right.astype(F32))
        for part in range(2):
            mine = slice(part * quarter, (part + 1) * quarter)
            to = pl.ds(pl.multiple_of(jnp.where(x == part, quarter, 0), 128), quarter)
            below = [lines[:, mine]] + extras(2 * side + part)
            below.append(jnp.zeros((EXTRA - len(below), quarter), F32))
            below = jnp.concatenate(below, 0).astype(BF)
            for k in range(2):
                start = pl.multiple_of(jnp.where(z == k, out_rows, 0), 16)
                out[pl.ds(start, half), to] = made[k * half : (k + 1) * half, mine]
                out[k * out_rows + half : k * out_rows + half + EXTRA, to] = below


def inner_output_grad(pos_ref, left_ref, right_ref, context_ref, ga_ref, small_ref, send_ref, keep_ref, held_ref):
    vectors = [small_ref[i : i + 1] for i in range(6)]
    vectors += [jnp.zeros_like(vectors[0])] * 2

    def extras(index):
        made = []
        for first in (0, 4):
            line = vectors[first]
            for k in range(1, 4):
                line = jnp.where(index == k, vectors[first + k], line)
            made.append(line)
        return made

    outs = (send_ref.at[0], keep_ref.at[0])
    out_rows = send_ref.shape[1] // 2
    grad_parts(pos_ref, left_ref[...], right_ref, outs, extras, out_rows)
    rows = left_ref.shape[1]
    size, half = rows // 8, ga_ref.shape[1] // 2
    held_ref[...] = dot(context_ref[...], ga_ref[...], 0, 0).astype(BF)
    for out, side in zip(outs, sides(pos_ref[1])):
        lanes = pl.ds(pl.multiple_of(side * half, 128), half)
        for k, part in enumerate(sides(pos_ref[2])):
            for m, low in enumerate(sides(pos_ref[3])):
                for i in range(2):
                    at = pl.ds(pl.multiple_of((4 * part + 2 * low + i) * size, 16), size)
                    to = (2 * k + i) * half
                    out[(m + 1) * out_rows - size : (m + 1) * out_rows, to : to + half] = held_ref[at, lanes]


def call_inner_output_grad(pos, left, right, context, ga, small):
    tokens, rows = left.shape
    columns = right.shape[1]
    half = rows // 2
    out_rows = half + 2 * EXTRA + half // 4
    block = pl.BlockSpec((tokens, half), lambda i, pos: (0, jnp.where(i == 0, 1 - pos[0], pos[0])))
    return pl.pallas_call(
        inner_output_grad,
        out_shape=[shaped((2, out_rows, columns // 2), BF)] * 2,
        grid_spec=pltpu.PrefetchScalarGridSpec(
            num_scalar_prefetch=1,
            grid=(2,),
            in_specs=[block, whole(right), block, whole(ga), whole(small)],
            out_specs=[pl.BlockSpec((1, out_rows, columns // 2), lambda i, pos: (i, 0, 0))] * 2,
            scratch_shapes=[pltpu.VMEM((half, ga.shape[1]), BF)],
        ),
        compiler_params=settings(MOST_VMEM),
        cost_estimate=cost(1.8e10, 16 << 20),
        name="inner_grad",
    )(pos, left, right, context, ga, small)


def plus(*terms):
    total = terms[0].astype(F32)
    for term in terms[1:]:
        total = total + term.astype(F32)
    return total.astype(BF)


def add_parts(dim, mine_ref, come_ref, *out_refs):
    if dim is None:
        out_refs[0][...] = plus(mine_ref[...], come_ref[...])
        return
    size = mine_ref.shape[dim] // 2
    for k, out_ref in enumerate(out_refs):
        if len(mine_ref.shape) == 3:
            at = k
        else:
            part = pl.ds(k * size, size)
            at = (part, slice(None)) if dim == 0 else (slice(None), part)
        out_ref[...] = plus(mine_ref[at], come_ref[at])


def put_together(mine_ref, come_ref, out_ref):
    rows = mine_ref.shape[0]
    out_ref[:rows, :] = mine_ref[...]
    out_ref[rows:, :] = come_ref[...]


def pair_call(kernel, name, mine, come, shapes):
    return pl.pallas_call(
        kernel,
        out_shape=[shaped(shape, BF) for shape in shapes],
        in_specs=[pl.BlockSpec(memory_space=pltpu.VMEM)] * 2,
        out_specs=[pl.BlockSpec(memory_space=pltpu.VMEM)] * len(shapes),
        compiler_params=pltpu.CompilerParams(vmem_limit_bytes=VMEM),
        cost_estimate=cost(1000, 1000),
        name=name,
    )(mine, come)


def add_call(dim, mine, come):
    shape = mine.shape
    if dim is None:
        shapes = [shape]
    elif len(shape) == 3:
        shapes = [shape[1:]] * 2
    else:
        shapes = [tuple(size // 2 if i == dim else size for i, size in enumerate(shape))] * 2
    return pair_call(partial(add_parts, dim), "add", mine, come, shapes)


def small_call(kernel, name, pos, inputs, shapes):
    return pl.pallas_call(
        kernel,
        out_shape=[shaped(shape, dtype) for shape, dtype in shapes],
        in_specs=[pl.BlockSpec(memory_space=pltpu.SMEM)]
        + [pl.BlockSpec(memory_space=pltpu.VMEM)] * len(inputs),
        out_specs=[pl.BlockSpec(memory_space=pltpu.VMEM)] * len(shapes),
        compiler_params=pltpu.CompilerParams(vmem_limit_bytes=VMEM),
        cost_estimate=cost(3e9, 4 << 20),
        name=name,
    )(pos, *inputs)


def corners(pos_ref):
    c, x = pos_ref[1], pos_ref[2]
    return ((c, x), (c, 1 - x), (1 - c, x), (1 - c, 1 - x))


def join_down(pos_ref, *rest):
    out_ref = rest[4]
    z = pos_ref[3]
    for ref, (c, x) in zip(rest[:4], corners(pos_ref)):
        rows, columns = ref.shape[0] // 2, ref.shape[1]
        lanes = pl.ds(pl.multiple_of(c * columns, 128), columns)
        for m, low in enumerate((z, 1 - z)):
            at = pl.ds(pl.multiple_of((2 * x + low) * rows, 16), rows)
            out_ref[at, lanes] = ref[m * rows : (m + 1) * rows, :].astype(F32)


def join_inner(pos_ref, *rest):
    out_ref, output_ref, extra_ref = rest[4:]
    z = pos_ref[3]
    for ref, (c, x) in zip(rest[:4], corners(pos_ref)):
        columns = ref.shape[1]
        rows = out_ref.shape[0] // 2
        held = ref.shape[0] // 2
        lanes = pl.ds(pl.multiple_of((2 * c + x) * columns, 128), columns)
        extra_ref[:, lanes] = ref[rows : rows + EXTRA, :].astype(F32)
        size, half = rows // 4, columns // 2
        for m, low in enumerate((z, 1 - z)):
            at = pl.ds(pl.multiple_of(low * rows, 16), rows)
            out_ref[at, lanes] = ref[m * held : m * held + rows, :].astype(F32)
            for i in range(2):
                at = pl.ds(pl.multiple_of((4 * x + 2 * low + i) * size, 16), size)
                to = pl.ds(pl.multiple_of(c * half, 128), half)
                value = ref[(m + 1) * held - size : (m + 1) * held, i * half : (i + 1) * half]
                output_ref[at, to] = value.astype(F32)


def join_groups(n_pieces, pos_ref, *rest):
    wide_ref, parts, outs = rest[0], rest[1 : 1 + 4 * n_pieces], rest[1 + 4 * n_pieces :]
    query_ref, key_value_ref, small_ref, extra_ref = outs
    width = GROUP * n_pieces
    rows = query_ref.shape[0] // 2
    z = pos_ref[3]
    mine = 2 * pos_ref[1] + pos_ref[2]
    for case in range(4):

        @pl.when(mine == case)
        def _(case=case):
            for piece in range(n_pieces):
                for k in range(4):
                    ref = parts[4 * piece + k]
                    columns = ref.shape[1]
                    held = ref.shape[0] // 2
                    start = (case ^ k) * columns
                    extra_ref[piece, :, start : start + columns] = ref[rows:held, :].astype(F32)
                    for at in range(0, columns, 128):
                        block, more = divmod(start + at, GROUP)
                        to = query_ref if block < 4 else key_value_ref
                        first = block % 4 * width + piece * GROUP + more
                        for m, low in enumerate((z, 1 - z)):
                            there = pl.ds(pl.multiple_of(low * rows, 16), rows)
                            value = ref[m * held : m * held + rows, at : at + 128]
                            to[there, first : first + 128] = value.astype(F32)

    late = [extra_ref[k, 0:1, :] for k in range(n_pieces)]
    query = jnp.concatenate(
        [row[:, k * GROUP : (k + 1) * GROUP] for k in range(4) for row in late], 1
    )
    value = jnp.concatenate([row[:, 5 * GROUP :] for row in late], 1)
    early = [wide_ref[1 + i : 2 + i, k * width : (k + 1) * width] for i in range(2) for k in range(4)]
    gain_ffn, bias_ffn, b_down, gain_attn, bias_attn, b_output = early[:6]
    wide = wide_ref[0:1, :]
    order = (query, value, b_output, gain_attn, bias_attn, wide, b_down, gain_ffn, bias_ffn)
    lower = jnp.concatenate([v[:, : v.shape[1] // 2] for v in order], 1)
    upper = jnp.concatenate([v[:, v.shape[1] // 2 :] for v in order], 1)
    small_ref[...] = jnp.where(pos_ref[0] == 0, lower, upper)


def pack_kernel(loads, n_refs, n_outs, pos_ref, *rest):
    refs, outs, sems = rest[:n_refs], rest[n_refs : n_refs + n_outs], rest[-1]
    made = copies(
        pos_ref, refs, [load[:3] for load in loads], [outs[load[3]] for load in loads], sems
    )
    begin(made)
    finish(made)


def call_pack(pos, refs, shapes, loads):
    return pl.pallas_call(
        partial(pack_kernel, loads, len(refs), len(shapes)),
        out_shape=[shaped(shape, BF) for shape in shapes],
        in_specs=[pl.BlockSpec(memory_space=pltpu.SMEM)]
        + [pl.BlockSpec(memory_space=pl.ANY)] * len(refs),
        out_specs=[pl.BlockSpec(memory_space=pltpu.VMEM)] * len(shapes),
        scratch_shapes=[pltpu.SemaphoreType.DMA((len(loads),))],
        compiler_params=pltpu.CompilerParams(vmem_limit_bytes=MOST_VMEM),
        cost_estimate=cost(2e9, 2 << 20),
        name="pack",
    )(pos, *refs)


def token_grad(loads, n_refs, n_parts, pos_ref, sum_ref, *rest):
    parts, rest = rest[:n_parts], rest[n_parts:]
    refs, rest = rest[:n_refs], rest[n_refs:]
    out_ref, w_ref, sems = rest
    load = [partial(copies, pos_ref, refs, loads[k], w_ref.at[k], sems.at[k]) for k in range(n_parts)]
    start = pl.program_id(0) == 0

    @pl.when(start)
    def _():
        for one in load:
            begin(one())

    total = sum_ref[...]
    for k in range(n_parts):

        @pl.when(start)
        def _(k=k):
            finish(load[k]())

        total = total + dot(parts[k][...], w_ref[k], 1, 1)
    out_ref[...] = total.astype(out_ref.dtype)


def call_token_grad(pos, parts, summed, refs, loads, kind):
    tokens, width = summed.shape
    columns = parts[0].shape[1]
    rows = TOKEN_ROWS
    return pl.pallas_call(
        partial(token_grad, loads, len(refs), len(parts)),
        out_shape=shaped((tokens, width), kind),
        grid_spec=pltpu.PrefetchScalarGridSpec(
            num_scalar_prefetch=1,
            grid=(tokens // rows,),
            in_specs=[row_block(rows, width)]
            + [row_block(rows, columns)] * len(parts)
            + [pl.BlockSpec(memory_space=pl.ANY)] * len(refs),
            out_specs=row_block(rows, width),
            scratch_shapes=[
                pltpu.VMEM((len(parts), width, columns), BF),
                pltpu.SemaphoreType.DMA((len(parts), len(loads[0]))),
            ],
        ),
        compiler_params=settings(),
        cost_estimate=cost(8e9 * len(parts), 12 << 20),
        name="token_grad",
    )(pos, summed, *parts, *refs)


def facts(first_ref, segments_ref, kinds_ref, lo_ref, n_ref, word_ref, mq_ref, mk_ref):
    seqs, length = segments_ref.shape
    blocks = length // BLOCK
    lane = lax.broadcasted_iota(jnp.int32, (BLOCK, 128), 1)

    def column(ref, s, i):
        row = ref[s : s + 1, i * BLOCK : (i + 1) * BLOCK].astype(F32)
        return jnp.transpose(jnp.broadcast_to(row, (128, BLOCK)))

    for s in range(seqs):
        for i in range(blocks):
            at = slice((s * blocks + i) * BLOCK, (s * blocks + i + 1) * BLOCK)
            word_ref[at, :] = jnp.where(column(kinds_ref, s, i) == 0.0, 1.0, 0.0)
            own = column(segments_ref, s, i) == lane.astype(F32)
            mk_ref[at, :] = jnp.where(own, 1.0, 0.0).astype(BF)
            mq_ref[at, :] = jnp.where(own, 0.0, jnp.where(lane < 4, -FAR, 0.0)).astype(BF)
            lo, n = 0, 0
            for j in range(blocks - 1, -1, -1):
                meets = jnp.logical_and(
                    first_ref[s, j * BLOCK] <= first_ref[s, (i + 1) * BLOCK - 1],
                    first_ref[s, i * BLOCK] <= first_ref[s, (j + 1) * BLOCK - 1],
                )
                lo = jnp.where(meets, j, lo)
                n = n + jnp.where(meets, 1, 0)
            lo_ref[s, i] = lo
            n_ref[s, i] = n


def document_facts(segments, kinds):
    seqs, length = segments.shape
    tokens, blocks = seqs * length, length // BLOCK
    smem, vmem = pl.BlockSpec(memory_space=pltpu.SMEM), pl.BlockSpec(memory_space=pltpu.VMEM)
    return pl.pallas_call(
        facts,
        out_shape=[
            shaped((seqs, blocks), jnp.int32),
            shaped((seqs, blocks), jnp.int32),
            shaped((tokens, 128), F32),
            shaped((tokens, 128), BF),
            shaped((tokens, 128), BF),
        ],
        in_specs=[smem, vmem, vmem],
        out_specs=[smem, smem, vmem, vmem, vmem],
        compiler_params=pltpu.CompilerParams(vmem_limit_bytes=VMEM),
        cost_estimate=cost(1000, 1000),
        name="facts",
    )(segments, segments, kinds)


def gathered_vectors(sizes, everyone):
    spans, parts, at, start = [], [], 0, 0
    for size in sizes:
        parts.append(everyone[:, at : at + size].reshape(1, -1))
        spans.append((start, size * everyone.shape[0]))
        at += size
        start += size * everyone.shape[0]
    return jnp.concatenate(parts, 1).astype(F32), spans


def tie(value, deps):
    return lax.optimization_barrier((value, *deps))[0] if deps else value


def by_dp(bit):
    return lambda v: lax.ppermute(v, DP, [(i, i ^ bit) for i in range(16)])


def over_y(v):
    return lax.ppermute(v, FSDP, [(0, 1), (1, 0)])


over_core, over_x, over_z, over_far_z = (by_dp(1 << k) for k in range(4))


class NearWeights:
    def __init__(self, weights, vectors, pos, width, hidden):
        self.weights, self.pos, self.width = weights, pos, width
        groups = width // GROUP
        self.shard, self.part = width // 2, width // 8
        self.d_shard, self.d_part = hidden // 2, hidden // 8
        self.columns = 2 * width
        o_rows, i_rows, d_rows = self.part // 2, self.part, self.d_part // 2
        self.rows = o_rows, i_rows, d_rows

        def chunk(size, more=0):
            return lambda pos: (2 * pos[2] + pos[1]) * size + more

        def group_loads(group, to, row):
            return [
                (source, ((chunk(self.part), self.part), (column, GROUP)), ((row, self.part), (k * GROUP, GROUP)), to)
                for k, (source, column) in enumerate(group_columns(group, width))
            ]

        lines = -(-vectors.shape[0] // self.columns)
        vectors = jnp.pad(vectors, (0, lines * self.columns - vectors.shape[0])).reshape(lines, self.columns)
        at = (0, lines), (0, self.columns)
        below = (2, at, ((self.part, lines), (0, self.columns)), 0)
        shape = (self.part + EXTRA, self.columns)
        first = call_pack(pos, weights[:2] + [vectors], [shape], group_loads(0, 0, 0) + [below])[0]
        loads = []
        for group in range(1, groups):
            loads += group_loads(group, 0, (group - 1) * self.part)
        for side in range(2):
            at = (side * width, width)
            loads.append((2, ((chunk(self.part, side * o_rows), o_rows), (0, width)), ((0, o_rows), at), 1))
            loads.append(
                (
                    3,
                    ((chunk(self.part), i_rows), (side * self.columns, self.columns)),
                    ((o_rows + side * i_rows, i_rows), (0, self.columns)),
                    1,
                )
            )
            loads.append((4, ((chunk(self.d_part, side * d_rows), d_rows), (0, width)), ((0, d_rows), at), 2))
        shapes = [(groups - 1) * self.part, o_rows + 2 * i_rows, d_rows]
        self.from_y = [over_y(first)]
        packs = call_pack(tie(pos, (first,)), weights, [(rows, self.columns) for rows in shapes], loads)
        self.from_y += [over_y(v) for v in packs]
        other = self.from_y[0][self.part : self.part + lines]
        both = jnp.where(pos[0] == 0, jnp.stack([vectors, other]), jnp.stack([other, vectors]))
        self.vec = both.reshape(2, lines * self.columns).astype(F32)
        self.arrived = [None] * 4

    def spread(self, k, before_x=(), before_core=()):
        v = tie(self.from_y[k], before_x)
        from_x = over_x(v)
        self.arrived[k] = [v, from_x, over_core(v), over_core(tie(from_x, before_core))]

    def others(self, size, more=0):
        other = lambda turn: lambda pos: (4 * (1 - pos[0]) + ((2 * pos[2] + pos[1]) ^ turn)) * size + more
        return [other(turn) for turn in (0, 2, 1, 3)]

    def own(self, size):
        return lambda pos: pos[0] * size

    def group(self, group):
        width, part = self.width, self.part
        loads = [
            (source, ((0, self.shard), (column, GROUP)), ((self.own(self.shard), self.shard), (k * GROUP, GROUP)))
            for k, (source, column) in enumerate(group_columns(group, width))
        ]
        row = 0 if group == 0 else (group - 1) * part
        for k, place in enumerate(self.others(part)):
            at = (0, self.columns)
            loads.append((2 + k, ((row, part), at), ((place, part), at)))
        return self.weights[:2] + self.arrived[min(group, 1)], loads

    def rest(self):
        width, columns = self.width, self.columns
        o_rows, i_rows, d_rows = self.rows
        whole_o, whole_i = (0, width), (0, 2 * columns)
        loads = [
            [(0, ((0, self.shard), whole_o), ((self.own(self.shard), self.shard), whole_o))],
            [(1, ((0, self.shard), whole_i), ((self.own(self.shard), self.shard), whole_i))],
            [(2, ((0, self.d_shard), whole_o), ((self.own(self.d_shard), self.d_shard), whole_o))],
        ]
        for side in range(2):
            at = (side * width, width)
            for k, place in enumerate(self.others(self.part, side * o_rows)):
                loads[0].append((3 + k, ((0, o_rows), at), ((place, o_rows), whole_o)))
            for k, place in enumerate(self.others(self.part)):
                from_rows = (o_rows + side * i_rows, i_rows)
                to = (side * columns, columns)
                loads[1].append((3 + k, (from_rows, (0, columns)), ((place, i_rows), to)))
            for k, place in enumerate(self.others(self.d_part, side * d_rows)):
                loads[2].append((7 + k, ((0, d_rows), at), ((place, d_rows), whole_o)))
        return self.weights[2:] + self.arrived[2] + self.arrived[3], loads


class FarWeights:
    def __init__(self, weights, vectors, sizes, width, hidden):
        self.weights = [lax.all_gather(v, FSDP, axis=0, tiled=True) for v in weights]
        self.vec, self.spans = gathered_vectors(sizes, lax.all_gather(vectors, FSDP))
        self.width = width

    def group(self, group):
        rows = (0, self.width)
        loads = [
            (source, (rows, (column, GROUP)), (rows, (k * GROUP, GROUP)))
            for k, (source, column) in enumerate(group_columns(group, self.width))
        ]
        return self.weights[:2], loads

    def rest(self):
        loads = []
        for k, v in enumerate(self.weights[2:]):
            spec = tuple((0, size) for size in v.shape)
            loads.append([(k, spec, spec)])
        return self.weights[2:], loads


def group_columns(group, width):
    blocks = [(0, part * width + group * GROUP) for part in range(4)]
    return blocks + [(1, part * width + group * GROUP) for part in range(2)]


def body(mesh_shape, hidden_in, segments, kinds, *rest):
    weights = [rest[i] for i in (0, 2, 4, 8, 10)]
    vectors = [rest[i] for i in (1, 3, 5, 6, 7, 9, 11, 12, 13)]
    near = mesh_shape[DP] == 16 and mesh_shape[FSDP] == 2
    seqs, length, width = hidden_in.shape
    tokens = seqs * length
    groups = width // GROUP
    x = hidden_in.reshape(tokens, width)
    g = rest[14].reshape(tokens, width)
    fsdp = mesh_shape[FSDP]
    hidden = weights[4].shape[0] * fsdp
    y, place = lax.axis_index(FSDP), lax.axis_index(DP)
    sizes = [v.shape[0] for v in vectors]
    total, start, parts, spans = sum(sizes), 0, [], []
    for v, size in zip(vectors, sizes):
        parts.append(lax.pad(v, jnp.zeros((), BF), [(start, total - start - size, 0)]))
        spans.append((start, size))
        start += size
    vector_shard = sum(parts[1:], parts[0])
    if near:
        bits = jnp.array([0, 1, 2, 4], jnp.int32)
        pos = jnp.stack([y, place & 1, (place >> 1) & 1, (place >> 2) & 1]).astype(jnp.int32)
        source = NearWeights(weights, vector_shard, pos, width, hidden)
        source.spread(0)
    else:
        pos = jnp.ones((4,), jnp.int32)
        source = FarWeights(weights, vector_shard, sizes, width, hidden)
        spans = source.spans
    vec = source.vec
    lo, n, word, mq, mk = document_facts(segments, kinds)
    kept = []
    for group in range(groups):
        deps = tuple(k[3] for k in kept[-1:])
        if near and group == 0:
            deps = (source.from_y[1],)
        if near and group == 1:
            source.spread(1, (), (kept[0][3],))
        refs, loads = source.group(group)
        kept.append(
            call_qkv_attention(
                group, lo, n, pos, tie(x, deps), vec, spans, word, mq, mk, refs, loads
            )
        )
    if near:
        source.spread(2, (kept[0][3],), (kept[1][3],))
        source.spread(3, (kept[1][3],), (kept[2][3],))
    refs, loads = source.rest()
    context, first_low, act, output, gb, gi, gx, ga, gc, small_sums = call_middle(
        pos, [k[3] for k in kept], x, g, vec, spans, refs, loads, hidden
    )

    made, sent, partial_sums, results = {}, {}, [], {}

    def run(kernel, deps):
        kind, k = kernel
        if kind == DOWN:
            made[kind] = call_down_grad(pos, tie(act, deps), gb)
            return tuple(made[kind][:1])
        if kind == INNER:
            made[kind] = call_inner_output_grad(pos, tie(first_low, deps), gi, context, ga, small_sums)
            return tuple(made[kind][:1])
        if kind == ATTENTION:
            part, *made[k] = call_attention_back(
                k, lo, n, pos, kept[k], tie(gc, deps), word, mq, mk, x
            )
            partial_sums.append(part)
            return (part,)
        held = [source.group(i) for i in k]
        count = len(held[0][0])
        results[TOKEN] = call_token_grad(
            pos, [partial_sums[i] for i in k], tie(results.get(TOKEN, gx), deps),
            [ref for refs, _ in held for ref in refs],
            [[(load[0] + i * count,) + load[1:] for load in loads] for i, (_, loads) in enumerate(held)],
            BF if groups - 1 in k else F32,
        )
        return (results[TOKEN],)

    def advance(k, step, deps):
        if step == 0:
            sent[k] = (over_core(made[k][0]), made[k][1])
            return ()
        come, mine = sent[k]
        come = tie(come, deps)
        if step == 1:
            out = add_call(0, mine, come)
            sent[k] = (over_y(out[0]), out[1])
        elif step in (2, 3):
            out = add_call(1 if step == 2 and k != DOWN else 0, mine, come)
            sent[k] = ((over_x if step == 2 else over_z)(out[0]), out[1])
        elif step in (4, 5):
            out = add_call(None, mine, come)
            sent[k] = ((over_far_z if step == 4 else over_z)(out[0]), out[0])
        elif step == 6:
            rows, columns = mine.shape
            out = pair_call(put_together, "put_together", mine, come, [(2 * rows, columns)])
            sent[k] = (over_x(out[0]), [out[0], over_core(out[0])])
        elif step == 7:
            out = [come]
            sent[k] = (over_core(come), [mine[0], come, mine[1]])
        else:
            sent[k] = [*mine, come]
            return finished(k)
        return tuple(out)

    def finished(k):
        shard = width // 2
        if k == DOWN:
            results[k] = small_call(join_down, "join_down", pos, sent[k], [((hidden // 2, width), F32)])
        elif k == INNER:
            results[k] = small_call(
                join_inner, "join_inner", pos, sent[k],
                [((shard, hidden), F32), ((shard, width), F32), ((EXTRA, hidden), F32)],
            )
        else:
            return tuple(sent[k])
        return tuple(results[k])

    kernels = [(DOWN, 0), (INNER, 0)] + [(ATTENTION, k) for k in range(groups)]
    kernels += [(TOKEN, [k]) for k in range(groups)]
    if near:
        base, since, tail = (), (), False
        for item in PLAN:
            if item is None:
                tail = True
            elif isinstance(item, tuple):
                made_now = advance(*item, base)
                base, since = (made_now or base, ()) if tail else (base, since + made_now)
            else:
                base = since = run(kernels[item], since)
        grad_inner, grad_output, extra = results[INNER]
        shard = width // 2
        grad_query, grad_key_value, small, _ = small_call(
            partial(join_groups, groups), "join_groups", pos,
            [extra] + [v for k in range(groups) for v in sent[k]],
            [
                ((shard, 4 * width), F32),
                ((shard, 2 * width), F32),
                ((1, total), F32),
                ((groups, EXTRA, 6 * GROUP), F32),
            ],
        )
        small = small.reshape(total)
        shares = [small[start : start + size] for start, size in spans]
        grad_down = results[DOWN][0]
    else:
        for kernel in kernels:
            run(kernel, ())

        def flat(v):
            return v.reshape(v.shape[0], -1).astype(F32)

        def far(v):
            return lax.psum(lax.psum_scatter(v, FSDP, scatter_dimension=0, tiled=True), DP)

        def main_and_extra(k, rows):
            both = jnp.stack(made[k], 2).reshape(2, 2, made[k][0].shape[1] // 2, 2, -1)
            main = both[:, :, :rows].reshape(4 * rows, 2, -1)
            more = both[1, 1, rows : rows + EXTRA]
            return flat(far(main)), flat(lax.psum(more, (DP, FSDP)))

        rows = width // 4
        grad_inner, wide = main_and_extra(INNER, rows)
        grad_down = flat(far(jnp.stack(made[DOWN], 2).reshape(hidden, 2, -1)))
        out = jnp.stack(made[INNER], 0).reshape(2, 2, 2, -1, hidden // 2)[:, :, :, rows + EXTRA :]
        size = out.shape[3]
        out = out.reshape(2, 2, 2, size, 2, 2, width // 2).transpose(1, 4, 2, 5, 3, 0, 6)
        grad_output = flat(far(out.reshape(width, 2, -1)))
        by_group, late = zip(*[main_and_extra(k, rows) for k in range(groups)])
        late = [e[0] for e in late]
        early = [wide[1 + i, k * width : (k + 1) * width] for i in range(2) for k in range(4)]
        gain_ffn, bias_ffn, b_down, gain_attn, bias_attn, b_output = early[:6]
        query = jnp.concatenate([e[k * GROUP : (k + 1) * GROUP] for k in range(4) for e in late])
        value = jnp.concatenate([e[5 * GROUP :] for e in late])
        order = (query, value, b_output, gain_attn, bias_attn, wide[0], b_down, gain_ffn, bias_ffn)
        shares = [lax.dynamic_slice_in_dim(v, y * size, size, 0) for v, size in zip(order, sizes)]
        grad_query = jnp.concatenate(
            [m[:, k * GROUP : (k + 1) * GROUP] for k in range(4) for m in by_group], 1
        )
        grad_key_value = jnp.concatenate(
            [m[:, k * GROUP : (k + 1) * GROUP] for k in range(4, 6) for m in by_group], 1
        )
    return (
        output.reshape(seqs, length, width),
        results[TOKEN].reshape(seqs, length, width),
        grad_query,
        shares[B_QUERY],
        grad_key_value,
        shares[B_VALUE],
        grad_output,
        shares[B_OUTPUT],
        shares[GAIN_ATTN],
        shares[BIAS_ATTN],
        grad_inner,
        shares[B_INNER],
        grad_down,
        shares[B_DOWN],
        shares[GAIN_FFN],
        shares[BIAS_FFN],
    )


DOWN, INNER, ATTENTION, TOKEN = range(-4, 0)
PLAN = (
    0, (DOWN, 0), 1, (DOWN, 1), (INNER, 0), 2, (INNER, 1), (0, 0), 3, (0, 1), (1, 0), (DOWN, 2), 4, (1,
    1), (2, 0), (DOWN, 3), 5, (2, 1), (DOWN, 4), (INNER, 2), 6, (DOWN, 5), (0, 2), 7, (INNER, 3), (1,
    2), None, (DOWN, 6), (0, 3), (2, 2), (1, 3), (INNER, 4), (1, 4), (INNER, 5), (1, 5), (2, 3), (INNER,
    6), (DOWN, 7), (0, 4), (1, 6), (DOWN, 8), (2, 4), (0, 5), (2, 5), (INNER, 7), (0, 6), (INNER, 8),
    (1, 7), (2, 6), (1, 8), (0, 7), (0, 8), (2, 7), (2, 8),
)
def solution(mesh):
    split = P((DP, FSDP), None, None)
    tokens = P((DP, FSDP), None)
    matrix, line = P(FSDP, None), P(FSDP)
    weights = (matrix, line, matrix, line, matrix, line, line, line, matrix, line, matrix, line, line, line)
    return jax.shard_map(
        partial(body, dict(mesh.shape)),
        mesh=mesh,
        in_specs=(split, tokens, tokens) + weights + (split,),
        out_specs=(split, split) + weights,
        check_vma=False,
    )
```

```python
from functools import partial

import jax
import jax.numpy as jnp
from jax import lax
from jax.experimental import pallas as pl
from jax.experimental.pallas import tpu as pltpu
from jax.sharding import PartitionSpec as P

F32 = jnp.float32
BF = jnp.bfloat16
HEAD = 64
HEADS_PER_GROUP = 4
GROUP = HEAD * HEADS_PER_GROUP
BLOCK = 128
EXTRA = 16
EPS = 1e-05
LOG2E = 1.4426950408889634
SCALE = HEAD**-0.5
ROOT_HALF = 0.7071067811865476
INV_ROOT_2PI = 0.3989422804014327
FAR = float(2.0**33)
VMEM = 24 << 20
MIDDLE_VMEM = 56 << 20
MOST_VMEM = 60 << 20
DP, FSDP = "dp", "fsdp"
VECTORS = range(9)
B_QUERY, B_VALUE, B_OUTPUT, GAIN_ATTN, BIAS_ATTN, B_INNER, B_DOWN, GAIN_FFN, BIAS_FFN = VECTORS
ROWS = 320
TOKEN_ROWS = 320


def dot(left, right, over_left=1, over_right=0):
    return lax.dot_general(
        left, right, (((over_left,), (over_right,)), ((), ())), preferred_element_type=F32
    )


def shaped(shape, dtype):
    return jax.ShapeDtypeStruct(shape, dtype)


def low_lanes(rows):
    return lax.broadcasted_iota(jnp.int32, (rows, 128), 1) < HEAD


def column_sums(values):
    return jnp.sum(values, axis=0, keepdims=True)


def row_block(rows, columns, part=0):
    return pl.BlockSpec((rows, columns), lambda i, *_: (i, part))


def whole(array):
    return pl.BlockSpec(array.shape, lambda i, *_: (0,) * array.ndim)


def settings(vmem=VMEM):
    return pltpu.CompilerParams(vmem_limit_bytes=vmem, dimension_semantics=("arbitrary",))


def cost(flops, nbytes):
    return pl.CostEstimate(flops=int(flops), bytes_accessed=int(nbytes), transcendentals=0)


def spans_of(spec, position):
    made = []
    for start, size in spec:
        if callable(start):
            start = pl.multiple_of(start(position), 16)
        made.append(pl.ds(start, size))
    return tuple(made)


def copies(position, refs, loads, targets, sems):
    made = []
    for i, (source, spec, to) in enumerate(loads):
        target = targets[i] if isinstance(targets, list) else targets
        made.append(
            pltpu.make_async_copy(
                refs[source].at[spans_of(spec, position)],
                target.at[spans_of(to, position)],
                sems.at[i],
            )
        )
    return made


def begin(made):
    for copy in made:
        copy.start()


def finish(made):
    for copy in made:
        copy.wait()


def moments(summed):
    center = summed - jnp.mean(summed, axis=-1, keepdims=True)
    inverse = lax.rsqrt(jnp.mean(center * center, axis=-1, keepdims=True) + EPS)
    return center * inverse, inverse


def norm_back(grad, hat, inverse, gain):
    scaled = grad * gain
    return inverse * (
        scaled
        - jnp.mean(scaled, axis=-1, keepdims=True)
        - hat * jnp.mean(scaled * hat, axis=-1, keepdims=True)
    )


def vector(vec_ref, spans, name):
    start, size = spans[name]
    rows = [vec_ref[i : i + 1, start : start + size] for i in range(vec_ref.shape[0])]
    return rows[0] if len(rows) == 1 else jnp.concatenate(rows, 1)


def qkv_attention(loads, spans, group, n_refs, lo_ref, n_ref, at_ref, x_ref, vec_ref, word_ref, mq_ref, mk_ref, *rest):
    refs, rest = rest[:n_refs], rest[n_refs:]
    qd_ref, kd_ref, v_ref, context_ref, log_ref, w_ref, vx_ref, sems = rest
    s = pl.program_id(0)

    @pl.when(s == 0)
    def _():
        made = copies(at_ref, refs, loads, w_ref, sems)
        begin(made)
        finish(made)

    x = x_ref[...]
    rows, width = x.shape
    blocks = rows // BLOCK
    word = word_ref[...]
    low = low_lanes(rows)
    key_mask = jnp.where(low, word, 1.0 - word)
    is_word = jnp.concatenate([word] * (GROUP // 128), 1) > 0.5

    def project(part, name, at):
        made = dot(x, w_ref[:, part * GROUP : (part + 1) * GROUP])
        if name is None:
            return made
        start = at + group * GROUP
        return made + vector(vec_ref, spans, name)[:, start : start + GROUP]

    to_words = jnp.where(
        is_word, project(0, B_QUERY, 0), project(2, B_QUERY, 2 * width)
    )
    to_entities = jnp.where(
        is_word, project(1, B_QUERY, width), project(3, B_QUERY, 3 * width)
    )
    keys = project(4, None, 0).astype(BF).astype(F32)
    vals = project(5, B_VALUE, 0).astype(BF)
    v_ref[...] = vals
    for p in range(GROUP // 128):
        lanes = slice(128 * p, 128 * p + 128)
        a, e, k = to_words[:, lanes], to_entities[:, lanes], keys[:, lanes]
        first, second = slice(256 * p, 256 * p + 128), slice(256 * p + 128, 256 * p + 256)
        qd_ref[:, first] = jnp.where(low, a, pltpu.roll(e, 64, 1)).astype(BF)
        qd_ref[:, second] = jnp.where(low, pltpu.roll(a, 64, 1), e).astype(BF)
        turned = pltpu.roll(k, 64, 1)
        kd_ref[:, first] = (jnp.where(low, k, turned) * key_mask).astype(BF)
        kd_ref[:, second] = (jnp.where(low, turned, k) * key_mask).astype(BF)
        v = vals[:, lanes].astype(F32)
        zero, one = jnp.zeros_like(v), jnp.ones_like(v)
        vx_ref[p, 0] = jnp.concatenate(
            [jnp.where(low, v, zero), jnp.where(low, one, zero)], 1
        ).astype(BF)
        vx_ref[p, 1] = jnp.concatenate(
            [jnp.where(low, zero, v), jnp.where(low, zero, one)], 1
        ).astype(BF)
    low_block = low_lanes(BLOCK)

    def query_block(i, carry):
        lo, n = lo_ref[s, i], n_ref[s, i]
        q_at = pl.ds(pl.multiple_of(i * BLOCK, BLOCK), BLOCK)
        for nk in range(1, blocks + 1):

            @pl.when(n == nk)
            def _(nk=nk):
                k_at = pl.ds(pl.multiple_of(lo * BLOCK, BLOCK), nk * BLOCK)
                mq, mk = mq_ref[q_at, :], mk_ref[k_at, :]
                heads, pairs = range(HEADS_PER_GROUP), range(GROUP // 128)
                scores = []
                for h in heads:
                    q = jnp.concatenate([qd_ref[q_at, 128 * h : 128 * h + 128], mq], 1)
                    k = jnp.concatenate([kd_ref[k_at, 128 * h : 128 * h + 128], mk], 1)
                    scores.append(dot(q, k, 1, 1))
                tops = [jnp.max(score, axis=1, keepdims=True) for score in scores]
                parts = [
                    jnp.exp2((score - top) * (LOG2E * SCALE)).astype(BF)
                    for score, top in zip(scores, tops)
                ]
                made = [
                    dot(
                        jnp.concatenate(parts[2 * p : 2 * p + 2], 1),
                        jnp.concatenate([vx_ref[p, 0, k_at, :], vx_ref[p, 1, k_at, :]], 0),
                    )
                    for p in pairs
                ]
                logs = []
                for p in pairs:
                    total = made[p][:, 128:]
                    context_ref[q_at, 128 * p : 128 * p + 128] = (made[p][:, :128] / total).astype(BF)
                    top = jnp.where(low_block, tops[2 * p], tops[2 * p + 1])
                    log_total = jnp.transpose(top * (LOG2E * SCALE) + jnp.log2(total))
                    logs += [log_total[0:1], log_total[64:65]]
                logs.append(jnp.zeros((8 - HEADS_PER_GROUP, 128), F32))
                log_ref[0, i] = jnp.concatenate(logs, 0)

        return carry

    lax.fori_loop(0, blocks, query_block, 0)


def call_qkv_attention(group, lo, n, at, x, vec, spans, word, mq, mk, refs, loads):
    tokens, width = x.shape
    seqs, blocks = lo.shape
    length = tokens // seqs
    return pl.pallas_call(
        partial(qkv_attention, loads, spans, group, len(refs)),
        out_shape=[
            shaped((tokens, 2 * GROUP), BF),
            shaped((tokens, 2 * GROUP), BF),
            shaped((tokens, GROUP), BF),
            shaped((tokens, GROUP), BF),
            shaped((seqs, blocks, 8, 128), F32),
        ],
        grid_spec=pltpu.PrefetchScalarGridSpec(
            num_scalar_prefetch=3,
            grid=(seqs,),
            in_specs=[row_block(length, width), whole(vec)]
            + [row_block(length, 128)] * 3
            + [pl.BlockSpec(memory_space=pl.ANY)] * len(refs),
            out_specs=[
                row_block(length, 2 * GROUP),
                row_block(length, 2 * GROUP),
                row_block(length, GROUP),
                row_block(length, GROUP),
                pl.BlockSpec((1, blocks, 8, 128), lambda i, *_: (i, 0, 0, 0)),
            ],
            scratch_shapes=[
                pltpu.VMEM((width, 6 * GROUP), BF),
                pltpu.VMEM((GROUP // 128, 2, length, 256), BF),
                pltpu.SemaphoreType.DMA((len(loads),)),
            ],
        ),
        compiler_params=settings(MOST_VMEM),
        cost_estimate=cost(6e9, 12 << 20),
        name="qkv_attention",
    )(lo, n, at, x, vec, word, mq, mk, *refs)


def attention_back(lo_ref, n_ref, pos_ref, qd_ref, kd_ref, v_ref, context_ref, gc_ref, log_ref, word_ref, mq_ref, mk_ref, x_ref, out_ref, send_ref, keep_ref, gq_ref, gx_ref, dots_ref, all_ref):
    s = pl.program_id(0)
    rows = v_ref.shape[0]
    blocks = rows // BLOCK
    low, low_block = low_lanes(rows), low_lanes(BLOCK)
    gq_ref[...] = jnp.zeros_like(gq_ref)
    for p in range(GROUP // 128):
        lanes = slice(128 * p, 128 * p + 128)
        g = gc_ref[:, lanes].astype(F32)
        zero = jnp.zeros_like(g)
        gx_ref[p, 0] = jnp.where(low, g, zero).astype(BF)
        gx_ref[p, 1] = jnp.where(low, zero, g).astype(BF)
        product = g * context_ref[:, lanes].astype(F32)
        for i in range(blocks):
            turned = jnp.transpose(product[i * BLOCK : (i + 1) * BLOCK])
            dots_ref[i, 2 * p : 2 * p + 1] = column_sums(turned[:64])
            dots_ref[i, 2 * p + 1 : 2 * p + 2] = column_sums(turned[64:])

    def corner(first, second):
        zero = jnp.zeros_like(first)
        return jnp.concatenate(
            [jnp.concatenate([first, zero], 1), jnp.concatenate([zero, second], 1)], 0
        )

    def key_block(j, carry):
        lo, n = lo_ref[s, j], n_ref[s, j]
        k_at = pl.ds(pl.multiple_of(j * BLOCK, BLOCK), BLOCK)
        for nq in range(1, blocks + 1):

            @pl.when(n == nq)
            def _(nq=nq):
                q_at = pl.ds(pl.multiple_of(lo * BLOCK, BLOCK), nq * BLOCK)
                mq, mk = mq_ref[q_at, :], mk_ref[k_at, :]
                word = word_ref[k_at, :]
                key_mask = jnp.where(low_block, word, 1.0 - word) * SCALE
                logs = [log_ref[0, lo + t] for t in range(nq)]
                dots = [dots_ref[lo + t] for t in range(nq)]
                heads, pairs = range(HEADS_PER_GROUP), range(GROUP // 128)
                qs = [qd_ref[q_at, 128 * h : 128 * h + 128] for h in heads]
                ks = [kd_ref[k_at, 128 * h : 128 * h + 128] for h in heads]
                scores = [
                    dot(jnp.concatenate([k, mk], 1), jnp.concatenate([q, mq], 1), 1, 1)
                    for q, k in zip(qs, ks)
                ]
                grad_probs = [
                    dot(v_ref[k_at, 128 * (h // 2) : 128 * (h // 2) + 128], gx_ref[h // 2, h % 2, q_at, :], 1, 1)
                    for h in heads
                ]
                probs, grads = [], []
                for h in heads:
                    log_row = jnp.concatenate([a[h : h + 1] for a in logs], 1)
                    dot_row = jnp.concatenate([a[h : h + 1] for a in dots], 1)
                    prob = jnp.exp2(scores[h] * (LOG2E * SCALE) - log_row)
                    probs.append(prob.astype(BF))
                    grads.append((prob * (grad_probs[h] - dot_row)).astype(BF))
                grad_v = [
                    dot(
                        jnp.concatenate(probs[2 * p : 2 * p + 2], 1),
                        jnp.concatenate([gx_ref[p, 0, q_at, :], gx_ref[p, 1, q_at, :]], 0),
                    )
                    for p in pairs
                ]
                grad_k = [
                    dot(jnp.concatenate(grads[2 * p : 2 * p + 2], 1), corner(*qs[2 * p : 2 * p + 2]))
                    for p in pairs
                ]
                grad_q = [
                    dot(jnp.concatenate(grads[2 * p : 2 * p + 2], 0), corner(*ks[2 * p : 2 * p + 2]), 0, 0)
                    for p in pairs
                ]
                for p in pairs:
                    a, b = grad_k[p][:, :128] * key_mask, grad_k[p][:, 128:] * key_mask
                    a, b = a + pltpu.roll(a, 64, 1), b + pltpu.roll(b, 64, 1)
                    at = 4 * GROUP + 128 * p
                    out_ref[k_at, at : at + 128] = jnp.where(low_block, a, b).astype(BF)
                    at = 5 * GROUP + 128 * p
                    out_ref[k_at, at : at + 128] = grad_v[p].astype(BF)
                    gq_ref[q_at, 256 * p : 256 * p + 256] += grad_q[p]

        return carry

    lax.fori_loop(0, blocks, key_block, 0)
    word = word_ref[...]
    entity = 1.0 - word
    for p in range(GROUP // 128):
        a = gq_ref[:, 256 * p : 256 * p + 128] * SCALE
        b = gq_ref[:, 256 * p + 128 : 256 * p + 256] * SCALE
        to_words = jnp.where(low, a, pltpu.roll(b, 64, 1))
        to_entities = jnp.where(low, pltpu.roll(a, 64, 1), b)
        made = (to_words * word, to_entities * word, to_words * entity, to_entities * entity)
        for part, value in enumerate(made):
            at = part * GROUP + 128 * p
            out_ref[:, at : at + 128] = value.astype(BF)
    all_ref[pl.ds(pl.multiple_of(s * rows, BLOCK), rows), :] = out_ref[...]

    @pl.when(s == pl.num_programs(0) - 1)
    def _():
        half = x_ref.shape[1] // 2
        for i, side in enumerate(sides(pos_ref[0])):
            left = x_ref[:, pl.ds(pl.multiple_of(side * half, 128), half)]
            outs = (send_ref.at[i], keep_ref.at[i])
            grad_parts(pos_ref, left, all_ref, outs, lambda index: [], half // 2 + EXTRA)


def call_attention_back(group, lo, n, pos, kept, grad_context, word, mq, mk, x):
    qd, kd, v, context, log_total = kept
    tokens = v.shape[0]
    seqs, blocks = lo.shape
    length = tokens // seqs
    return pl.pallas_call(
        attention_back,
        out_shape=[shaped((tokens, 6 * GROUP), BF)]
        + [shaped((2, x.shape[1] // 2 + 2 * EXTRA, 3 * GROUP), BF)] * 2,
        grid_spec=pltpu.PrefetchScalarGridSpec(
            num_scalar_prefetch=3,
            grid=(seqs,),
            in_specs=[
                row_block(length, 2 * GROUP),
                row_block(length, 2 * GROUP),
                row_block(length, GROUP),
                row_block(length, GROUP),
                row_block(length, GROUP, group),
                pl.BlockSpec((1, blocks, 8, 128), lambda i, *_: (i, 0, 0, 0)),
            ]
            + [row_block(length, 128)] * 3
            + [whole(x)],
            out_specs=[row_block(length, 6 * GROUP)]
            + [pl.BlockSpec((2, x.shape[1] // 2 + 2 * EXTRA, 3 * GROUP), lambda i, *_: (0, 0, 0))] * 2,
            scratch_shapes=[
                pltpu.VMEM((length, 2 * GROUP), F32),
                pltpu.VMEM((GROUP // 128, 2, length, 128), BF),
                pltpu.VMEM((blocks, 8, 128), F32),
                pltpu.VMEM((tokens, 6 * GROUP), BF),
            ],
        ),
        compiler_params=settings(),
        cost_estimate=cost(2e10, 12 << 20),
        name="attention_back",
    )(lo, n, pos, qd, kd, v, context, grad_context, log_total, word, mq, mk, x)


def middle(loads, spans, n_refs, n_parts, pos_ref, x_ref, g_ref, vec_ref, *rest):
    parts, rest = rest[:n_parts], rest[n_parts:]
    refs, rest = rest[:n_refs], rest[n_refs:]
    outs, scratch = rest[:10], rest[10:]
    context_ref, low_ref, act_ref, output_ref, gb_ref, gi_ref, gx_ref, ga_ref, gc_ref, small_ref = outs
    wo_ref, wi_ref, wd_ref, slope_ref, so, si, sd = scratch
    load_o = partial(copies, pos_ref, refs, loads[0], wo_ref, so)
    load_i = partial(copies, pos_ref, refs, loads[1], wi_ref, si)
    load_d = partial(copies, pos_ref, refs, loads[2], wd_ref, sd)
    start = pl.program_id(0) == 0

    @pl.when(start)
    def _():
        made = load_o()
        begin(made)
        begin(load_i())
        begin(load_d())
        small_ref[...] = jnp.zeros_like(small_ref)
        finish(made)

    take = partial(vector, vec_ref, spans)
    context = jnp.concatenate([part[...] for part in parts], 1)
    context_ref[...] = context
    attended = dot(context, wo_ref[...]) + take(B_OUTPUT)
    first_hat, first_inverse = moments(x_ref[...].astype(F32) + attended)
    gain_attn = take(GAIN_ATTN)
    first = first_hat * gain_attn + take(BIAS_ATTN)
    low = first.astype(BF)
    low_ref[...] = low

    @pl.when(start)
    def _():
        finish(load_i())

    hidden = wi_ref.shape[1]
    step = 512
    b_inner = take(B_INNER)
    for at in range(0, hidden, step):
        lanes = slice(at, at + step)
        inner = dot(low, wi_ref[:, lanes]) + b_inner[:, lanes]
        below = 0.5 * lax.erf(inner * ROOT_HALF) + 0.5
        act_ref[:, lanes] = (inner * below).astype(BF)
        bell = INV_ROOT_2PI * jnp.exp(-0.5 * inner * inner)
        slope_ref[:, lanes] = (below + inner * bell).astype(BF)

    @pl.when(start)
    def _():
        finish(load_d())

    branch = dot(act_ref[...], wd_ref[...]) + take(B_DOWN)
    hat, inverse = moments(first + branch)
    gain_ffn = take(GAIN_FFN)
    output_ref[...] = (hat * gain_ffn + take(BIAS_FFN)).astype(BF)
    g = g_ref[...].astype(F32)
    grad_sum = norm_back(g, hat, inverse, gain_ffn)
    gb = grad_sum.astype(BF)
    gb_ref[...] = gb
    small_ref[0:1] += column_sums(g * hat)
    small_ref[1:2] += column_sums(g)
    small_ref[2:3] += column_sums(gb.astype(F32))
    for at in range(0, hidden, step):
        lanes = slice(at, at + step)
        grad = dot(gb, wd_ref[lanes, :], 1, 1) * slope_ref[:, lanes].astype(F32)
        gi_ref[:, lanes] = grad.astype(BF)
    grad_first = grad_sum + dot(gi_ref[...], wi_ref[...], 1, 1)
    grad = norm_back(grad_first, first_hat, first_inverse, gain_attn)
    gx_ref[...] = grad
    ga = grad.astype(BF)
    ga_ref[...] = ga
    small_ref[3:4] += column_sums(grad_first * first_hat)
    small_ref[4:5] += column_sums(grad_first)
    small_ref[5:6] += column_sums(ga.astype(F32))
    gc_ref[...] = dot(ga, wo_ref[...], 1, 1).astype(BF)


def call_middle(pos, parts, x, g, vec, spans, refs, loads, hidden):
    tokens, width = x.shape
    rows = ROWS
    narrow, broad = row_block(rows, width), row_block(rows, hidden)
    return pl.pallas_call(
        partial(middle, loads, spans, len(refs), len(parts)),
        out_shape=[
            shaped((tokens, width), BF),
            shaped((tokens, width), BF),
            shaped((tokens, hidden), BF),
            shaped((tokens, width), BF),
            shaped((tokens, width), BF),
            shaped((tokens, hidden), BF),
            shaped((tokens, width), F32),
            shaped((tokens, width), BF),
            shaped((tokens, width), BF),
            shaped((8, width), F32),
        ],
        grid_spec=pltpu.PrefetchScalarGridSpec(
            num_scalar_prefetch=1,
            grid=(tokens // rows,),
            in_specs=[narrow, narrow, whole(vec)]
            + [row_block(rows, GROUP)] * len(parts)
            + [pl.BlockSpec(memory_space=pl.ANY)] * len(refs),
            out_specs=[narrow, narrow, broad, narrow, narrow, broad, narrow, narrow, narrow]
            + [pl.BlockSpec((8, width), lambda i, *_: (0, 0))],
            scratch_shapes=[
                pltpu.VMEM((width, width), BF),
                pltpu.VMEM((width, hidden), BF),
                pltpu.VMEM((hidden, width), BF),
                pltpu.VMEM((rows, hidden), BF),
            ]
            + [pltpu.SemaphoreType.DMA((len(load),)) for load in loads],
        ),
        compiler_params=settings(MIDDLE_VMEM),
        cost_estimate=cost(5e10, 50 << 20),
        name="middle",
    )(pos, x, g, vec, *parts, *refs)


def sides(c):
    return (1 - c, c)


def down_grad(pos_ref, left_ref, right_ref, send_ref, keep_ref, held_ref):
    half = right_ref.shape[1] // 2
    held_ref[...] = dot(left_ref[...], right_ref[...], 0, 0).astype(BF)
    for out_ref, side in zip((send_ref, keep_ref), sides(pos_ref[1])):
        out_ref[0] = held_ref[:, pl.ds(pl.multiple_of(side * half, 128), half)]


def call_down_grad(pos, left, right):
    tokens, rows = left.shape
    columns = right.shape[1]
    eighth = rows // 8

    def block(i, pos):
        place = 0
        for k, at in ((i // 4, pos[0]), (i // 2 % 2, pos[2]), (i % 2, pos[3])):
            place = 2 * place + jnp.where(k == 0, 1 - at, at)
        return (0, place)

    return pl.pallas_call(
        down_grad,
        out_shape=[shaped((2, rows // 2, columns // 2), BF)] * 2,
        grid_spec=pltpu.PrefetchScalarGridSpec(
            num_scalar_prefetch=1,
            grid=(8,),
            in_specs=[pl.BlockSpec((tokens, eighth), block), whole(right)],
            out_specs=[pl.BlockSpec((1, eighth, columns // 2), lambda i, pos: (i // 4, i % 4, 0))] * 2,
            scratch_shapes=[pltpu.VMEM((eighth, columns), BF)],
        ),
        compiler_params=settings(MOST_VMEM),
        cost_estimate=cost(1.3e10, 12 << 20),
        name="down_grad",
    )(pos, left, right)


def grad_parts(pos_ref, left, right_ref, outs, extras, out_rows):
    half = left.shape[1] // 2
    quarter = right_ref.shape[1] // 4
    c, x, z = pos_ref[1], pos_ref[2], pos_ref[3]
    for out, side in zip(outs, sides(c)):
        right = right_ref[:, pl.ds(pl.multiple_of(2 * side * quarter, 128), 2 * quarter)]
        made = dot(left, right, 0, 0).astype(BF)
        lines = column_sums(right.astype(F32))
        for part in range(2):
            mine = slice(part * quarter, (part + 1) * quarter)
            to = pl.ds(pl.multiple_of(jnp.where(x == part, quarter, 0), 128), quarter)
            below = [lines[:, mine]] + extras(2 * side + part)
            below.append(jnp.zeros((EXTRA - len(below), quarter), F32))
            below = jnp.concatenate(below, 0).astype(BF)
            for k in range(2):
                start = pl.multiple_of(jnp.where(z == k, out_rows, 0), 16)
                out[pl.ds(start, half), to] = made[k * half : (k + 1) * half, mine]
                out[k * out_rows + half : k * out_rows + half + EXTRA, to] = below


def inner_output_grad(pos_ref, left_ref, right_ref, context_ref, ga_ref, small_ref, send_ref, keep_ref, held_ref):
    vectors = [small_ref[i : i + 1] for i in range(6)]
    vectors += [jnp.zeros_like(vectors[0])] * 2

    def extras(index):
        made = []
        for first in (0, 4):
            line = vectors[first]
            for k in range(1, 4):
                line = jnp.where(index == k, vectors[first + k], line)
            made.append(line)
        return made

    outs = (send_ref.at[0], keep_ref.at[0])
    out_rows = send_ref.shape[1] // 2
    grad_parts(pos_ref, left_ref[...], right_ref, outs, extras, out_rows)
    rows = left_ref.shape[1]
    size, half = rows // 8, ga_ref.shape[1] // 2
    held_ref[...] = dot(context_ref[...], ga_ref[...], 0, 0).astype(BF)
    for out, side in zip(outs, sides(pos_ref[1])):
        lanes = pl.ds(pl.multiple_of(side * half, 128), half)
        for k, part in enumerate(sides(pos_ref[2])):
            for m, low in enumerate(sides(pos_ref[3])):
                for i in range(2):
                    at = pl.ds(pl.multiple_of((4 * part + 2 * low + i) * size, 16), size)
                    to = (2 * k + i) * half
                    out[(m + 1) * out_rows - size : (m + 1) * out_rows, to : to + half] = held_ref[at, lanes]


def call_inner_output_grad(pos, left, right, context, ga, small):
    tokens, rows = left.shape
    columns = right.shape[1]
    half = rows // 2
    out_rows = half + 2 * EXTRA + half // 4
    block = pl.BlockSpec((tokens, half), lambda i, pos: (0, jnp.where(i == 0, 1 - pos[0], pos[0])))
    return pl.pallas_call(
        inner_output_grad,
        out_shape=[shaped((2, out_rows, columns // 2), BF)] * 2,
        grid_spec=pltpu.PrefetchScalarGridSpec(
            num_scalar_prefetch=1,
            grid=(2,),
            in_specs=[block, whole(right), block, whole(ga), whole(small)],
            out_specs=[pl.BlockSpec((1, out_rows, columns // 2), lambda i, pos: (i, 0, 0))] * 2,
            scratch_shapes=[pltpu.VMEM((half, ga.shape[1]), BF)],
        ),
        compiler_params=settings(MOST_VMEM),
        cost_estimate=cost(1.8e10, 16 << 20),
        name="inner_grad",
    )(pos, left, right, context, ga, small)


def plus(*terms):
    total = terms[0].astype(F32)
    for term in terms[1:]:
        total = total + term.astype(F32)
    return total.astype(BF)


def add_parts(dim, mine_ref, come_ref, *out_refs):
    if dim is None:
        out_refs[0][...] = plus(mine_ref[...], come_ref[...])
        return
    size = mine_ref.shape[dim] // 2
    for k, out_ref in enumerate(out_refs):
        if len(mine_ref.shape) == 3:
            at = k
        else:
            part = pl.ds(k * size, size)
            at = (part, slice(None)) if dim == 0 else (slice(None), part)
        out_ref[...] = plus(mine_ref[at], come_ref[at])


def put_together(mine_ref, come_ref, out_ref):
    rows = mine_ref.shape[0]
    out_ref[:rows, :] = mine_ref[...]
    out_ref[rows:, :] = come_ref[...]


def pair_call(kernel, name, mine, come, shapes):
    return pl.pallas_call(
        kernel,
        out_shape=[shaped(shape, BF) for shape in shapes],
        in_specs=[pl.BlockSpec(memory_space=pltpu.VMEM)] * 2,
        out_specs=[pl.BlockSpec(memory_space=pltpu.VMEM)] * len(shapes),
        compiler_params=pltpu.CompilerParams(vmem_limit_bytes=VMEM),
        cost_estimate=cost(1000, 1000),
        name=name,
    )(mine, come)


def add_call(dim, mine, come):
    shape = mine.shape
    if dim is None:
        shapes = [shape]
    elif len(shape) == 3:
        shapes = [shape[1:]] * 2
    else:
        shapes = [tuple(size // 2 if i == dim else size for i, size in enumerate(shape))] * 2
    return pair_call(partial(add_parts, dim), "add", mine, come, shapes)


def small_call(kernel, name, pos, inputs, shapes):
    return pl.pallas_call(
        kernel,
        out_shape=[shaped(shape, dtype) for shape, dtype in shapes],
        in_specs=[pl.BlockSpec(memory_space=pltpu.SMEM)]
        + [pl.BlockSpec(memory_space=pltpu.VMEM)] * len(inputs),
        out_specs=[pl.BlockSpec(memory_space=pltpu.VMEM)] * len(shapes),
        compiler_params=pltpu.CompilerParams(vmem_limit_bytes=VMEM),
        cost_estimate=cost(3e9, 4 << 20),
        name=name,
    )(pos, *inputs)


def corners(pos_ref):
    c, x = pos_ref[1], pos_ref[2]
    return ((c, x), (c, 1 - x), (1 - c, x), (1 - c, 1 - x))


def join_down(pos_ref, *rest):
    out_ref = rest[4]
    z = pos_ref[3]
    for ref, (c, x) in zip(rest[:4], corners(pos_ref)):
        rows, columns = ref.shape[0] // 2, ref.shape[1]
        lanes = pl.ds(pl.multiple_of(c * columns, 128), columns)
        for m, low in enumerate((z, 1 - z)):
            at = pl.ds(pl.multiple_of((2 * x + low) * rows, 16), rows)
            out_ref[at, lanes] = ref[m * rows : (m + 1) * rows, :].astype(F32)


def join_inner(pos_ref, *rest):
    out_ref, output_ref, extra_ref = rest[4:]
    z = pos_ref[3]
    for ref, (c, x) in zip(rest[:4], corners(pos_ref)):
        columns = ref.shape[1]
        rows = out_ref.shape[0] // 2
        held = ref.shape[0] // 2
        lanes = pl.ds(pl.multiple_of((2 * c + x) * columns, 128), columns)
        extra_ref[:, lanes] = ref[rows : rows + EXTRA, :].astype(F32)
        size, half = rows // 4, columns // 2
        for m, low in enumerate((z, 1 - z)):
            at = pl.ds(pl.multiple_of(low * rows, 16), rows)
            out_ref[at, lanes] = ref[m * held : m * held + rows, :].astype(F32)
            for i in range(2):
                at = pl.ds(pl.multiple_of((4 * x + 2 * low + i) * size, 16), size)
                to = pl.ds(pl.multiple_of(c * half, 128), half)
                value = ref[(m + 1) * held - size : (m + 1) * held, i * half : (i + 1) * half]
                output_ref[at, to] = value.astype(F32)


def join_groups(n_pieces, pos_ref, *rest):
    wide_ref, parts, outs = rest[0], rest[1 : 1 + 4 * n_pieces], rest[1 + 4 * n_pieces :]
    query_ref, key_value_ref, small_ref, extra_ref = outs
    width = GROUP * n_pieces
    rows = query_ref.shape[0] // 2
    z = pos_ref[3]
    mine = 2 * pos_ref[1] + pos_ref[2]
    for case in range(4):

        @pl.when(mine == case)
        def _(case=case):
            for piece in range(n_pieces):
                for k in range(4):
                    ref = parts[4 * piece + k]
                    columns = ref.shape[1]
                    held = ref.shape[0] // 2
                    start = (case ^ k) * columns
                    extra_ref[piece, :, start : start + columns] = ref[rows:held, :].astype(F32)
                    for at in range(0, columns, 128):
                        block, more = divmod(start + at, GROUP)
                        to = query_ref if block < 4 else key_value_ref
                        first = block % 4 * width + piece * GROUP + more
                        for m, low in enumerate((z, 1 - z)):
                            there = pl.ds(pl.multiple_of(low * rows, 16), rows)
                            value = ref[m * held : m * held + rows, at : at + 128]
                            to[there, first : first + 128] = value.astype(F32)

    late = [extra_ref[k, 0:1, :] for k in range(n_pieces)]
    query = jnp.concatenate(
        [row[:, k * GROUP : (k + 1) * GROUP] for k in range(4) for row in late], 1
    )
    value = jnp.concatenate([row[:, 5 * GROUP :] for row in late], 1)
    early = [wide_ref[1 + i : 2 + i, k * width : (k + 1) * width] for i in range(2) for k in range(4)]
    gain_ffn, bias_ffn, b_down, gain_attn, bias_attn, b_output = early[:6]
    wide = wide_ref[0:1, :]
    order = (query, value, b_output, gain_attn, bias_attn, wide, b_down, gain_ffn, bias_ffn)
    lower = jnp.concatenate([v[:, : v.shape[1] // 2] for v in order], 1)
    upper = jnp.concatenate([v[:, v.shape[1] // 2 :] for v in order], 1)
    small_ref[...] = jnp.where(pos_ref[0] == 0, lower, upper)


def pack_kernel(loads, n_refs, n_outs, pos_ref, *rest):
    refs, outs, sems = rest[:n_refs], rest[n_refs : n_refs + n_outs], rest[-1]
    made = copies(
        pos_ref, refs, [load[:3] for load in loads], [outs[load[3]] for load in loads], sems
    )
    begin(made)
    finish(made)


def call_pack(pos, refs, shapes, loads):
    return pl.pallas_call(
        partial(pack_kernel, loads, len(refs), len(shapes)),
        out_shape=[shaped(shape, BF) for shape in shapes],
        in_specs=[pl.BlockSpec(memory_space=pltpu.SMEM)]
        + [pl.BlockSpec(memory_space=pl.ANY)] * len(refs),
        out_specs=[pl.BlockSpec(memory_space=pltpu.VMEM)] * len(shapes),
        scratch_shapes=[pltpu.SemaphoreType.DMA((len(loads),))],
        compiler_params=pltpu.CompilerParams(vmem_limit_bytes=MOST_VMEM),
        cost_estimate=cost(2e9, 2 << 20),
        name="pack",
    )(pos, *refs)


def token_grad(loads, n_refs, n_parts, pos_ref, sum_ref, *rest):
    parts, rest = rest[:n_parts], rest[n_parts:]
    refs, rest = rest[:n_refs], rest[n_refs:]
    out_ref, w_ref, sems = rest
    load = [partial(copies, pos_ref, refs, loads[k], w_ref.at[k], sems.at[k]) for k in range(n_parts)]
    start = pl.program_id(0) == 0

    @pl.when(start)
    def _():
        for one in load:
            begin(one())

    total = sum_ref[...]
    for k in range(n_parts):

        @pl.when(start)
        def _(k=k):
            finish(load[k]())

        total = total + dot(parts[k][...], w_ref[k], 1, 1)
    out_ref[...] = total.astype(out_ref.dtype)


def call_token_grad(pos, parts, summed, refs, loads, kind):
    tokens, width = summed.shape
    columns = parts[0].shape[1]
    rows = TOKEN_ROWS
    return pl.pallas_call(
        partial(token_grad, loads, len(refs), len(parts)),
        out_shape=shaped((tokens, width), kind),
        grid_spec=pltpu.PrefetchScalarGridSpec(
            num_scalar_prefetch=1,
            grid=(tokens // rows,),
            in_specs=[row_block(rows, width)]
            + [row_block(rows, columns)] * len(parts)
            + [pl.BlockSpec(memory_space=pl.ANY)] * len(refs),
            out_specs=row_block(rows, width),
            scratch_shapes=[
                pltpu.VMEM((len(parts), width, columns), BF),
                pltpu.SemaphoreType.DMA((len(parts), len(loads[0]))),
            ],
        ),
        compiler_params=settings(),
        cost_estimate=cost(8e9 * len(parts), 12 << 20),
        name="token_grad",
    )(pos, summed, *parts, *refs)


def facts(first_ref, segments_ref, kinds_ref, lo_ref, n_ref, word_ref, mq_ref, mk_ref):
    seqs, length = segments_ref.shape
    blocks = length // BLOCK
    lane = lax.broadcasted_iota(jnp.int32, (BLOCK, 128), 1)

    def column(ref, s, i):
        row = ref[s : s + 1, i * BLOCK : (i + 1) * BLOCK].astype(F32)
        return jnp.transpose(jnp.broadcast_to(row, (128, BLOCK)))

    for s in range(seqs):
        for i in range(blocks):
            at = slice((s * blocks + i) * BLOCK, (s * blocks + i + 1) * BLOCK)
            word_ref[at, :] = jnp.where(column(kinds_ref, s, i) == 0.0, 1.0, 0.0)
            own = column(segments_ref, s, i) == lane.astype(F32)
            mk_ref[at, :] = jnp.where(own, 1.0, 0.0).astype(BF)
            mq_ref[at, :] = jnp.where(own, 0.0, jnp.where(lane < 4, -FAR, 0.0)).astype(BF)
            lo, n = 0, 0
            for j in range(blocks - 1, -1, -1):
                meets = jnp.logical_and(
                    first_ref[s, j * BLOCK] <= first_ref[s, (i + 1) * BLOCK - 1],
                    first_ref[s, i * BLOCK] <= first_ref[s, (j + 1) * BLOCK - 1],
                )
                lo = jnp.where(meets, j, lo)
                n = n + jnp.where(meets, 1, 0)
            lo_ref[s, i] = lo
            n_ref[s, i] = n


def document_facts(segments, kinds):
    seqs, length = segments.shape
    tokens, blocks = seqs * length, length // BLOCK
    smem, vmem = pl.BlockSpec(memory_space=pltpu.SMEM), pl.BlockSpec(memory_space=pltpu.VMEM)
    return pl.pallas_call(
        facts,
        out_shape=[
            shaped((seqs, blocks), jnp.int32),
            shaped((seqs, blocks), jnp.int32),
            shaped((tokens, 128), F32),
            shaped((tokens, 128), BF),
            shaped((tokens, 128), BF),
        ],
        in_specs=[smem, vmem, vmem],
        out_specs=[smem, smem, vmem, vmem, vmem],
        compiler_params=pltpu.CompilerParams(vmem_limit_bytes=VMEM),
        cost_estimate=cost(1000, 1000),
        name="facts",
    )(segments, segments, kinds)


def gathered_vectors(sizes, everyone):
    spans, parts, at, start = [], [], 0, 0
    for size in sizes:
        parts.append(everyone[:, at : at + size].reshape(1, -1))
        spans.append((start, size * everyone.shape[0]))
        at += size
        start += size * everyone.shape[0]
    return jnp.concatenate(parts, 1).astype(F32), spans


def tie(value, deps):
    return lax.optimization_barrier((value, *deps))[0] if deps else value


def by_dp(bit):
    return lambda v: lax.ppermute(v, DP, [(i, i ^ bit) for i in range(16)])


def over_y(v):
    return lax.ppermute(v, FSDP, [(0, 1), (1, 0)])


over_core, over_x, over_z, over_far_z = (by_dp(1 << k) for k in range(4))


class NearWeights:
    def __init__(self, weights, vectors, pos, width, hidden):
        self.weights, self.pos, self.width = weights, pos, width
        groups = width // GROUP
        self.shard, self.part = width // 2, width // 8
        self.d_shard, self.d_part = hidden // 2, hidden // 8
        self.columns = 2 * width
        o_rows, i_rows, d_rows = self.part // 2, self.part, self.d_part // 2
        self.rows = o_rows, i_rows, d_rows

        def chunk(size, more=0):
            return lambda pos: (2 * pos[2] + pos[1]) * size + more

        def group_loads(group, to, row):
            return [
                (source, ((chunk(self.part), self.part), (column, GROUP)), ((row, self.part), (k * GROUP, GROUP)), to)
                for k, (source, column) in enumerate(group_columns(group, width))
            ]

        lines = -(-vectors.shape[0] // self.columns)
        vectors = jnp.pad(vectors, (0, lines * self.columns - vectors.shape[0])).reshape(lines, self.columns)
        at = (0, lines), (0, self.columns)
        below = (2, at, ((self.part, lines), (0, self.columns)), 0)
        shape = (self.part + EXTRA, self.columns)
        first = call_pack(pos, weights[:2] + [vectors], [shape], group_loads(0, 0, 0) + [below])[0]
        loads = []
        for group in range(1, groups):
            loads += group_loads(group, 0, (group - 1) * self.part)
        for side in range(2):
            at = (side * width, width)
            loads.append((2, ((chunk(self.part, side * o_rows), o_rows), (0, width)), ((0, o_rows), at), 1))
            loads.append(
                (
                    3,
                    ((chunk(self.part), i_rows), (side * self.columns, self.columns)),
                    ((o_rows + side * i_rows, i_rows), (0, self.columns)),
                    1,
                )
            )
            loads.append((4, ((chunk(self.d_part, side * d_rows), d_rows), (0, width)), ((0, d_rows), at), 2))
        shapes = [(groups - 1) * self.part, o_rows + 2 * i_rows, d_rows]
        self.from_y = [over_y(first)]
        packs = call_pack(tie(pos, (first,)), weights, [(rows, self.columns) for rows in shapes], loads)
        self.from_y += [over_y(v) for v in packs]
        other = self.from_y[0][self.part : self.part + lines]
        both = jnp.where(pos[0] == 0, jnp.stack([vectors, other]), jnp.stack([other, vectors]))
        self.vec = both.reshape(2, lines * self.columns).astype(F32)
        self.arrived = [None] * 4

    def spread(self, k, before_x=(), before_core=()):
        v = tie(self.from_y[k], before_x)
        from_x = over_x(v)
        self.arrived[k] = [v, from_x, over_core(v), over_core(tie(from_x, before_core))]

    def others(self, size, more=0):
        other = lambda turn: lambda pos: (4 * (1 - pos[0]) + ((2 * pos[2] + pos[1]) ^ turn)) * size + more
        return [other(turn) for turn in (0, 2, 1, 3)]

    def own(self, size):
        return lambda pos: pos[0] * size

    def group(self, group):
        width, part = self.width, self.part
        loads = [
            (source, ((0, self.shard), (column, GROUP)), ((self.own(self.shard), self.shard), (k * GROUP, GROUP)))
            for k, (source, column) in enumerate(group_columns(group, width))
        ]
        row = 0 if group == 0 else (group - 1) * part
        for k, place in enumerate(self.others(part)):
            at = (0, self.columns)
            loads.append((2 + k, ((row, part), at), ((place, part), at)))
        return self.weights[:2] + self.arrived[min(group, 1)], loads

    def rest(self):
        width, columns = self.width, self.columns
        o_rows, i_rows, d_rows = self.rows
        whole_o, whole_i = (0, width), (0, 2 * columns)
        loads = [
            [(0, ((0, self.shard), whole_o), ((self.own(self.shard), self.shard), whole_o))],
            [(1, ((0, self.shard), whole_i), ((self.own(self.shard), self.shard), whole_i))],
            [(2, ((0, self.d_shard), whole_o), ((self.own(self.d_shard), self.d_shard), whole_o))],
        ]
        for side in range(2):
            at = (side * width, width)
            for k, place in enumerate(self.others(self.part, side * o_rows)):
                loads[0].append((3 + k, ((0, o_rows), at), ((place, o_rows), whole_o)))
            for k, place in enumerate(self.others(self.part)):
                from_rows = (o_rows + side * i_rows, i_rows)
                to = (side * columns, columns)
                loads[1].append((3 + k, (from_rows, (0, columns)), ((place, i_rows), to)))
            for k, place in enumerate(self.others(self.d_part, side * d_rows)):
                loads[2].append((7 + k, ((0, d_rows), at), ((place, d_rows), whole_o)))
        return self.weights[2:] + self.arrived[2] + self.arrived[3], loads


class FarWeights:
    def __init__(self, weights, vectors, sizes, width, hidden):
        self.weights = [lax.all_gather(v, FSDP, axis=0, tiled=True) for v in weights]
        self.vec, self.spans = gathered_vectors(sizes, lax.all_gather(vectors, FSDP))
        self.width = width

    def group(self, group):
        rows = (0, self.width)
        loads = [
            (source, (rows, (column, GROUP)), (rows, (k * GROUP, GROUP)))
            for k, (source, column) in enumerate(group_columns(group, self.width))
        ]
        return self.weights[:2], loads

    def rest(self):
        loads = []
        for k, v in enumerate(self.weights[2:]):
            spec = tuple((0, size) for size in v.shape)
            loads.append([(k, spec, spec)])
        return self.weights[2:], loads


def group_columns(group, width):
    blocks = [(0, part * width + group * GROUP) for part in range(4)]
    return blocks + [(1, part * width + group * GROUP) for part in range(2)]


def body(mesh_shape, hidden_in, segments, kinds, *rest):
    weights = [rest[i] for i in (0, 2, 4, 8, 10)]
    vectors = [rest[i] for i in (1, 3, 5, 6, 7, 9, 11, 12, 13)]
    near = mesh_shape[DP] == 16 and mesh_shape[FSDP] == 2
    seqs, length, width = hidden_in.shape
    tokens = seqs * length
    groups = width // GROUP
    x = hidden_in.reshape(tokens, width)
    g = rest[14].reshape(tokens, width)
    fsdp = mesh_shape[FSDP]
    hidden = weights[4].shape[0] * fsdp
    y, place = lax.axis_index(FSDP), lax.axis_index(DP)
    sizes = [v.shape[0] for v in vectors]
    total, start, parts, spans = sum(sizes), 0, [], []
    for v, size in zip(vectors, sizes):
        parts.append(lax.pad(v, jnp.zeros((), BF), [(start, total - start - size, 0)]))
        spans.append((start, size))
        start += size
    vector_shard = sum(parts[1:], parts[0])
    if near:
        bits = jnp.array([0, 1, 2, 4], jnp.int32)
        pos = jnp.stack([y, place & 1, (place >> 1) & 1, (place >> 2) & 1]).astype(jnp.int32)
        source = NearWeights(weights, vector_shard, pos, width, hidden)
        source.spread(0)
    else:
        pos = jnp.ones((4,), jnp.int32)
        source = FarWeights(weights, vector_shard, sizes, width, hidden)
        spans = source.spans
    vec = source.vec
    lo, n, word, mq, mk = document_facts(segments, kinds)
    kept = []
    for group in range(groups):
        deps = tuple(k[3] for k in kept[-1:])
        if near and group == 0:
            deps = (source.from_y[1],)
        if near and group == 1:
            source.spread(1, (), (kept[0][3],))
        refs, loads = source.group(group)
        kept.append(
            call_qkv_attention(
                group, lo, n, pos, tie(x, deps), vec, spans, word, mq, mk, refs, loads
            )
        )
    if near:
        source.spread(2, (kept[0][3],), (kept[1][3],))
        source.spread(3, (kept[1][3],), (kept[2][3],))
    refs, loads = source.rest()
    context, first_low, act, output, gb, gi, gx, ga, gc, small_sums = call_middle(
        pos, [k[3] for k in kept], x, g, vec, spans, refs, loads, hidden
    )

    made, sent, partial_sums, results = {}, {}, [], {}

    def run(kernel, deps):
        kind, k = kernel
        if kind == DOWN:
            made[kind] = call_down_grad(pos, tie(act, deps), gb)
            return tuple(made[kind][:1])
        if kind == INNER:
            made[kind] = call_inner_output_grad(pos, tie(first_low, deps), gi, context, ga, small_sums)
            return tuple(made[kind][:1])
        if kind == ATTENTION:
            part, *made[k] = call_attention_back(
                k, lo, n, pos, kept[k], tie(gc, deps), word, mq, mk, x
            )
            partial_sums.append(part)
            return (part,)
        held = [source.group(i) for i in k]
        count = len(held[0][0])
        results[TOKEN] = call_token_grad(
            pos, [partial_sums[i] for i in k], tie(results.get(TOKEN, gx), deps),
            [ref for refs, _ in held for ref in refs],
            [[(load[0] + i * count,) + load[1:] for load in loads] for i, (_, loads) in enumerate(held)],
            BF if groups - 1 in k else F32,
        )
        return (results[TOKEN],)

    def advance(k, step, deps):
        if step == 0:
            sent[k] = (over_core(made[k][0]), made[k][1])
            return ()
        come, mine = sent[k]
        come = tie(come, deps)
        if step == 1:
            out = add_call(0, mine, come)
            sent[k] = (over_y(out[0]), out[1])
        elif step in (2, 3):
            out = add_call(1 if step == 2 and k != DOWN else 0, mine, come)
            sent[k] = ((over_x if step == 2 else over_z)(out[0]), out[1])
        elif step in (4, 5):
            out = add_call(None, mine, come)
            sent[k] = ((over_far_z if step == 4 else over_z)(out[0]), out[0])
        elif step == 6:
            rows, columns = mine.shape
            out = pair_call(put_together, "put_together", mine, come, [(2 * rows, columns)])
            sent[k] = (over_x(out[0]), [out[0], over_core(out[0])])
        elif step == 7:
            out = [come]
            sent[k] = (over_core(come), [mine[0], come, mine[1]])
        else:
            sent[k] = [*mine, come]
            return finished(k)
        return tuple(out)

    def finished(k):
        shard = width // 2
        if k == DOWN:
            results[k] = small_call(join_down, "join_down", pos, sent[k], [((hidden // 2, width), F32)])
        elif k == INNER:
            results[k] = small_call(
                join_inner, "join_inner", pos, sent[k],
                [((shard, hidden), F32), ((shard, width), F32), ((EXTRA, hidden), F32)],
            )
        else:
            return tuple(sent[k])
        return tuple(results[k])

    kernels = [(DOWN, 0), (INNER, 0)] + [(ATTENTION, k) for k in range(groups)]
    kernels += [(TOKEN, [k]) for k in range(groups)]
    if near:
        base, since, tail = (), (), False
        for item in PLAN:
            if item is None:
                tail = True
            elif isinstance(item, tuple):
                made_now = advance(*item, base)
                base, since = (made_now or base, ()) if tail else (base, since + made_now)
            else:
                base = run(kernels[item], base if tail else since)
                since = () if tail else base
        grad_inner, grad_output, extra = results[INNER]
        shard = width // 2
        grad_query, grad_key_value, small, _ = small_call(
            partial(join_groups, groups), "join_groups", pos,
            [extra] + [v for k in range(groups) for v in sent[k]],
            [
                ((shard, 4 * width), F32),
                ((shard, 2 * width), F32),
                ((1, total), F32),
                ((groups, EXTRA, 6 * GROUP), F32),
            ],
        )
        small = small.reshape(total)
        shares = [small[start : start + size] for start, size in spans]
        grad_down = results[DOWN][0]
    else:
        for kernel in kernels:
            run(kernel, ())

        def flat(v):
            return v.reshape(v.shape[0], -1).astype(F32)

        def far(v):
            return lax.psum(lax.psum_scatter(v, FSDP, scatter_dimension=0, tiled=True), DP)

        def main_and_extra(k, rows):
            both = jnp.stack(made[k], 2).reshape(2, 2, made[k][0].shape[1] // 2, 2, -1)
            main = both[:, :, :rows].reshape(4 * rows, 2, -1)
            more = both[1, 1, rows : rows + EXTRA]
            return flat(far(main)), flat(lax.psum(more, (DP, FSDP)))

        rows = width // 4
        grad_inner, wide = main_and_extra(INNER, rows)
        grad_down = flat(far(jnp.stack(made[DOWN], 2).reshape(hidden, 2, -1)))
        out = jnp.stack(made[INNER], 0).reshape(2, 2, 2, -1, hidden // 2)[:, :, :, rows + EXTRA :]
        size = out.shape[3]
        out = out.reshape(2, 2, 2, size, 2, 2, width // 2).transpose(1, 4, 2, 5, 3, 0, 6)
        grad_output = flat(far(out.reshape(width, 2, -1)))
        by_group, late = zip(*[main_and_extra(k, rows) for k in range(groups)])
        late = [e[0] for e in late]
        early = [wide[1 + i, k * width : (k + 1) * width] for i in range(2) for k in range(4)]
        gain_ffn, bias_ffn, b_down, gain_attn, bias_attn, b_output = early[:6]
        query = jnp.concatenate([e[k * GROUP : (k + 1) * GROUP] for k in range(4) for e in late])
        value = jnp.concatenate([e[5 * GROUP :] for e in late])
        order = (query, value, b_output, gain_attn, bias_attn, wide[0], b_down, gain_ffn, bias_ffn)
        shares = [lax.dynamic_slice_in_dim(v, y * size, size, 0) for v, size in zip(order, sizes)]
        grad_query = jnp.concatenate(
            [m[:, k * GROUP : (k + 1) * GROUP] for k in range(4) for m in by_group], 1
        )
        grad_key_value = jnp.concatenate(
            [m[:, k * GROUP : (k + 1) * GROUP] for k in range(4, 6) for m in by_group], 1
        )
    return (
        output.reshape(seqs, length, width),
        results[TOKEN].reshape(seqs, length, width),
        grad_query,
        shares[B_QUERY],
        grad_key_value,
        shares[B_VALUE],
        grad_output,
        shares[B_OUTPUT],
        shares[GAIN_ATTN],
        shares[BIAS_ATTN],
        grad_inner,
        shares[B_INNER],
        grad_down,
        shares[B_DOWN],
        shares[GAIN_FFN],
        shares[BIAS_FFN],
    )


DOWN, INNER, ATTENTION, TOKEN = range(-4, 0)
PLAN = (
    0, (DOWN, 0), 1, (DOWN, 1), (INNER, 0), 2, (INNER, 1), 3, (DOWN, 2), (0, 0), 4, (DOWN, 3), None, (2,
    0), (1, 0), (0, 1), (DOWN, 4), (INNER, 2), (1, 1), 5, (0, 2), (DOWN, 5), (2, 1), (INNER, 3), (1, 2),
    (DOWN, 6), (0, 3), (INNER, 4), (1, 3), (2, 2), (0, 4), 6, 7, (INNER, 5), (2, 3), (1, 4), (DOWN, 7),
    (DOWN, 8), (0, 5), (INNER, 6), (2, 4), (0, 6), (1, 5), (2, 5), (1, 6), (INNER, 7), (0, 7), (2, 6),
    (INNER, 8), (0, 8), (1, 7), (1, 8), (2, 7), (2, 8),
)
def solution(mesh):
    split = P((DP, FSDP), None, None)
    tokens = P((DP, FSDP), None)
    matrix, line = P(FSDP, None), P(FSDP)
    weights = (matrix, line, matrix, line, matrix, line, line, line, matrix, line, matrix, line, line, line)
    return jax.shard_map(
        partial(body, dict(mesh.shape)),
        mesh=mesh,
        in_specs=(split, tokens, tokens) + weights + (split,),
        out_specs=(split, split) + weights,
        check_vma=False,
    )
```

```python
from functools import partial

import jax
import jax.numpy as jnp
from jax import lax
from jax.experimental import pallas as pl
from jax.experimental.pallas import tpu as pltpu
from jax.sharding import PartitionSpec as P

F32 = jnp.float32
BF = jnp.bfloat16
HEAD = 64
HEADS_PER_GROUP = 4
GROUP = HEAD * HEADS_PER_GROUP
BLOCK = 128
EXTRA = 16
EPS = 1e-05
LOG2E = 1.4426950408889634
SCALE = HEAD**-0.5
ROOT_HALF = 0.7071067811865476
INV_ROOT_2PI = 0.3989422804014327
FAR = float(2.0**33)
VMEM = 24 << 20
MIDDLE_VMEM = 56 << 20
MOST_VMEM = 60 << 20
DP, FSDP = "dp", "fsdp"
VECTORS = range(9)
B_QUERY, B_VALUE, B_OUTPUT, GAIN_ATTN, BIAS_ATTN, B_INNER, B_DOWN, GAIN_FFN, BIAS_FFN = VECTORS
ROWS = 320
TOKEN_ROWS = 320


def dot(left, right, over_left=1, over_right=0):
    return lax.dot_general(
        left, right, (((over_left,), (over_right,)), ((), ())), preferred_element_type=F32
    )


def shaped(shape, dtype):
    return jax.ShapeDtypeStruct(shape, dtype)


def low_lanes(rows):
    return lax.broadcasted_iota(jnp.int32, (rows, 128), 1) < HEAD


def column_sums(values):
    return jnp.sum(values, axis=0, keepdims=True)


def row_block(rows, columns, part=0):
    return pl.BlockSpec((rows, columns), lambda i, *_: (i, part))


def whole(array):
    return pl.BlockSpec(array.shape, lambda i, *_: (0,) * array.ndim)


def settings(vmem=VMEM):
    return pltpu.CompilerParams(vmem_limit_bytes=vmem, dimension_semantics=("arbitrary",))


def cost(flops, nbytes):
    return pl.CostEstimate(flops=int(flops), bytes_accessed=int(nbytes), transcendentals=0)


def spans_of(spec, position):
    made = []
    for start, size in spec:
        if callable(start):
            start = pl.multiple_of(start(position), 16)
        made.append(pl.ds(start, size))
    return tuple(made)


def copies(position, refs, loads, targets, sems):
    made = []
    for i, (source, spec, to) in enumerate(loads):
        target = targets[i] if isinstance(targets, list) else targets
        made.append(
            pltpu.make_async_copy(
                refs[source].at[spans_of(spec, position)],
                target.at[spans_of(to, position)],
                sems.at[i],
            )
        )
    return made


def begin(made):
    for copy in made:
        copy.start()


def finish(made):
    for copy in made:
        copy.wait()


def moments(summed):
    center = summed - jnp.mean(summed, axis=-1, keepdims=True)
    inverse = lax.rsqrt(jnp.mean(center * center, axis=-1, keepdims=True) + EPS)
    return center * inverse, inverse


def norm_back(grad, hat, inverse, gain):
    scaled = grad * gain
    return inverse * (
        scaled
        - jnp.mean(scaled, axis=-1, keepdims=True)
        - hat * jnp.mean(scaled * hat, axis=-1, keepdims=True)
    )


def vector(vec_ref, spans, name):
    start, size = spans[name]
    rows = [vec_ref[i : i + 1, start : start + size] for i in range(vec_ref.shape[0])]
    return rows[0] if len(rows) == 1 else jnp.concatenate(rows, 1)


def qkv_attention(loads, spans, group, n_refs, lo_ref, n_ref, at_ref, x_ref, vec_ref, word_ref, mq_ref, mk_ref, *rest):
    refs, rest = rest[:n_refs], rest[n_refs:]
    qd_ref, kd_ref, v_ref, context_ref, log_ref, w_ref, vx_ref, sems = rest
    s = pl.program_id(0)

    @pl.when(s == 0)
    def _():
        made = copies(at_ref, refs, loads, w_ref, sems)
        begin(made)
        finish(made)

    x = x_ref[...]
    rows, width = x.shape
    blocks = rows // BLOCK
    word = word_ref[...]
    low = low_lanes(rows)
    key_mask = jnp.where(low, word, 1.0 - word)
    is_word = jnp.concatenate([word] * (GROUP // 128), 1) > 0.5

    def project(part, name, at):
        made = dot(x, w_ref[:, part * GROUP : (part + 1) * GROUP])
        if name is None:
            return made
        start = at + group * GROUP
        return made + vector(vec_ref, spans, name)[:, start : start + GROUP]

    to_words = jnp.where(
        is_word, project(0, B_QUERY, 0), project(2, B_QUERY, 2 * width)
    )
    to_entities = jnp.where(
        is_word, project(1, B_QUERY, width), project(3, B_QUERY, 3 * width)
    )
    keys = project(4, None, 0).astype(BF).astype(F32)
    vals = project(5, B_VALUE, 0).astype(BF)
    v_ref[...] = vals
    for p in range(GROUP // 128):
        lanes = slice(128 * p, 128 * p + 128)
        a, e, k = to_words[:, lanes], to_entities[:, lanes], keys[:, lanes]
        first, second = slice(256 * p, 256 * p + 128), slice(256 * p + 128, 256 * p + 256)
        qd_ref[:, first] = jnp.where(low, a, pltpu.roll(e, 64, 1)).astype(BF)
        qd_ref[:, second] = jnp.where(low, pltpu.roll(a, 64, 1), e).astype(BF)
        turned = pltpu.roll(k, 64, 1)
        kd_ref[:, first] = (jnp.where(low, k, turned) * key_mask).astype(BF)
        kd_ref[:, second] = (jnp.where(low, turned, k) * key_mask).astype(BF)
        v = vals[:, lanes].astype(F32)
        zero, one = jnp.zeros_like(v), jnp.ones_like(v)
        vx_ref[p, 0] = jnp.concatenate(
            [jnp.where(low, v, zero), jnp.where(low, one, zero)], 1
        ).astype(BF)
        vx_ref[p, 1] = jnp.concatenate(
            [jnp.where(low, zero, v), jnp.where(low, zero, one)], 1
        ).astype(BF)
    low_block = low_lanes(BLOCK)

    def query_block(i, carry):
        lo, n = lo_ref[s, i], n_ref[s, i]
        q_at = pl.ds(pl.multiple_of(i * BLOCK, BLOCK), BLOCK)
        for nk in range(1, blocks + 1):

            @pl.when(n == nk)
            def _(nk=nk):
                k_at = pl.ds(pl.multiple_of(lo * BLOCK, BLOCK), nk * BLOCK)
                mq, mk = mq_ref[q_at, :], mk_ref[k_at, :]
                heads, pairs = range(HEADS_PER_GROUP), range(GROUP // 128)
                scores = []
                for h in heads:
                    q = jnp.concatenate([qd_ref[q_at, 128 * h : 128 * h + 128], mq], 1)
                    k = jnp.concatenate([kd_ref[k_at, 128 * h : 128 * h + 128], mk], 1)
                    scores.append(dot(q, k, 1, 1))
                tops = [jnp.max(score, axis=1, keepdims=True) for score in scores]
                parts = [
                    jnp.exp2((score - top) * (LOG2E * SCALE)).astype(BF)
                    for score, top in zip(scores, tops)
                ]
                made = [
                    dot(
                        jnp.concatenate(parts[2 * p : 2 * p + 2], 1),
                        jnp.concatenate([vx_ref[p, 0, k_at, :], vx_ref[p, 1, k_at, :]], 0),
                    )
                    for p in pairs
                ]
                logs = []
                for p in pairs:
                    total = made[p][:, 128:]
                    context_ref[q_at, 128 * p : 128 * p + 128] = (made[p][:, :128] / total).astype(BF)
                    top = jnp.where(low_block, tops[2 * p], tops[2 * p + 1])
                    log_total = jnp.transpose(top * (LOG2E * SCALE) + jnp.log2(total))
                    logs += [log_total[0:1], log_total[64:65]]
                logs.append(jnp.zeros((8 - HEADS_PER_GROUP, 128), F32))
                log_ref[0, i] = jnp.concatenate(logs, 0)

        return carry

    lax.fori_loop(0, blocks, query_block, 0)


def call_qkv_attention(group, lo, n, at, x, vec, spans, word, mq, mk, refs, loads):
    tokens, width = x.shape
    seqs, blocks = lo.shape
    length = tokens // seqs
    return pl.pallas_call(
        partial(qkv_attention, loads, spans, group, len(refs)),
        out_shape=[
            shaped((tokens, 2 * GROUP), BF),
            shaped((tokens, 2 * GROUP), BF),
            shaped((tokens, GROUP), BF),
            shaped((tokens, GROUP), BF),
            shaped((seqs, blocks, 8, 128), F32),
        ],
        grid_spec=pltpu.PrefetchScalarGridSpec(
            num_scalar_prefetch=3,
            grid=(seqs,),
            in_specs=[row_block(length, width), whole(vec)]
            + [row_block(length, 128)] * 3
            + [pl.BlockSpec(memory_space=pl.ANY)] * len(refs),
            out_specs=[
                row_block(length, 2 * GROUP),
                row_block(length, 2 * GROUP),
                row_block(length, GROUP),
                row_block(length, GROUP),
                pl.BlockSpec((1, blocks, 8, 128), lambda i, *_: (i, 0, 0, 0)),
            ],
            scratch_shapes=[
                pltpu.VMEM((width, 6 * GROUP), BF),
                pltpu.VMEM((GROUP // 128, 2, length, 256), BF),
                pltpu.SemaphoreType.DMA((len(loads),)),
            ],
        ),
        compiler_params=settings(MOST_VMEM),
        cost_estimate=cost(6e9, 12 << 20),
        name="qkv_attention",
    )(lo, n, at, x, vec, word, mq, mk, *refs)


def attention_back(lo_ref, n_ref, pos_ref, qd_ref, kd_ref, v_ref, context_ref, gc_ref, log_ref, word_ref, mq_ref, mk_ref, x_ref, out_ref, send_ref, keep_ref, gq_ref, gx_ref, dots_ref, all_ref):
    s = pl.program_id(0)
    rows = v_ref.shape[0]
    blocks = rows // BLOCK
    low, low_block = low_lanes(rows), low_lanes(BLOCK)
    gq_ref[...] = jnp.zeros_like(gq_ref)
    for p in range(GROUP // 128):
        lanes = slice(128 * p, 128 * p + 128)
        g = gc_ref[:, lanes].astype(F32)
        zero = jnp.zeros_like(g)
        gx_ref[p, 0] = jnp.where(low, g, zero).astype(BF)
        gx_ref[p, 1] = jnp.where(low, zero, g).astype(BF)
        product = g * context_ref[:, lanes].astype(F32)
        for i in range(blocks):
            turned = jnp.transpose(product[i * BLOCK : (i + 1) * BLOCK])
            dots_ref[i, 2 * p : 2 * p + 1] = column_sums(turned[:64])
            dots_ref[i, 2 * p + 1 : 2 * p + 2] = column_sums(turned[64:])

    def corner(first, second):
        zero = jnp.zeros_like(first)
        return jnp.concatenate(
            [jnp.concatenate([first, zero], 1), jnp.concatenate([zero, second], 1)], 0
        )

    def key_block(j, carry):
        lo, n = lo_ref[s, j], n_ref[s, j]
        k_at = pl.ds(pl.multiple_of(j * BLOCK, BLOCK), BLOCK)
        for nq in range(1, blocks + 1):

            @pl.when(n == nq)
            def _(nq=nq):
                q_at = pl.ds(pl.multiple_of(lo * BLOCK, BLOCK), nq * BLOCK)
                mq, mk = mq_ref[q_at, :], mk_ref[k_at, :]
                word = word_ref[k_at, :]
                key_mask = jnp.where(low_block, word, 1.0 - word) * SCALE
                logs = [log_ref[0, lo + t] for t in range(nq)]
                dots = [dots_ref[lo + t] for t in range(nq)]
                heads, pairs = range(HEADS_PER_GROUP), range(GROUP // 128)
                qs = [qd_ref[q_at, 128 * h : 128 * h + 128] for h in heads]
                ks = [kd_ref[k_at, 128 * h : 128 * h + 128] for h in heads]
                scores = [
                    dot(jnp.concatenate([k, mk], 1), jnp.concatenate([q, mq], 1), 1, 1)
                    for q, k in zip(qs, ks)
                ]
                grad_probs = [
                    dot(v_ref[k_at, 128 * (h // 2) : 128 * (h // 2) + 128], gx_ref[h // 2, h % 2, q_at, :], 1, 1)
                    for h in heads
                ]
                probs, grads = [], []
                for h in heads:
                    log_row = jnp.concatenate([a[h : h + 1] for a in logs], 1)
                    dot_row = jnp.concatenate([a[h : h + 1] for a in dots], 1)
                    prob = jnp.exp2(scores[h] * (LOG2E * SCALE) - log_row)
                    probs.append(prob.astype(BF))
                    grads.append((prob * (grad_probs[h] - dot_row)).astype(BF))
                grad_v = [
                    dot(
                        jnp.concatenate(probs[2 * p : 2 * p + 2], 1),
                        jnp.concatenate([gx_ref[p, 0, q_at, :], gx_ref[p, 1, q_at, :]], 0),
                    )
                    for p in pairs
                ]
                grad_k = [
                    dot(jnp.concatenate(grads[2 * p : 2 * p + 2], 1), corner(*qs[2 * p : 2 * p + 2]))
                    for p in pairs
                ]
                grad_q = [
                    dot(jnp.concatenate(grads[2 * p : 2 * p + 2], 0), corner(*ks[2 * p : 2 * p + 2]), 0, 0)
                    for p in pairs
                ]
                for p in pairs:
                    a, b = grad_k[p][:, :128] * key_mask, grad_k[p][:, 128:] * key_mask
                    a, b = a + pltpu.roll(a, 64, 1), b + pltpu.roll(b, 64, 1)
                    at = 4 * GROUP + 128 * p
                    out_ref[k_at, at : at + 128] = jnp.where(low_block, a, b).astype(BF)
                    at = 5 * GROUP + 128 * p
                    out_ref[k_at, at : at + 128] = grad_v[p].astype(BF)
                    gq_ref[q_at, 256 * p : 256 * p + 256] += grad_q[p]

        return carry

    lax.fori_loop(0, blocks, key_block, 0)
    word = word_ref[...]
    entity = 1.0 - word
    for p in range(GROUP // 128):
        a = gq_ref[:, 256 * p : 256 * p + 128] * SCALE
        b = gq_ref[:, 256 * p + 128 : 256 * p + 256] * SCALE
        to_words = jnp.where(low, a, pltpu.roll(b, 64, 1))
        to_entities = jnp.where(low, pltpu.roll(a, 64, 1), b)
        made = (to_words * word, to_entities * word, to_words * entity, to_entities * entity)
        for part, value in enumerate(made):
            at = part * GROUP + 128 * p
            out_ref[:, at : at + 128] = value.astype(BF)
    all_ref[pl.ds(pl.multiple_of(s * rows, BLOCK), rows), :] = out_ref[...]

    @pl.when(s == pl.num_programs(0) - 1)
    def _():
        half = x_ref.shape[1] // 2
        for i, side in enumerate(sides(pos_ref[0])):
            left = x_ref[:, pl.ds(pl.multiple_of(side * half, 128), half)]
            outs = (send_ref.at[i], keep_ref.at[i])
            grad_parts(pos_ref, left, all_ref, outs, lambda index: [], half // 2 + EXTRA)


def call_attention_back(group, lo, n, pos, kept, grad_context, word, mq, mk, x):
    qd, kd, v, context, log_total = kept
    tokens = v.shape[0]
    seqs, blocks = lo.shape
    length = tokens // seqs
    return pl.pallas_call(
        attention_back,
        out_shape=[shaped((tokens, 6 * GROUP), BF)]
        + [shaped((2, x.shape[1] // 2 + 2 * EXTRA, 3 * GROUP), BF)] * 2,
        grid_spec=pltpu.PrefetchScalarGridSpec(
            num_scalar_prefetch=3,
            grid=(seqs,),
            in_specs=[
                row_block(length, 2 * GROUP),
                row_block(length, 2 * GROUP),
                row_block(length, GROUP),
                row_block(length, GROUP),
                row_block(length, GROUP, group),
                pl.BlockSpec((1, blocks, 8, 128), lambda i, *_: (i, 0, 0, 0)),
            ]
            + [row_block(length, 128)] * 3
            + [whole(x)],
            out_specs=[row_block(length, 6 * GROUP)]
            + [pl.BlockSpec((2, x.shape[1] // 2 + 2 * EXTRA, 3 * GROUP), lambda i, *_: (0, 0, 0))] * 2,
            scratch_shapes=[
                pltpu.VMEM((length, 2 * GROUP), F32),
                pltpu.VMEM((GROUP // 128, 2, length, 128), BF),
                pltpu.VMEM((blocks, 8, 128), F32),
                pltpu.VMEM((tokens, 6 * GROUP), BF),
            ],
        ),
        compiler_params=settings(),
        cost_estimate=cost(2e10, 12 << 20),
        name="attention_back",
    )(lo, n, pos, qd, kd, v, context, grad_context, log_total, word, mq, mk, x)


def middle(loads, spans, n_refs, n_parts, pos_ref, x_ref, g_ref, vec_ref, *rest):
    parts, rest = rest[:n_parts], rest[n_parts:]
    refs, rest = rest[:n_refs], rest[n_refs:]
    outs, scratch = rest[:10], rest[10:]
    context_ref, low_ref, act_ref, output_ref, gb_ref, gi_ref, gx_ref, ga_ref, gc_ref, small_ref = outs
    wo_ref, wi_ref, wd_ref, slope_ref, so, si, sd = scratch
    load_o = partial(copies, pos_ref, refs, loads[0], wo_ref, so)
    load_i = partial(copies, pos_ref, refs, loads[1], wi_ref, si)
    load_d = partial(copies, pos_ref, refs, loads[2], wd_ref, sd)
    start = pl.program_id(0) == 0

    @pl.when(start)
    def _():
        made = load_o()
        begin(made)
        begin(load_i())
        begin(load_d())
        small_ref[...] = jnp.zeros_like(small_ref)
        finish(made)

    take = partial(vector, vec_ref, spans)
    context = jnp.concatenate([part[...] for part in parts], 1)
    context_ref[...] = context
    attended = dot(context, wo_ref[...]) + take(B_OUTPUT)
    first_hat, first_inverse = moments(x_ref[...].astype(F32) + attended)
    gain_attn = take(GAIN_ATTN)
    first = first_hat * gain_attn + take(BIAS_ATTN)
    low = first.astype(BF)
    low_ref[...] = low

    @pl.when(start)
    def _():
        finish(load_i())

    hidden = wi_ref.shape[1]
    step = 512
    b_inner = take(B_INNER)

    @pl.when(start)
    def _():
        finish(load_d())

    branch = take(B_DOWN)
    following = dot(low, wi_ref[:, :step])
    for at in range(0, hidden, step):
        lanes = slice(at, at + step)
        inner = following + b_inner[:, lanes]
        if at + step < hidden:
            following = dot(low, wi_ref[:, at + step : at + 2 * step])
        below = 0.5 * lax.erf(inner * ROOT_HALF) + 0.5
        part = (inner * below).astype(BF)
        act_ref[:, lanes] = part
        bell = INV_ROOT_2PI * jnp.exp(-0.5 * inner * inner)
        slope_ref[:, lanes] = (below + inner * bell).astype(BF)
        branch = branch + dot(part, wd_ref[lanes, :])
    hat, inverse = moments(first + branch)
    gain_ffn = take(GAIN_FFN)
    output_ref[...] = (hat * gain_ffn + take(BIAS_FFN)).astype(BF)
    g = g_ref[...].astype(F32)
    grad_sum = norm_back(g, hat, inverse, gain_ffn)
    gb = grad_sum.astype(BF)
    gb_ref[...] = gb
    small_ref[0:1] += column_sums(g * hat)
    small_ref[1:2] += column_sums(g)
    small_ref[2:3] += column_sums(gb.astype(F32))
    for at in range(0, hidden, step):
        lanes = slice(at, at + step)
        grad = dot(gb, wd_ref[lanes, :], 1, 1) * slope_ref[:, lanes].astype(F32)
        gi_ref[:, lanes] = grad.astype(BF)
    grad_first = grad_sum + dot(gi_ref[...], wi_ref[...], 1, 1)
    grad = norm_back(grad_first, first_hat, first_inverse, gain_attn)
    gx_ref[...] = grad
    ga = grad.astype(BF)
    ga_ref[...] = ga
    small_ref[3:4] += column_sums(grad_first * first_hat)
    small_ref[4:5] += column_sums(grad_first)
    small_ref[5:6] += column_sums(ga.astype(F32))
    gc_ref[...] = dot(ga, wo_ref[...], 1, 1).astype(BF)


def call_middle(pos, parts, x, g, vec, spans, refs, loads, hidden):
    tokens, width = x.shape
    rows = ROWS
    narrow, broad = row_block(rows, width), row_block(rows, hidden)
    return pl.pallas_call(
        partial(middle, loads, spans, len(refs), len(parts)),
        out_shape=[
            shaped((tokens, width), BF),
            shaped((tokens, width), BF),
            shaped((tokens, hidden), BF),
            shaped((tokens, width), BF),
            shaped((tokens, width), BF),
            shaped((tokens, hidden), BF),
            shaped((tokens, width), F32),
            shaped((tokens, width), BF),
            shaped((tokens, width), BF),
            shaped((8, width), F32),
        ],
        grid_spec=pltpu.PrefetchScalarGridSpec(
            num_scalar_prefetch=1,
            grid=(tokens // rows,),
            in_specs=[narrow, narrow, whole(vec)]
            + [row_block(rows, GROUP)] * len(parts)
            + [pl.BlockSpec(memory_space=pl.ANY)] * len(refs),
            out_specs=[narrow, narrow, broad, narrow, narrow, broad, narrow, narrow, narrow]
            + [pl.BlockSpec((8, width), lambda i, *_: (0, 0))],
            scratch_shapes=[
                pltpu.VMEM((width, width), BF),
                pltpu.VMEM((width, hidden), BF),
                pltpu.VMEM((hidden, width), BF),
                pltpu.VMEM((rows, hidden), BF),
            ]
            + [pltpu.SemaphoreType.DMA((len(load),)) for load in loads],
        ),
        compiler_params=settings(MIDDLE_VMEM),
        cost_estimate=cost(5e10, 50 << 20),
        name="middle",
    )(pos, x, g, vec, *parts, *refs)


def sides(c):
    return (1 - c, c)


def down_grad(pos_ref, left_ref, right_ref, send_ref, keep_ref, held_ref):
    half = right_ref.shape[1] // 2
    held_ref[...] = dot(left_ref[...], right_ref[...], 0, 0).astype(BF)
    for out_ref, side in zip((send_ref, keep_ref), sides(pos_ref[1])):
        out_ref[...] = held_ref[:, pl.ds(pl.multiple_of(side * half, 128), half)]


def call_down_grad(pos, left, right, own):
    tokens, rows = left.shape
    columns = right.shape[1]
    eighth = rows // 8

    def block(i, pos):
        place = pos[0] if own else 1 - pos[0]
        for k, at in ((i // 2, pos[2]), (i % 2, pos[3])):
            place = 2 * place + jnp.where(k == 0, 1 - at, at)
        return (0, place)

    return pl.pallas_call(
        down_grad,
        out_shape=[shaped((rows // 2, columns // 2), BF)] * 2,
        grid_spec=pltpu.PrefetchScalarGridSpec(
            num_scalar_prefetch=1,
            grid=(4,),
            in_specs=[pl.BlockSpec((tokens, eighth), block), whole(right)],
            out_specs=[pl.BlockSpec((eighth, columns // 2), lambda i, pos: (i, 0))] * 2,
            scratch_shapes=[pltpu.VMEM((eighth, columns), BF)],
        ),
        compiler_params=settings(MOST_VMEM),
        cost_estimate=cost(7e9, 12 << 20),
        name="down_grad",
    )(pos, left, right)


def grad_parts(pos_ref, left, right_ref, outs, extras, out_rows):
    half = left.shape[1] // 2
    quarter = right_ref.shape[1] // 4
    c, x, z = pos_ref[1], pos_ref[2], pos_ref[3]
    for out, side in zip(outs, sides(c)):
        right = right_ref[:, pl.ds(pl.multiple_of(2 * side * quarter, 128), 2 * quarter)]
        made = dot(left, right, 0, 0).astype(BF)
        lines = column_sums(right.astype(F32))
        for part in range(2):
            mine = slice(part * quarter, (part + 1) * quarter)
            to = pl.ds(pl.multiple_of(jnp.where(x == part, quarter, 0), 128), quarter)
            below = [lines[:, mine]] + extras(2 * side + part)
            below.append(jnp.zeros((EXTRA - len(below), quarter), F32))
            below = jnp.concatenate(below, 0).astype(BF)
            for k in range(2):
                start = pl.multiple_of(jnp.where(z == k, out_rows, 0), 16)
                out[pl.ds(start, half), to] = made[k * half : (k + 1) * half, mine]
                out[k * out_rows + half : k * out_rows + half + EXTRA, to] = below


def inner_output_grad(pos_ref, left_ref, right_ref, context_ref, ga_ref, small_ref, send_ref, keep_ref, held_ref):
    vectors = [small_ref[i : i + 1] for i in range(6)]
    vectors += [jnp.zeros_like(vectors[0])] * 2

    def extras(index):
        made = []
        for first in (0, 4):
            line = vectors[first]
            for k in range(1, 4):
                line = jnp.where(index == k, vectors[first + k], line)
            made.append(line)
        return made

    outs = (send_ref.at[0], keep_ref.at[0])
    out_rows = send_ref.shape[1] // 2
    grad_parts(pos_ref, left_ref[...], right_ref, outs, extras, out_rows)
    rows = left_ref.shape[1]
    size, half = rows // 8, ga_ref.shape[1] // 2
    held_ref[...] = dot(context_ref[...], ga_ref[...], 0, 0).astype(BF)
    for out, side in zip(outs, sides(pos_ref[1])):
        lanes = pl.ds(pl.multiple_of(side * half, 128), half)
        for k, part in enumerate(sides(pos_ref[2])):
            for m, low in enumerate(sides(pos_ref[3])):
                for i in range(2):
                    at = pl.ds(pl.multiple_of((4 * part + 2 * low + i) * size, 16), size)
                    to = (2 * k + i) * half
                    out[(m + 1) * out_rows - size : (m + 1) * out_rows, to : to + half] = held_ref[at, lanes]


def call_inner_output_grad(pos, left, right, context, ga, small):
    tokens, rows = left.shape
    columns = right.shape[1]
    half = rows // 2
    out_rows = half + 2 * EXTRA + half // 4
    block = pl.BlockSpec((tokens, half), lambda i, pos: (0, jnp.where(i == 0, 1 - pos[0], pos[0])))
    return pl.pallas_call(
        inner_output_grad,
        out_shape=[shaped((2, out_rows, columns // 2), BF)] * 2,
        grid_spec=pltpu.PrefetchScalarGridSpec(
            num_scalar_prefetch=1,
            grid=(2,),
            in_specs=[block, whole(right), block, whole(ga), whole(small)],
            out_specs=[pl.BlockSpec((1, out_rows, columns // 2), lambda i, pos: (i, 0, 0))] * 2,
            scratch_shapes=[pltpu.VMEM((half, ga.shape[1]), BF)],
        ),
        compiler_params=settings(MOST_VMEM),
        cost_estimate=cost(1.8e10, 16 << 20),
        name="inner_grad",
    )(pos, left, right, context, ga, small)


def plus(*terms):
    total = terms[0].astype(F32)
    for term in terms[1:]:
        total = total + term.astype(F32)
    return total.astype(BF)


def add_parts(dim, mine_ref, come_ref, *out_refs):
    if dim is None:
        out_refs[0][...] = plus(mine_ref[...], come_ref[...])
        return
    size = mine_ref.shape[dim] // 2
    for k, out_ref in enumerate(out_refs):
        if len(mine_ref.shape) == 3:
            at = k
        else:
            part = pl.ds(k * size, size)
            at = (part, slice(None)) if dim == 0 else (slice(None), part)
        out_ref[...] = plus(mine_ref[at], come_ref[at])


def put_together(mine_ref, come_ref, out_ref):
    rows = mine_ref.shape[0]
    out_ref[:rows, :] = mine_ref[...]
    out_ref[rows:, :] = come_ref[...]


def pair_call(kernel, name, mine, come, shapes):
    return pl.pallas_call(
        kernel,
        out_shape=[shaped(shape, BF) for shape in shapes],
        in_specs=[pl.BlockSpec(memory_space=pltpu.VMEM)] * 2,
        out_specs=[pl.BlockSpec(memory_space=pltpu.VMEM)] * len(shapes),
        compiler_params=pltpu.CompilerParams(vmem_limit_bytes=VMEM),
        cost_estimate=cost(1000, 1000),
        name=name,
    )(mine, come)


def add_call(dim, mine, come):
    shape = mine.shape
    if dim is None:
        shapes = [shape]
    elif len(shape) == 3:
        shapes = [shape[1:]] * 2
    else:
        shapes = [tuple(size // 2 if i == dim else size for i, size in enumerate(shape))] * 2
    return pair_call(partial(add_parts, dim), "add", mine, come, shapes)


def small_call(kernel, name, pos, inputs, shapes):
    return pl.pallas_call(
        kernel,
        out_shape=[shaped(shape, dtype) for shape, dtype in shapes],
        in_specs=[pl.BlockSpec(memory_space=pltpu.SMEM)]
        + [pl.BlockSpec(memory_space=pltpu.VMEM)] * len(inputs),
        out_specs=[pl.BlockSpec(memory_space=pltpu.VMEM)] * len(shapes),
        compiler_params=pltpu.CompilerParams(vmem_limit_bytes=VMEM),
        cost_estimate=cost(3e9, 4 << 20),
        name=name,
    )(pos, *inputs)


def corners(pos_ref):
    c, x = pos_ref[1], pos_ref[2]
    return ((c, x), (c, 1 - x), (1 - c, x), (1 - c, 1 - x))


def join_down(pos_ref, *rest):
    out_ref = rest[4]
    z = pos_ref[3]
    for ref, (c, x) in zip(rest[:4], corners(pos_ref)):
        rows, columns = ref.shape[0] // 2, ref.shape[1]
        lanes = pl.ds(pl.multiple_of(c * columns, 128), columns)
        for m, low in enumerate((z, 1 - z)):
            at = pl.ds(pl.multiple_of((2 * x + low) * rows, 16), rows)
            out_ref[at, lanes] = ref[m * rows : (m + 1) * rows, :].astype(F32)


def join_inner(pos_ref, *rest):
    out_ref, output_ref, extra_ref = rest[4:]
    z = pos_ref[3]
    for ref, (c, x) in zip(rest[:4], corners(pos_ref)):
        columns = ref.shape[1]
        rows = out_ref.shape[0] // 2
        held = ref.shape[0] // 2
        lanes = pl.ds(pl.multiple_of((2 * c + x) * columns, 128), columns)
        extra_ref[:, lanes] = ref[rows : rows + EXTRA, :].astype(F32)
        size, half = rows // 4, columns // 2
        for m, low in enumerate((z, 1 - z)):
            at = pl.ds(pl.multiple_of(low * rows, 16), rows)
            out_ref[at, lanes] = ref[m * held : m * held + rows, :].astype(F32)
            for i in range(2):
                at = pl.ds(pl.multiple_of((4 * x + 2 * low + i) * size, 16), size)
                to = pl.ds(pl.multiple_of(c * half, 128), half)
                value = ref[(m + 1) * held - size : (m + 1) * held, i * half : (i + 1) * half]
                output_ref[at, to] = value.astype(F32)


def join_groups(n_pieces, pos_ref, *rest):
    wide_ref, parts, outs = rest[0], rest[1 : 1 + 4 * n_pieces], rest[1 + 4 * n_pieces :]
    query_ref, key_value_ref, small_ref, extra_ref = outs
    width = GROUP * n_pieces
    rows = query_ref.shape[0] // 2
    z = pos_ref[3]
    mine = 2 * pos_ref[1] + pos_ref[2]
    for case in range(4):

        @pl.when(mine == case)
        def _(case=case):
            for piece in range(n_pieces):
                for k in range(4):
                    ref = parts[4 * piece + k]
                    columns = ref.shape[1]
                    held = ref.shape[0] // 2
                    start = (case ^ k) * columns
                    extra_ref[piece, :, start : start + columns] = ref[rows:held, :].astype(F32)
                    for at in range(0, columns, 128):
                        block, more = divmod(start + at, GROUP)
                        to = query_ref if block < 4 else key_value_ref
                        first = block % 4 * width + piece * GROUP + more
                        for m, low in enumerate((z, 1 - z)):
                            there = pl.ds(pl.multiple_of(low * rows, 16), rows)
                            value = ref[m * held : m * held + rows, at : at + 128]
                            to[there, first : first + 128] = value.astype(F32)

    late = [extra_ref[k, 0:1, :] for k in range(n_pieces)]
    query = jnp.concatenate(
        [row[:, k * GROUP : (k + 1) * GROUP] for k in range(4) for row in late], 1
    )
    value = jnp.concatenate([row[:, 5 * GROUP :] for row in late], 1)
    early = [wide_ref[1 + i : 2 + i, k * width : (k + 1) * width] for i in range(2) for k in range(4)]
    gain_ffn, bias_ffn, b_down, gain_attn, bias_attn, b_output = early[:6]
    wide = wide_ref[0:1, :]
    order = (query, value, b_output, gain_attn, bias_attn, wide, b_down, gain_ffn, bias_ffn)
    lower = jnp.concatenate([v[:, : v.shape[1] // 2] for v in order], 1)
    upper = jnp.concatenate([v[:, v.shape[1] // 2 :] for v in order], 1)
    small_ref[...] = jnp.where(pos_ref[0] == 0, lower, upper)


def pack_kernel(loads, n_refs, n_outs, pos_ref, *rest):
    refs, outs, sems = rest[:n_refs], rest[n_refs : n_refs + n_outs], rest[-1]
    made = copies(
        pos_ref, refs, [load[:3] for load in loads], [outs[load[3]] for load in loads], sems
    )
    begin(made)
    finish(made)


def call_pack(pos, refs, shapes, loads):
    return pl.pallas_call(
        partial(pack_kernel, loads, len(refs), len(shapes)),
        out_shape=[shaped(shape, BF) for shape in shapes],
        in_specs=[pl.BlockSpec(memory_space=pltpu.SMEM)]
        + [pl.BlockSpec(memory_space=pl.ANY)] * len(refs),
        out_specs=[pl.BlockSpec(memory_space=pltpu.VMEM)] * len(shapes),
        scratch_shapes=[pltpu.SemaphoreType.DMA((len(loads),))],
        compiler_params=pltpu.CompilerParams(vmem_limit_bytes=MOST_VMEM),
        cost_estimate=cost(2e9, 2 << 20),
        name="pack",
    )(pos, *refs)


def token_grad(loads, n_refs, n_parts, pos_ref, sum_ref, *rest):
    parts, rest = rest[:n_parts], rest[n_parts:]
    refs, rest = rest[:n_refs], rest[n_refs:]
    out_ref, w_ref, sems = rest
    load = [partial(copies, pos_ref, refs, loads[k], w_ref.at[k], sems.at[k]) for k in range(n_parts)]
    start = pl.program_id(0) == 0

    @pl.when(start)
    def _():
        for one in load:
            begin(one())

    total = sum_ref[...]
    for k in range(n_parts):

        @pl.when(start)
        def _(k=k):
            finish(load[k]())

        total = total + dot(parts[k][...], w_ref[k], 1, 1)
    out_ref[...] = total.astype(out_ref.dtype)


def call_token_grad(pos, parts, summed, refs, loads, kind):
    tokens, width = summed.shape
    columns = parts[0].shape[1]
    rows = TOKEN_ROWS
    return pl.pallas_call(
        partial(token_grad, loads, len(refs), len(parts)),
        out_shape=shaped((tokens, width), kind),
        grid_spec=pltpu.PrefetchScalarGridSpec(
            num_scalar_prefetch=1,
            grid=(tokens // rows,),
            in_specs=[row_block(rows, width)]
            + [row_block(rows, columns)] * len(parts)
            + [pl.BlockSpec(memory_space=pl.ANY)] * len(refs),
            out_specs=row_block(rows, width),
            scratch_shapes=[
                pltpu.VMEM((len(parts), width, columns), BF),
                pltpu.SemaphoreType.DMA((len(parts), len(loads[0]))),
            ],
        ),
        compiler_params=settings(),
        cost_estimate=cost(8e9 * len(parts), 12 << 20),
        name="token_grad",
    )(pos, summed, *parts, *refs)


def facts(first_ref, segments_ref, kinds_ref, lo_ref, n_ref, word_ref, mq_ref, mk_ref):
    seqs, length = segments_ref.shape
    blocks = length // BLOCK
    lane = lax.broadcasted_iota(jnp.int32, (BLOCK, 128), 1)

    def column(ref, s, i):
        row = ref[s : s + 1, i * BLOCK : (i + 1) * BLOCK].astype(F32)
        return jnp.transpose(jnp.broadcast_to(row, (128, BLOCK)))

    for s in range(seqs):
        for i in range(blocks):
            at = slice((s * blocks + i) * BLOCK, (s * blocks + i + 1) * BLOCK)
            word_ref[at, :] = jnp.where(column(kinds_ref, s, i) == 0.0, 1.0, 0.0)
            own = column(segments_ref, s, i) == lane.astype(F32)
            mk_ref[at, :] = jnp.where(own, 1.0, 0.0).astype(BF)
            mq_ref[at, :] = jnp.where(own, 0.0, jnp.where(lane < 4, -FAR, 0.0)).astype(BF)
            lo, n = 0, 0
            for j in range(blocks - 1, -1, -1):
                meets = jnp.logical_and(
                    first_ref[s, j * BLOCK] <= first_ref[s, (i + 1) * BLOCK - 1],
                    first_ref[s, i * BLOCK] <= first_ref[s, (j + 1) * BLOCK - 1],
                )
                lo = jnp.where(meets, j, lo)
                n = n + jnp.where(meets, 1, 0)
            lo_ref[s, i] = lo
            n_ref[s, i] = n


def document_facts(segments, kinds):
    seqs, length = segments.shape
    tokens, blocks = seqs * length, length // BLOCK
    smem, vmem = pl.BlockSpec(memory_space=pltpu.SMEM), pl.BlockSpec(memory_space=pltpu.VMEM)
    return pl.pallas_call(
        facts,
        out_shape=[
            shaped((seqs, blocks), jnp.int32),
            shaped((seqs, blocks), jnp.int32),
            shaped((tokens, 128), F32),
            shaped((tokens, 128), BF),
            shaped((tokens, 128), BF),
        ],
        in_specs=[smem, vmem, vmem],
        out_specs=[smem, smem, vmem, vmem, vmem],
        compiler_params=pltpu.CompilerParams(vmem_limit_bytes=VMEM),
        cost_estimate=cost(1000, 1000),
        name="facts",
    )(segments, segments, kinds)


def gathered_vectors(sizes, everyone):
    spans, parts, at, start = [], [], 0, 0
    for size in sizes:
        parts.append(everyone[:, at : at + size].reshape(1, -1))
        spans.append((start, size * everyone.shape[0]))
        at += size
        start += size * everyone.shape[0]
    return jnp.concatenate(parts, 1).astype(F32), spans


def tie(value, deps):
    return lax.optimization_barrier((value, *deps))[0] if deps else value


def by_dp(bit):
    return lambda v: lax.ppermute(v, DP, [(i, i ^ bit) for i in range(16)])


def over_y(v):
    return lax.ppermute(v, FSDP, [(0, 1), (1, 0)])


over_core, over_x, over_z, over_far_z = (by_dp(1 << k) for k in range(4))


class NearWeights:
    def __init__(self, weights, vectors, pos, width, hidden):
        self.weights, self.pos, self.width = weights, pos, width
        groups = width // GROUP
        self.shard, self.part = width // 2, width // 8
        self.d_shard, self.d_part = hidden // 2, hidden // 8
        self.columns = 2 * width
        o_rows, i_rows, d_rows = self.part // 2, self.part, self.d_part // 2
        self.rows = o_rows, i_rows, d_rows

        def chunk(size, more=0):
            return lambda pos: (2 * pos[2] + pos[1]) * size + more

        def group_loads(group, to, row):
            return [
                (source, ((chunk(self.part), self.part), (column, GROUP)), ((row, self.part), (k * GROUP, GROUP)), to)
                for k, (source, column) in enumerate(group_columns(group, width))
            ]

        lines = -(-vectors.shape[0] // self.columns)
        vectors = jnp.pad(vectors, (0, lines * self.columns - vectors.shape[0])).reshape(lines, self.columns)
        at = (0, lines), (0, self.columns)
        below = (2, at, ((self.part, lines), (0, self.columns)), 0)
        shape = (self.part + EXTRA, self.columns)
        first = call_pack(pos, weights[:2] + [vectors], [shape], group_loads(0, 0, 0) + [below])[0]
        loads = []
        for group in range(1, groups):
            loads += group_loads(group, 0, (group - 1) * self.part)
        for side in range(2):
            at = (side * width, width)
            loads.append((2, ((chunk(self.part, side * o_rows), o_rows), (0, width)), ((0, o_rows), at), 1))
            loads.append(
                (
                    3,
                    ((chunk(self.part), i_rows), (side * self.columns, self.columns)),
                    ((o_rows + side * i_rows, i_rows), (0, self.columns)),
                    1,
                )
            )
            loads.append((4, ((chunk(self.d_part, side * d_rows), d_rows), (0, width)), ((0, d_rows), at), 2))
        shapes = [(groups - 1) * self.part, o_rows + 2 * i_rows, d_rows]
        self.from_y = [over_y(first)]
        packs = call_pack(tie(pos, (first,)), weights, [(rows, self.columns) for rows in shapes], loads)
        self.from_y += [over_y(v) for v in packs]
        other = self.from_y[0][self.part : self.part + lines]
        both = jnp.where(pos[0] == 0, jnp.stack([vectors, other]), jnp.stack([other, vectors]))
        self.vec = both.reshape(2, lines * self.columns).astype(F32)
        self.arrived = [None] * 4

    def spread(self, k, before_x=(), before_core=()):
        v = tie(self.from_y[k], before_x)
        from_x = over_x(v)
        self.arrived[k] = [v, from_x, over_core(v), over_core(tie(from_x, before_core))]

    def others(self, size, more=0):
        other = lambda turn: lambda pos: (4 * (1 - pos[0]) + ((2 * pos[2] + pos[1]) ^ turn)) * size + more
        return [other(turn) for turn in (0, 2, 1, 3)]

    def own(self, size):
        return lambda pos: pos[0] * size

    def group(self, group):
        width, part = self.width, self.part
        loads = [
            (source, ((0, self.shard), (column, GROUP)), ((self.own(self.shard), self.shard), (k * GROUP, GROUP)))
            for k, (source, column) in enumerate(group_columns(group, width))
        ]
        row = 0 if group == 0 else (group - 1) * part
        for k, place in enumerate(self.others(part)):
            at = (0, self.columns)
            loads.append((2 + k, ((row, part), at), ((place, part), at)))
        return self.weights[:2] + self.arrived[min(group, 1)], loads

    def rest(self):
        width, columns = self.width, self.columns
        o_rows, i_rows, d_rows = self.rows
        whole_o, whole_i = (0, width), (0, 2 * columns)
        loads = [
            [(0, ((0, self.shard), whole_o), ((self.own(self.shard), self.shard), whole_o))],
            [(1, ((0, self.shard), whole_i), ((self.own(self.shard), self.shard), whole_i))],
            [(2, ((0, self.d_shard), whole_o), ((self.own(self.d_shard), self.d_shard), whole_o))],
        ]
        for side in range(2):
            at = (side * width, width)
            for k, place in enumerate(self.others(self.part, side * o_rows)):
                loads[0].append((3 + k, ((0, o_rows), at), ((place, o_rows), whole_o)))
            for k, place in enumerate(self.others(self.part)):
                from_rows = (o_rows + side * i_rows, i_rows)
                to = (side * columns, columns)
                loads[1].append((3 + k, (from_rows, (0, columns)), ((place, i_rows), to)))
            for k, place in enumerate(self.others(self.d_part, side * d_rows)):
                loads[2].append((7 + k, ((0, d_rows), at), ((place, d_rows), whole_o)))
        return self.weights[2:] + self.arrived[2] + self.arrived[3], loads


class FarWeights:
    def __init__(self, weights, vectors, sizes, width, hidden):
        self.weights = [lax.all_gather(v, FSDP, axis=0, tiled=True) for v in weights]
        self.vec, self.spans = gathered_vectors(sizes, lax.all_gather(vectors, FSDP))
        self.width = width

    def group(self, group):
        rows = (0, self.width)
        loads = [
            (source, (rows, (column, GROUP)), (rows, (k * GROUP, GROUP)))
            for k, (source, column) in enumerate(group_columns(group, self.width))
        ]
        return self.weights[:2], loads

    def rest(self):
        loads = []
        for k, v in enumerate(self.weights[2:]):
            spec = tuple((0, size) for size in v.shape)
            loads.append([(k, spec, spec)])
        return self.weights[2:], loads


def group_columns(group, width):
    blocks = [(0, part * width + group * GROUP) for part in range(4)]
    return blocks + [(1, part * width + group * GROUP) for part in range(2)]


def body(mesh_shape, hidden_in, segments, kinds, *rest):
    weights = [rest[i] for i in (0, 2, 4, 8, 10)]
    vectors = [rest[i] for i in (1, 3, 5, 6, 7, 9, 11, 12, 13)]
    near = mesh_shape[DP] == 16 and mesh_shape[FSDP] == 2
    seqs, length, width = hidden_in.shape
    tokens = seqs * length
    groups = width // GROUP
    x = hidden_in.reshape(tokens, width)
    g = rest[14].reshape(tokens, width)
    fsdp = mesh_shape[FSDP]
    hidden = weights[4].shape[0] * fsdp
    y, place = lax.axis_index(FSDP), lax.axis_index(DP)
    sizes = [v.shape[0] for v in vectors]
    total, start, parts, spans = sum(sizes), 0, [], []
    for v, size in zip(vectors, sizes):
        parts.append(lax.pad(v, jnp.zeros((), BF), [(start, total - start - size, 0)]))
        spans.append((start, size))
        start += size
    vector_shard = sum(parts[1:], parts[0])
    if near:
        bits = jnp.array([0, 1, 2, 4], jnp.int32)
        pos = jnp.stack([y, place & 1, (place >> 1) & 1, (place >> 2) & 1]).astype(jnp.int32)
        source = NearWeights(weights, vector_shard, pos, width, hidden)
        source.spread(0)
    else:
        pos = jnp.ones((4,), jnp.int32)
        source = FarWeights(weights, vector_shard, sizes, width, hidden)
        spans = source.spans
    vec = source.vec
    lo, n, word, mq, mk = document_facts(segments, kinds)
    kept = []
    for group in range(groups):
        deps = tuple(k[3] for k in kept[-1:])
        if near and group == 0:
            deps = (source.from_y[1],)
        if near and group == 1:
            source.spread(1, (), (kept[0][3],))
        refs, loads = source.group(group)
        kept.append(
            call_qkv_attention(
                group, lo, n, pos, tie(x, deps), vec, spans, word, mq, mk, refs, loads
            )
        )
    if near:
        source.spread(2, (kept[0][3],), (kept[1][3],))
        source.spread(3, (kept[1][3],), (kept[2][3],))
    refs, loads = source.rest()
    context, first_low, act, output, gb, gi, gx, ga, gc, small_sums = call_middle(
        pos, [k[3] for k in kept], x, g, vec, spans, refs, loads, hidden
    )

    made, sent, partial_sums, results = {}, {}, [], {}

    def run(kernel, deps):
        kind, k = kernel
        if kind == DOWN:
            made[kind, k] = call_down_grad(pos, tie(act, deps), gb, k)
            return tuple(made[kind, k][:1])
        if kind == INNER:
            made[kind] = call_inner_output_grad(pos, tie(first_low, deps), gi, context, ga, small_sums)
            return tuple(made[kind][:1])
        if kind == ATTENTION:
            part, *made[k] = call_attention_back(
                k, lo, n, pos, kept[k], tie(gc, deps), word, mq, mk, x
            )
            partial_sums.append(part)
            return (part,)
        held = [source.group(i) for i in k]
        count = len(held[0][0])
        results[TOKEN] = call_token_grad(
            pos, [partial_sums[i] for i in k], tie(results.get(TOKEN, gx), deps),
            [ref for refs, _ in held for ref in refs],
            [[(load[0] + i * count,) + load[1:] for load in loads] for i, (_, loads) in enumerate(held)],
            BF if groups - 1 in k else F32,
        )
        return (results[TOKEN],)

    def advance(k, step, deps):
        if k == DOWN and step < 2:
            send, keep = made[DOWN, 0]
            if step == 0:
                sent[k] = over_core(send)
                return ()
            out = add_call(None, keep, tie(sent[k], deps))
            send, keep = made[DOWN, 1]
            sent[k] = (over_y(out[0]), (keep, over_core(send)))
            return tuple(out)
        if step == 0:
            sent[k] = (over_core(tie(made[k][0], deps)), made[k][1])
            return ()
        come, mine = sent[k]
        come = tie(come, deps)
        if k == DOWN and step == 2:
            mine = add_call(None, *mine)[0]
        if step == 1:
            out = add_call(0, mine, come)
            sent[k] = (over_y(out[0]), out[1])
        elif step in (2, 3):
            out = add_call(1 if step == 2 and k != DOWN else 0, mine, come)
            sent[k] = ((over_x if step == 2 else over_z)(out[0]), out[1])
        elif step in (4, 5):
            out = add_call(None, mine, come)
            sent[k] = ((over_far_z if step == 4 else over_z)(out[0]), out[0])
        elif step == 6:
            rows, columns = mine.shape
            out = pair_call(put_together, "put_together", mine, come, [(2 * rows, columns)])
            sent[k] = (over_x(out[0]), [out[0], over_core(out[0])])
        elif step == 7:
            out = [come]
            sent[k] = (over_core(come), [mine[0], come, mine[1]])
        else:
            sent[k] = [*mine, come]
            return finished(k)
        return tuple(out)

    def finished(k):
        shard = width // 2
        if k == DOWN:
            results[k] = small_call(join_down, "join_down", pos, sent[k], [((hidden // 2, width), F32)])
        elif k == INNER:
            results[k] = small_call(
                join_inner, "join_inner", pos, sent[k],
                [((shard, hidden), F32), ((shard, width), F32), ((EXTRA, hidden), F32)],
            )
        else:
            return tuple(sent[k])
        return tuple(results[k])

    kernels = [(DOWN, 0), (INNER, 0)] + [(ATTENTION, k) for k in range(groups)]
    kernels += [(TOKEN, [k]) for k in range(groups)] + [(DOWN, 1)]
    if near:
        base, since, tail = (), (), False
        for item in PLAN:
            if item is None:
                tail = True
            elif isinstance(item, tuple):
                made_now = advance(*item, base if tail or item != (INNER, 0) else base + since)
                base, since = (made_now or base, ()) if tail else (base, since + made_now)
            else:
                base = run(kernels[item], base if tail else since)
                since = () if tail else base
        grad_inner, grad_output, extra = results[INNER]
        shard = width // 2
        grad_query, grad_key_value, small, _ = small_call(
            partial(join_groups, groups), "join_groups", pos,
            [extra] + [v for k in range(groups) for v in sent[k]],
            [
                ((shard, 4 * width), F32),
                ((shard, 2 * width), F32),
                ((1, total), F32),
                ((groups, EXTRA, 6 * GROUP), F32),
            ],
        )
        small = small.reshape(total)
        shares = [small[start : start + size] for start, size in spans]
        grad_down = results[DOWN][0]
    else:
        for kernel in kernels:
            run(kernel, ())

        def flat(v):
            return v.reshape(v.shape[0], -1).astype(F32)

        def far(v):
            return lax.psum(lax.psum_scatter(v, FSDP, scatter_dimension=0, tiled=True), DP)

        def main_and_extra(k, rows):
            both = jnp.stack(made[k], 2).reshape(2, 2, made[k][0].shape[1] // 2, 2, -1)
            main = both[:, :, :rows].reshape(4 * rows, 2, -1)
            more = both[1, 1, rows : rows + EXTRA]
            return flat(far(main)), flat(lax.psum(more, (DP, FSDP)))

        rows = width // 4
        grad_inner, wide = main_and_extra(INNER, rows)
        both = jnp.concatenate([jnp.stack(made[DOWN, i], 1) for i in range(2)], 0)
        grad_down = flat(far(both))
        out = jnp.stack(made[INNER], 0).reshape(2, 2, 2, -1, hidden // 2)[:, :, :, rows + EXTRA :]
        size = out.shape[3]
        out = out.reshape(2, 2, 2, size, 2, 2, width // 2).transpose(1, 4, 2, 5, 3, 0, 6)
        grad_output = flat(far(out.reshape(width, 2, -1)))
        by_group, late = zip(*[main_and_extra(k, rows) for k in range(groups)])
        late = [e[0] for e in late]
        early = [wide[1 + i, k * width : (k + 1) * width] for i in range(2) for k in range(4)]
        gain_ffn, bias_ffn, b_down, gain_attn, bias_attn, b_output = early[:6]
        query = jnp.concatenate([e[k * GROUP : (k + 1) * GROUP] for k in range(4) for e in late])
        value = jnp.concatenate([e[5 * GROUP :] for e in late])
        order = (query, value, b_output, gain_attn, bias_attn, wide[0], b_down, gain_ffn, bias_ffn)
        shares = [lax.dynamic_slice_in_dim(v, y * size, size, 0) for v, size in zip(order, sizes)]
        grad_query = jnp.concatenate(
            [m[:, k * GROUP : (k + 1) * GROUP] for k in range(4) for m in by_group], 1
        )
        grad_key_value = jnp.concatenate(
            [m[:, k * GROUP : (k + 1) * GROUP] for k in range(4, 6) for m in by_group], 1
        )
    return (
        output.reshape(seqs, length, width),
        results[TOKEN].reshape(seqs, length, width),
        grad_query,
        shares[B_QUERY],
        grad_key_value,
        shares[B_VALUE],
        grad_output,
        shares[B_OUTPUT],
        shares[GAIN_ATTN],
        shares[BIAS_ATTN],
        grad_inner,
        shares[B_INNER],
        grad_down,
        shares[B_DOWN],
        shares[GAIN_FFN],
        shares[BIAS_FFN],
    )


DOWN, INNER, ATTENTION, TOKEN = range(-4, 0)
PLAN = (
    0, (DOWN, 0), 8, (DOWN, 1), 1, (DOWN, 2), (INNER, 0), (INNER, 1), 2, (DOWN, 3), (0, 0), 3, (0, 1),
    (1, 0), (DOWN, 4), 4, None, (2, 0), (INNER, 2), (1, 1), 5, (0, 2), (DOWN, 5), (2, 1), (INNER, 3),
    (1, 2), (DOWN, 6), (0, 3), (INNER, 4), (1, 3), (2, 2), (0, 4), 6, 7, (INNER, 5), (2, 3), (1, 4),
    (DOWN, 7), (DOWN, 8), (0, 5), (INNER, 6), (2, 4), (0, 6), (1, 5), (2, 5), (1, 6), (INNER, 7), (0,
    7), (2, 6), (INNER, 8), (0, 8), (1, 7), (1, 8), (2, 7), (2, 8),
)
def solution(mesh):
    split = P((DP, FSDP), None, None)
    tokens = P((DP, FSDP), None)
    matrix, line = P(FSDP, None), P(FSDP)
    weights = (matrix, line, matrix, line, matrix, line, line, line, matrix, line, matrix, line, line, line)
    return jax.shard_map(
        partial(body, dict(mesh.shape)),
        mesh=mesh,
        in_specs=(split, tokens, tokens) + weights + (split,),
        out_specs=(split, split) + weights,
        check_vma=False,
    )
```
